32 devices in a mesh: seq: 8 (over y, x, core), mp: 4 (over z).
Axes of the slice: x: 2, y: 2, z: 4, core: 2. Of those that a mesh axis runs over, the one named last changes fastest.
Arguments:
- tokens: bfloat16 [8192, 2048], P('seq'), may hold values from -6 to 6
- group_ids: int32 [8192], P('seq'), may hold values from -1 to 3, as said below
- gain_attn: bfloat16 [2048], P('seq'), may hold values from 0.099609375 to 1.8984375
- w_query: bfloat16 [2048, 2048], P('seq', 'mp'), may hold values from -0.1875 to 0.1875
- w_key: bfloat16 [2048, 2048], P('seq', 'mp'), may hold values from -0.1875 to 0.1875
- w_value: bfloat16 [2048, 2048], P('seq', 'mp'), may hold values from -0.125 to 0.125
- w_out: bfloat16 [2048, 2048], P('mp', 'seq'), may hold values from -0.375 to 0.375
- gain_mlp: bfloat16 [2048], P('seq'), may hold values from 0.099609375 to 1.8984375
- w_gate: bfloat16 [2048, 5632], P('seq', 'mp'), may hold values from -0.125 to 0.125
- w_up: bfloat16 [2048, 5632], P('seq', 'mp'), may hold values from -0.125 to 0.125
- w_down: bfloat16 [5632, 2048], P('mp', 'seq'), may hold values from -0.109375 to 0.109375
- cotangent: bfloat16 [8192, 2048], P('seq'), may hold values from -6 to 6
Outputs:
- out: bfloat16 [8192, 2048], P('seq')
- tokens_grad: float32 [8192, 2048], P('seq')
- gain_attn_grad: float32 [2048], P('seq')
- w_query_grad: float32 [2048, 2048], P('seq', 'mp')
- w_key_grad: float32 [2048, 2048], P('seq', 'mp')
- w_value_grad: float32 [2048, 2048], P('seq', 'mp')
- w_out_grad: float32 [2048, 2048], P('mp', 'seq')
- gain_mlp_grad: float32 [2048], P('seq')
- w_gate_grad: float32 [2048, 5632], P('seq', 'mp')
- w_up_grad: float32 [2048, 5632], P('seq', 'mp')
- w_down_grad: float32 [5632, 2048], P('mp', 'seq')
The draws below stay inside these ranges and needn't reach their ends.
Inputs may be any that keep to these rules, and one draw needn't show every extreme that they name: `group_ids`: within each aligned block of 1024 positions the positions holding -1 form one run of at most 512 positions.
All inputs are finite; a program needn't handle non-finite values.
Results may differ from the reference program's by a relative error of at most 0.02.
Values may be sent and summed in bfloat16 or wider, within the bound.
No kernel may reach another device: no remote copies, remote signals or barrier semaphores. Data moves between devices by JAX's collectives and lax.ppermute only.
A program may use at most 256 MiB of HBM per device.

```python
import math
import jax
import jax.numpy as jnp
from jax import lax

D = 2048
HEADS = 16
HEAD_DIM = 128
FF = 5632
WINDOW = 64
GROUPS = 4
TOK_DEV = 1024
TOKENS = 8192


def draw_group_ids(key, part):
    key = jax.random.fold_in(key, 7)
    key_change, key_table, key_start, key_length = jax.random.split(key, 4)
    change = (jax.random.randint(key_change, (TOKENS,), 0, 12) == 0).astype(jnp.int32)
    run_index = jnp.cumsum(change)
    table = jax.random.randint(key_table, (TOKENS + 1,), 0, GROUPS)
    groups = table[run_index]
    block_total = TOKENS // TOK_DEV
    pad_start = jax.random.randint(key_start, (block_total, 1), 0, TOK_DEV // 2)
    pad_length = jax.random.randint(key_length, (block_total, 1), 0, TOK_DEV // 2 + 1)
    position = jnp.arange(TOK_DEV, dtype=jnp.int32)[None, :]
    padding = (position >= pad_start) & (position < pad_start + pad_length)
    return jnp.where(padding.reshape(-1), -1, groups).astype(jnp.int32)


def strengthened(entries, stream_key, source, target, blocks, factor):
    owner, partner = [(jnp.arange(entries.shape[axis_at]) // (entries.shape[axis_at] // blocks)).reshape([-1 if axis == axis_at else 1 for axis in range(entries.ndim)]) for axis_at in (source, target)]
    chosen = jax.random.permutation(stream_key, blocks)[partner]
    strong = (owner == chosen) | (owner == (partner + blocks // 2) % blocks)
    return jnp.where(strong, factor * entries, entries)


def block_levels(rng, shape, pieces, smallest, top_value):
    gain, own = 1.0, jax.random.fold_in(rng, 6)
    for dim, parts in pieces:
        steps = jnp.exp(jax.random.uniform(jax.random.fold_in(own, dim), (parts,), jnp.float32, smallest / len(pieces), top_value / len(pieces)))
        gain = gain * jnp.repeat(steps, shape[dim] // parts).reshape([-1 if axis == dim else 1 for axis in range(len(shape))])
    return gain


def noise(stream_key, dims, deviation, most, cuts=(), held_as=jnp.bfloat16):
    values = jax.random.normal(stream_key, dims, jnp.float32) * deviation
    if len(cuts) > 0:
        values = block_levels(stream_key, dims, cuts, -0.22, 0.18) * values
    return jnp.clip(values, min=-most, max=most).astype(held_as)


def noise_with(own_key, extent, spread, limit, cuts, heavy, kind=jnp.bfloat16):
    entries = spread * jax.random.normal(own_key, extent, jnp.float32)
    if cuts:
        entries = entries * block_levels(own_key, extent, cuts, -0.22, 0.18)
    return jnp.clip(strengthened(entries, jax.random.fold_in(own_key, 3), *heavy), -limit, limit).astype(kind)


def setup_inputs(seed: int = 0) -> dict:
    streams_of = jax.random.split(jax.random.key(seed), 13)
    return {
        "tokens": noise_with(streams_of[0], (TOKENS, D), 1.0, 6.0, ((0, 8),), (0, 1, 8, 2.0)),
        "group_ids": draw_group_ids(jax.random.fold_in(streams_of[12], 71), 0),
        "gain_attn": jnp.clip(1.0 + 0.18 * jax.random.normal(streams_of[2], (D,), jnp.float32), 0.099609375, 1.8984375).astype(jnp.bfloat16),
        "w_query": noise(streams_of[3], (D, HEADS * HEAD_DIM), (D // 2) ** -0.5, 0.1875, ((0, 8), (1, 4))),
        "w_key": noise(streams_of[4], (D, HEADS * HEAD_DIM), (D // 2) ** -0.5, 0.1875, ((0, 8), (1, 4))),
        "w_value": noise(streams_of[5], (D, HEADS * HEAD_DIM), D ** -0.5, 0.125, ((0, 8), (1, 4))),
        "w_out": noise(streams_of[6], (HEADS * HEAD_DIM, D), (D // 8) ** -0.5, 0.375, ((0, 4), (1, 8))),
        "gain_mlp": jnp.clip(1.0 + 0.18 * jax.random.normal(streams_of[7], (D,), jnp.float32), 0.099609375, 1.8984375).astype(jnp.bfloat16),
        "w_gate": noise(streams_of[8], (D, FF), D ** -0.5, 0.125, ((0, 8), (1, 4))),
        "w_up": noise(streams_of[9], (D, FF), D ** -0.5, 0.125, ((0, 8), (1, 4))),
        "w_down": noise(streams_of[10], (FF, D), (FF // 2) ** -0.5, 0.109375, ((0, 4), (1, 8))),
        "cotangent": noise_with(streams_of[11], (TOKENS, D), 1.0, 6.0, ((0, 8),), (0, 1, 8, 2.0)),
    }


epsilon = 1e-05
masked_score = -1e+30
highest = lax.Precision.HIGHEST

@jax.custom_vjp
def low(v):
    return lax.optimization_barrier(v.astype(jnp.bfloat16)).astype(jnp.float32)

@jax.custom_vjp
def low_back(v):
    return v

def low_keep(v):
    return (low(v), None)

def low_pass(kept, grad):
    return (grad,)

def back_keep(v):
    return (v, None)

def back_low(kept, grad):
    return (low(grad),)
low.defvjp(low_keep, low_pass)
low_back.defvjp(back_keep, back_low)

def rounded_both(value_in):
    return low(low_back(value_in))

def matmul(left_matrix, right_matrix):
    return jnp.dot(left_matrix, right_matrix, precision=highest, preferred_element_type=jnp.float32)

def rms_norm(value_in, gain_full):
    factor = lax.rsqrt(lax.optimization_barrier(jnp.mean(value_in * value_in, axis=-1, keepdims=True)) + epsilon)
    return value_in * factor * gain_full

def allowed_mask(query_ids, key_ids, query_rows, window):
    query_pos = jnp.arange(query_rows, dtype=jnp.int32)[:, None]
    key_pos = jnp.arange(query_rows + window, dtype=jnp.int32)[None, :]
    inside = (key_pos >= query_pos) & (key_pos <= query_pos + window)
    same_group = (query_ids[:, None] == key_ids[None, :]) & (query_ids[:, None] >= 0)
    return inside & same_group

def attend(query_block, key_block, value_block, query_ids, key_ids):
    query_rows = query_block.shape[0]
    window = key_block.shape[0] - query_rows
    allowed = allowed_mask(query_ids, key_ids, query_rows, window)
    score_scale = query_block.shape[2] ** (-0.5)
    scores = low_back(jnp.einsum('qhd,khd->hqk', query_block, key_block, precision=highest) * score_scale)
    scores = jnp.where(allowed[None], scores, masked_score)
    top_score = lax.optimization_barrier(jnp.max(scores, axis=-1, keepdims=True))
    weights = jnp.where(allowed[None], jnp.exp(scores - top_score), 0.0)
    valid = (query_ids >= 0)[None, :, None]
    totals = jnp.where(valid, lax.optimization_barrier(jnp.sum(weights, axis=-1, keepdims=True)), 1.0)
    probs = weights / totals
    return jnp.einsum('hqk,khd->qhd', low(probs), value_block, precision=highest)

def reference(tokens, group_ids, gain_attn, w_query, w_key, w_value, w_out, gain_mlp, w_gate, w_up, w_down, cotangent):
    row_block = math.gcd(TOKENS, 4096)
    sub_block = math.gcd(row_block, 512)
    block_total = TOKENS // row_block
    head_width = HEADS * HEAD_DIM
    id_blocks = group_ids.reshape(block_total, row_block)
    checked_attend = jax.checkpoint(attend)

    def forward(inputs, gain_one, query_weight, key_weight, value_weight, out_weight, gain_two, gate_weight, up_weight, down_weight):

        def step_rows(carry, pair):
            row_inputs, row_ids = pair
            keys_prev, values_prev, ids_prev = carry
            normed = low(rms_norm(row_inputs, gain_one))
            queries = rounded_both(matmul(normed, query_weight)).reshape(row_block, HEADS, HEAD_DIM)
            keys_new = rounded_both(matmul(normed, key_weight)).reshape(row_block, HEADS, HEAD_DIM)
            values_new = rounded_both(matmul(normed, value_weight)).reshape(row_block, HEADS, HEAD_DIM)
            keys_ext = jnp.concatenate([keys_prev, keys_new], axis=0)
            values_ext = jnp.concatenate([values_prev, values_new], axis=0)
            ids_ext = jnp.concatenate([ids_prev, row_ids], axis=0)

            def one_block(block_index):
                start = (block_index * sub_block).astype(jnp.int32)
                return checked_attend(lax.dynamic_slice_in_dim(queries, start, sub_block, 0), lax.dynamic_slice_in_dim(keys_ext, start, sub_block + WINDOW, 0), lax.dynamic_slice_in_dim(values_ext, start, sub_block + WINDOW, 0), lax.dynamic_slice_in_dim(row_ids, start, sub_block, 0), lax.dynamic_slice_in_dim(ids_ext, start, sub_block + WINDOW, 0))
            attended = lax.map(one_block, jnp.arange(row_block // sub_block, dtype=jnp.int32))
            attended = rounded_both(attended.reshape(row_block, head_width))
            middle = row_inputs + low_back(matmul(attended, out_weight))
            normed_mid = low(rms_norm(middle, gain_two))
            gate = low_back(matmul(normed_mid, gate_weight))
            up_proj = low_back(matmul(normed_mid, up_weight))
            activation = low(jax.nn.silu(gate) * up_proj)
            result = middle + low_back(matmul(activation, down_weight))
            return ((keys_new[-WINDOW:], values_new[-WINDOW:], row_ids[-WINDOW:]), result)
        start_carry = (jnp.zeros((WINDOW, HEADS, HEAD_DIM), jnp.float32), jnp.zeros((WINDOW, HEADS, HEAD_DIM), jnp.float32), jnp.full((WINDOW,), -1, jnp.int32))
        unused, results = lax.scan(jax.checkpoint(step_rows), start_carry, (inputs.reshape(block_total, row_block, D), id_blocks))
        return results.reshape(TOKENS, D)
    floats = [array_in.astype(jnp.float32) for array_in in (tokens, gain_attn, w_query, w_key, w_value, w_out, gain_mlp, w_gate, w_up, w_down)]
    result, pullback = jax.vjp(forward, *floats)
    grads = pullback(cotangent.astype(jnp.float32))
    return (result.astype(jnp.bfloat16), grads[0], grads[1], grads[2], grads[3], grads[4], grads[5], grads[6], grads[7], grads[8], grads[9])
```

```python
import jax
import jax.numpy as jnp
from jax import lax
from jax.sharding import PartitionSpec as P

HEAD_DIM = 128
WINDOW = 64
CHUNKS = 4

epsilon = 1e-05
masked_score = -1e30


def from_behind(block, axis, distance):
    devices = range(lax.axis_size(axis))
    route = [(i - distance, i) for i in devices if i - distance in devices]
    return lax.ppermute(block, axis, route)


def inner_rows(left_matrix, right_matrix):
    return lax.dot_general(
        left_matrix, right_matrix, (((0,), (0,)), ((), ())), preferred_element_type=jnp.float32
    )


def times(left_matrix, right_matrix):
    return jnp.dot(left_matrix, right_matrix, preferred_element_type=jnp.float32)


def times_transposed(left_matrix, right_matrix):
    return lax.dot_general(
        left_matrix, right_matrix, (((1,), (1,)), ((), ())), preferred_element_type=jnp.float32
    )


def row_scale(value_in):
    return lax.rsqrt(jnp.mean(value_in * value_in, axis=-1, keepdims=True) + epsilon)


def norm_backward(grad_normed, normed_unit, row_factor, gain_full):
    scaled_grad = grad_normed * gain_full
    return row_factor * (
        scaled_grad - normed_unit * jnp.mean(scaled_grad * normed_unit, axis=-1, keepdims=True)
    )


def line_sum(part, axis):
    if lax.axis_size(axis) != 4:
        return lax.psum(part, axis).astype(jnp.float32)
    place = lax.axis_index(axis)
    inward = lax.ppermute(part, axis, [(0, 1), (3, 2)])
    half = (part.astype(jnp.float32) + inward.astype(jnp.float32)).astype(jnp.bfloat16)
    across = lax.ppermute(half, axis, [(1, 2), (2, 1)])
    total = (half.astype(jnp.float32) + across.astype(jnp.float32)).astype(jnp.bfloat16)
    outward = lax.ppermute(total, axis, [(1, 0), (2, 3)])
    middle_place = (place == 1) | (place == 2)
    return jnp.where(middle_place, total, outward).astype(jnp.float32)


def small_sum_scatter(value, axis):
    size = lax.axis_size(axis)
    place = lax.axis_index(axis)
    bit = size // 2
    while bit >= 1:
        half = value.shape[1] // 2
        low, high = value[:, :half], value[:, half:]
        upper = (place & bit) != 0
        keep = jnp.where(upper, high, low)
        give = jnp.where(upper, low, high)
        value = keep + lax.ppermute(give, axis, [(i, i ^ bit) for i in range(size)])
        bit //= 2
    return value


def small_sum(value, axis):
    size = lax.axis_size(axis)
    bit = 1
    while bit < size:
        value = value + lax.ppermute(value, axis, [(i, i ^ bit) for i in range(size)])
        bit *= 2
    return value


def block_allowed(query_ids, key_ids, block_rows):
    query_pos = jnp.arange(block_rows, dtype=jnp.int32)[:, None]
    key_pos = jnp.arange(block_rows + WINDOW, dtype=jnp.int32)[None, :]
    inside = (key_pos >= query_pos) & (key_pos <= query_pos + WINDOW)
    same_group = (query_ids[:, None] == key_ids[None, :]) & (query_ids[:, None] >= 0)
    return inside & same_group


def split_heads(matrix, head_count):
    return matrix.reshape(matrix.shape[0], head_count, HEAD_DIM)


def block_scores(query_heads, key_heads, allowed):
    scores = jnp.einsum(
        "qhd,khd->hqk", query_heads, key_heads, preferred_element_type=jnp.float32
    ) * HEAD_DIM ** (-0.5)
    return jnp.where(allowed[None], scores, masked_score)


def attend_forward(queries, keys_ext, values_ext, ids_ext, head_count):
    block_rows = queries.shape[0]
    query_ids = ids_ext[WINDOW:]
    allowed = block_allowed(query_ids, ids_ext, block_rows)
    scores = block_scores(
        split_heads(queries, head_count), split_heads(keys_ext, head_count), allowed
    )
    top_score = jnp.max(scores, axis=-1, keepdims=True)
    weights = jnp.where(allowed[None], jnp.exp(scores - top_score), 0.0)
    valid = (query_ids >= 0)[None, :, None]
    totals = jnp.where(valid, jnp.sum(weights, axis=-1, keepdims=True), 1.0)
    probs = (weights / totals).astype(jnp.bfloat16)
    mixed = jnp.einsum(
        "hqk,khd->qhd", probs, split_heads(values_ext, head_count), preferred_element_type=jnp.float32
    )
    return mixed.reshape(block_rows, -1).astype(jnp.bfloat16), top_score + jnp.log(totals)


def attend_backward(queries, keys_ext, values_ext, ids_ext, out_grad, log_totals, head_count):
    block_rows = queries.shape[0]
    span = keys_ext.shape[0]
    score_scale = HEAD_DIM ** (-0.5)
    query_ids = ids_ext[WINDOW:]
    allowed = block_allowed(query_ids, ids_ext, block_rows)
    query_heads = split_heads(queries, head_count)
    key_heads = split_heads(keys_ext, head_count)
    value_heads = split_heads(values_ext, head_count)
    grad_heads = split_heads(out_grad, head_count)
    scores = block_scores(query_heads, key_heads, allowed)
    probs = jnp.where(allowed[None], jnp.exp(scores - log_totals), 0.0)
    prob_grad = jnp.einsum(
        "qhd,khd->hqk", grad_heads, value_heads, preferred_element_type=jnp.float32
    )
    value_part = jnp.einsum(
        "hqk,qhd->khd", probs.astype(jnp.bfloat16), grad_heads, preferred_element_type=jnp.float32
    )
    centre = jnp.sum(prob_grad * probs, axis=-1, keepdims=True)
    score_grad = (probs * (prob_grad - centre)).astype(jnp.bfloat16)
    query_part = jnp.einsum(
        "hqk,khd->qhd", score_grad, key_heads, preferred_element_type=jnp.float32
    )
    key_part = jnp.einsum(
        "hqk,qhd->khd", score_grad, query_heads, preferred_element_type=jnp.float32
    )
    return (
        query_part.reshape(block_rows, -1) * score_scale,
        key_part.reshape(span, -1) * score_scale,
        value_part.reshape(span, -1),
    )


def body(
    tokens,
    group_ids,
    gain_attn,
    w_query,
    w_key,
    w_value,
    w_out,
    gain_mlp,
    w_gate,
    w_up,
    w_down,
    cotangent,
):
    rows = tokens.shape[0]
    chunk_rows = rows // CHUNKS
    chunks = [slice(c * chunk_rows, (c + 1) * chunk_rows) for c in range(CHUNKS)]
    head_width = w_query.shape[1]
    head_count = head_width // HEAD_DIM
    hidden = w_gate.shape[1]

    gains = lax.all_gather(jnp.stack([gain_attn, gain_mlp]), "seq", axis=1, tiled=True)
    gain_one = gains[:1].astype(jnp.float32)
    gain_two = gains[1:].astype(jnp.float32)
    attn_shard = jnp.concatenate([w_query, w_key, w_value, w_out.T], axis=1)
    attn_weight = lax.all_gather(attn_shard, "seq", axis=0, tiled=True)
    mlp_shard = jnp.concatenate([w_gate, w_up, w_down.T], axis=1)
    mlp_shard, attn_weight = lax.optimization_barrier((mlp_shard, attn_weight))
    mlp_weight = lax.all_gather(mlp_shard, "seq", axis=0, tiled=True)
    qkv_weight = attn_weight[:, : 3 * head_width]
    out_weight = attn_weight[:, 3 * head_width :]
    gate_up_weight = mlp_weight[:, : 2 * hidden]
    down_weight = mlp_weight[:, 2 * hidden :]

    inputs = tokens.astype(jnp.float32)
    factor_one = row_scale(inputs)
    unit_one = inputs * factor_one
    normed_attn = (unit_one * gain_one).astype(jnp.bfloat16)
    qkv = times(normed_attn, qkv_weight).astype(jnp.bfloat16)
    queries = qkv[:, :head_width]
    keys_values = qkv[:, head_width:]
    halo, ids_halo = from_behind((keys_values[-WINDOW:], group_ids[-WINDOW:] + 1), "seq", 1)
    keys_values_ext = jnp.concatenate([halo, keys_values], axis=0)
    ids_ext = jnp.concatenate([ids_halo - 1, group_ids], axis=0)

    spans = [slice(c * chunk_rows, (c + 1) * chunk_rows + WINDOW) for c in range(CHUNKS)]
    attended, log_totals, middle = [], [], []
    for own, span in zip(chunks, spans):
        mixed, logs = attend_forward(
            queries[own],
            keys_values_ext[span, :head_width],
            keys_values_ext[span, head_width:],
            ids_ext[span],
            head_count,
        )
        attended.append(mixed)
        log_totals.append(logs)
        term = times_transposed(mixed, out_weight).astype(jnp.bfloat16)
        middle.append(inputs[own] + line_sum(term, "mp"))

    normed_mlp, activations, gate_up_grads, middle_grads, outputs, gain_two_parts = [], [], [], [], [], []
    for own, mid in zip(chunks, middle):
        factor_two = row_scale(mid)
        unit_two = mid * factor_two
        normed = (unit_two * gain_two).astype(jnp.bfloat16)
        gate_up = times(normed, gate_up_weight)
        gate, up_proj = gate_up[:, :hidden], gate_up[:, hidden:]
        sigmoid_gate = jax.nn.sigmoid(gate)
        silu_gate = gate * sigmoid_gate
        activation = (silu_gate * up_proj).astype(jnp.bfloat16)
        act_grad = times(cotangent[own], down_weight)
        gate_grad = (
            act_grad * up_proj * (sigmoid_gate + gate * sigmoid_gate * (1.0 - sigmoid_gate))
        ).astype(jnp.bfloat16)
        up_grad = (act_grad * silu_gate).astype(jnp.bfloat16)
        gate_up_grad = jnp.concatenate([gate_grad, up_grad], axis=1)
        mlp_grad_term = times_transposed(gate_up_grad, gate_up_weight)
        gain_two_parts.append(jnp.sum(mlp_grad_term * unit_two, axis=0, keepdims=True))
        normed_mlp_grad = line_sum(mlp_grad_term.astype(jnp.bfloat16), "mp")
        middle_grads.append(
            cotangent[own].astype(jnp.float32)
            + norm_backward(normed_mlp_grad, unit_two, factor_two, gain_two)
        )
        mlp_term = times_transposed(activation, down_weight).astype(jnp.bfloat16)
        outputs.append((mid + line_sum(mlp_term, "mp")).astype(jnp.bfloat16))
        normed_mlp.append(normed)
        activations.append(activation)
        gate_up_grads.append(gate_up_grad)
    output_own = jnp.concatenate(outputs, axis=0)
    down_grad = inner_rows(cotangent, jnp.concatenate(activations, axis=0)).astype(jnp.bfloat16)
    gate_up_weight_grad = inner_rows(
        jnp.concatenate(normed_mlp, axis=0), jnp.concatenate(gate_up_grads, axis=0)
    ).astype(jnp.bfloat16)
    down_share = lax.psum_scatter(down_grad, "seq", scatter_dimension=0, tiled=True)
    gate_up_share = lax.psum_scatter(gate_up_weight_grad, "seq", scatter_dimension=0, tiled=True)

    query_grads, key_value_grads = [], []
    carry = None
    for c in range(CHUNKS):
        span = spans[c]
        middle_low = middle_grads[c].astype(jnp.bfloat16)
        attended_grad = times(middle_low, out_weight).astype(jnp.bfloat16)
        query_grad, key_grad, value_grad = attend_backward(
            queries[chunks[c]],
            keys_values_ext[span, :head_width],
            keys_values_ext[span, head_width:],
            ids_ext[span],
            attended_grad,
            log_totals[c],
            head_count,
        )
        query_grads.append(query_grad.astype(jnp.bfloat16))
        both = jnp.concatenate([key_grad, value_grad], axis=1)
        if c == 0:
            back = from_behind(both[:WINDOW].astype(jnp.bfloat16), "seq", -1).astype(jnp.float32)
        else:
            key_value_grads.append(carry.at[-WINDOW:].add(both[:WINDOW]).astype(jnp.bfloat16))
        carry = both[WINDOW:]
    key_value_grads.append(carry.at[-WINDOW:].add(back).astype(jnp.bfloat16))
    middle_low_all = jnp.concatenate([m.astype(jnp.bfloat16) for m in middle_grads], axis=0)
    out_weight_grad = inner_rows(middle_low_all, jnp.concatenate(attended, axis=0)).astype(jnp.bfloat16)

    qkv_grads = [
        jnp.concatenate([q, kv], axis=1) for q, kv in zip(query_grads, key_value_grads)
    ]
    tokens_grads, gain_one_parts = [], []
    for c, own in enumerate(chunks):
        attn_term = times_transposed(qkv_grads[c], qkv_weight)
        gain_one_parts.append(jnp.sum(attn_term * unit_one[own], axis=0, keepdims=True))
        normed_attn_grad = line_sum(attn_term.astype(jnp.bfloat16), "mp")
        tokens_grads.append(
            middle_grads[c]
            + norm_backward(normed_attn_grad, unit_one[own], factor_one[own], gain_one)
        )
    tokens_grad = jnp.concatenate(tokens_grads, axis=0)
    qkv_weight_grad = inner_rows(normed_attn, jnp.concatenate(qkv_grads, axis=0)).astype(jnp.bfloat16)
    attn_share = lax.psum_scatter(
        jnp.concatenate([qkv_weight_grad, out_weight_grad], axis=1),
        "seq",
        scatter_dimension=0,
        tiled=True,
    ).astype(jnp.float32)
    gain_parts = jnp.concatenate([sum(gain_one_parts), sum(gain_two_parts)], axis=0)
    gain_share = small_sum(small_sum_scatter(gain_parts, "seq"), "mp")
    gate_up_share = gate_up_share.astype(jnp.float32)
    return (
        output_own,
        tokens_grad,
        gain_share[0],
        attn_share[:, :head_width],
        attn_share[:, head_width : 2 * head_width],
        attn_share[:, 2 * head_width : 3 * head_width],
        attn_share[:, 3 * head_width :].T,
        gain_share[1],
        gate_up_share[:, :hidden],
        gate_up_share[:, hidden:],
        down_share.astype(jnp.float32).T,
    )


def solution(mesh):
    placed = (
        P("seq", None),
        P("seq"),
        P("seq"),
        P("seq", "mp"),
        P("seq", "mp"),
        P("seq", "mp"),
        P("mp", "seq"),
        P("seq"),
        P("seq", "mp"),
        P("seq", "mp"),
        P("mp", "seq"),
        P("seq", None),
    )
    return jax.shard_map(
        body,
        mesh=mesh,
        in_specs=placed,
        out_specs=(
            P("seq", None),
            P("seq", None),
            P("seq"),
            P("seq", "mp"),
            P("seq", "mp"),
            P("seq", "mp"),
            P("mp", "seq"),
            P("seq"),
            P("seq", "mp"),
            P("seq", "mp"),
            P("mp", "seq"),
        ),
        check_vma=False,
    )
```

```python
import jax
import jax.numpy as jnp
from jax import lax
from jax.experimental import pallas as pl
from jax.experimental.pallas import tpu as pltpu
from jax.sharding import PartitionSpec as P

HEAD_DIM = 128
WINDOW = 64
CHUNKS = 4
QUERY_ROWS = 128
WIDE = 256

epsilon = 1e-05
masked_score = -1e30
score_scale = HEAD_DIM ** (-0.5)
MEGA = 1024 * 1024
low_type = jnp.bfloat16


def times(left, right):
    return jnp.dot(left, right, preferred_element_type=jnp.float32)


def times_transposed(left, right):
    return lax.dot_general(
        left, right, (((1,), (1,)), ((), ())), preferred_element_type=jnp.float32
    )


def inner_rows(left, right):
    return lax.dot_general(
        left, right, (((0,), (0,)), ((), ())), preferred_element_type=jnp.float32
    )


def row_scale(value_in):
    return lax.rsqrt(jnp.mean(value_in * value_in, axis=-1, keepdims=True) + epsilon)


def norm_backward(grad_normed, normed_unit, row_factor, gain_full):
    scaled_grad = grad_normed * gain_full
    return row_factor * (
        scaled_grad - normed_unit * jnp.mean(scaled_grad * normed_unit, axis=-1, keepdims=True)
    )


def line_result(place_ref, total_ref, outward_ref):
    place = place_ref[0]
    in_middle = (place == 1) | (place == 2)
    return jnp.where(in_middle, total_ref[...], outward_ref[...])


def allowed_pairs(query_ids, key_ids):
    shape = (query_ids.shape[0], key_ids.shape[1])
    query_pos = lax.broadcasted_iota(jnp.int32, shape, 0)
    key_pos = lax.broadcasted_iota(jnp.int32, shape, 1)
    inside = (key_pos >= query_pos) & (key_pos <= query_pos + WINDOW)
    return inside & (query_ids == key_ids) & (query_ids >= 0)


def probabilities(query, key, allowed, valid):
    scores = jnp.where(allowed, times_transposed(query, key) * score_scale, masked_score)
    top_score = jnp.max(scores, axis=-1, keepdims=True)
    weights = jnp.where(allowed, jnp.exp(scores - top_score), 0.0)
    totals = jnp.where(valid, jnp.sum(weights, axis=-1, keepdims=True), 1.0)
    return weights / totals


def attend_kernel(
    q_ref, k_ref, v_ref, k_before_ref, v_before_ref, query_ids_ref, key_ids_ref, out_weight_ref,
    *rest,
):
    attended_ref, term_ref = rest[-2:]
    rows, width = q_ref.shape
    for start in range(0, rows, QUERY_ROWS):
        stop = start + QUERY_ROWS
        query_ids = query_ids_ref[start:stop, :]
        allowed = allowed_pairs(query_ids, key_ids_ref[start // QUERY_ROWS])
        valid = query_ids >= 0
        for head in range(width // HEAD_DIM):
            columns = slice(head * HEAD_DIM, (head + 1) * HEAD_DIM)

            def with_before(ref, before_ref):
                if start == 0:
                    return jnp.concatenate([before_ref[:, columns], ref[:stop, columns]], axis=0)
                return ref[start - WINDOW : stop, columns]

            probs = probabilities(
                q_ref[start:stop, columns], with_before(k_ref, k_before_ref), allowed, valid
            )
            attended_ref[start:stop, columns] = times(
                probs.astype(low_type), with_before(v_ref, v_before_ref)
            ).astype(low_type)
    term_ref[...] = times_transposed(attended_ref[...], out_weight_ref[...]).astype(low_type)


def attend_back_kernel(
    place_ref, tokens_ref, attn_sum_ref, total_ref, outward_ref, cotangent_ref, gain_ref,
    q_ref, k_ref, v_ref, k_before_ref, v_before_ref, query_ids_ref, key_ids_ref, out_weight_ref,
    *rest,
):
    middle_grad_ref, low_ref, gain_part_ref, query_grad_ref, own_ref, before_ref, spread = rest[-7:]
    rows, width = q_ref.shape
    middle = tokens_ref[...].astype(jnp.float32) + attn_sum_ref[...].astype(jnp.float32)
    factor = row_scale(middle)
    unit = middle * factor
    grad_sum = line_result(place_ref, total_ref, outward_ref).astype(jnp.float32)
    gain_part_ref[...] = jnp.sum(grad_sum * unit, axis=0, keepdims=True)
    middle_grad = cotangent_ref[...].astype(jnp.float32) + norm_backward(
        grad_sum, unit, factor, gain_ref[...]
    )
    middle_grad_ref[...] = middle_grad
    low_ref[...] = middle_grad.astype(low_type)
    attended_grad = times(low_ref[...], out_weight_ref[...]).astype(low_type)
    spread[...] = jnp.zeros_like(spread)
    for start in range(0, rows, QUERY_ROWS):
        stop = start + QUERY_ROWS
        query_ids = query_ids_ref[start:stop, :]
        allowed = allowed_pairs(query_ids, key_ids_ref[start // QUERY_ROWS])
        valid = query_ids >= 0
        span = slice(start, stop + WINDOW)
        for head in range(width // HEAD_DIM):
            columns = slice(head * HEAD_DIM, (head + 1) * HEAD_DIM)
            value_columns = slice(width + head * HEAD_DIM, width + (head + 1) * HEAD_DIM)

            def with_before(ref, before_ref):
                if start == 0:
                    return jnp.concatenate([before_ref[:, columns], ref[:stop, columns]], axis=0)
                return ref[start - WINDOW : stop, columns]

            query = q_ref[start:stop, columns]
            key = with_before(k_ref, k_before_ref)
            out_grad = attended_grad[start:stop, columns]
            probs = probabilities(query, key, allowed, valid)
            prob_grad = times_transposed(out_grad, with_before(v_ref, v_before_ref))
            centre = jnp.sum(prob_grad * probs, axis=-1, keepdims=True)
            score_grad = (probs * (prob_grad - centre)).astype(low_type)
            query_grad_ref[start:stop, columns] = (times(score_grad, key) * score_scale).astype(
                low_type
            )
            spread[span, columns] += inner_rows(score_grad, query) * score_scale
            spread[span, value_columns] += inner_rows(probs.astype(low_type), out_grad)
    own_ref[...] = spread[WINDOW:, :]
    before_ref[...] = spread[:WINDOW, :]


def attn_term_kernel(
    query_grad_ref, own_ref, after_ref, weight_ref, tokens_ref, factor_ref, *rest
):
    grads_ref, term_ref, gain_part_ref = rest[-3:]
    rows, width = query_grad_ref.shape

    @pl.when(pl.program_id(0) == 0)
    def _():
        kept = rows - WINDOW
        grads_ref[:, :width] = query_grad_ref[...]
        grads_ref[:kept, width:] = own_ref[:kept, :].astype(low_type)
        grads_ref[kept:, width:] = (own_ref[kept:, :] + after_ref[...]).astype(low_type)

    term = times_transposed(grads_ref[...], weight_ref[...])
    term_ref[...] = term.astype(low_type)
    unit = tokens_ref[...].astype(jnp.float32) * factor_ref[...]
    gain_part_ref[...] = jnp.sum(term * unit, axis=0, keepdims=True)


def tokens_back_kernel(
    place_ref, middle_grad_ref, total_ref, outward_ref, tokens_ref, factor_ref, gain_ref, *rest
):
    factor = factor_ref[...]
    unit = tokens_ref[...].astype(jnp.float32) * factor
    grad_sum = line_result(place_ref, total_ref, outward_ref).astype(jnp.float32)
    rest[-1][...] = middle_grad_ref[...] + norm_backward(grad_sum, unit, factor, gain_ref[...])


def output_kernel(place_ref, tokens_ref, attn_sum_ref, total_ref, outward_ref, *rest):
    middle = tokens_ref[...].astype(jnp.float32) + attn_sum_ref[...].astype(jnp.float32)
    mlp_sum = line_result(place_ref, total_ref, outward_ref).astype(jnp.float32)
    rest[-1][...] = (middle + mlp_sum).astype(low_type)


def add_kernel(*refs):
    count = len(refs) // 3
    for left, right, result in zip(refs[:count], refs[count : 2 * count], refs[2 * count :]):
        result[...] = (left[...].astype(jnp.float32) + right[...].astype(jnp.float32)).astype(
            low_type
        )


def mlp_pieces(hidden):
    whole = hidden // WIDE * WIDE
    pieces = []
    for start in range(0, whole, WIDE):
        for k in range(3):
            pieces.append(slice(k * whole + start, k * whole + start + WIDE))
    pieces.append(slice(3 * whole, 3 * hidden))
    return whole, pieces


def mlp_layout(gate, up, down):
    whole = gate.shape[1] // WIDE * WIDE
    return jnp.concatenate(
        [m[:, :whole] for m in (gate, up, down)] + [m[:, whole:] for m in (gate, up, down)], axis=1
    )


def mlp_kernel(
    place_ref, tokens_ref, total_ref, outward_ref, cotangent_ref, gain_ref, weight_ref, *rest
):
    attn_sum_ref, normed_ref, activation_ref, grads_ref, term_ref, mlp_ref, held, arrived = rest[-8:]
    hidden = activation_ref.shape[1]
    whole, pieces = mlp_pieces(hidden)
    half = hidden - whole
    tail = 3 * whole
    copies = [
        pltpu.make_async_copy(weight_ref.at[:, piece], held.at[:, piece], arrived.at[i])
        for i, piece in enumerate(pieces)
    ]
    for copy in copies:
        copy.start()

    attn_sum = line_result(place_ref, total_ref, outward_ref)
    attn_sum_ref[...] = attn_sum
    middle = tokens_ref[...].astype(jnp.float32) + attn_sum.astype(jnp.float32)
    normed_ref[...] = (middle * row_scale(middle) * gain_ref[...]).astype(low_type)
    normed = normed_ref[...]
    cotangent = cotangent_ref[...]

    def inner(start, stop, gate, up, act_grad):
        sigmoid_gate = jax.nn.sigmoid(gate)
        silu_gate = gate * sigmoid_gate
        activation_ref[:, start:stop] = (silu_gate * up).astype(low_type)
        grads_ref[:, start:stop] = (
            act_grad * up * (sigmoid_gate + silu_gate * (1.0 - sigmoid_gate))
        ).astype(low_type)
        grads_ref[:, hidden + start : hidden + stop] = (act_grad * silu_gate).astype(low_type)

    for j in range(whole // WIDE):
        for copy in copies[3 * j : 3 * j + 3]:
            copy.wait()
        gate, up, down = (held[:, piece] for piece in pieces[3 * j : 3 * j + 3])
        inner(
            j * WIDE, (j + 1) * WIDE, times(normed, gate), times(normed, up), times(cotangent, down)
        )
    copies[-1].wait()
    both = times(normed, held[:, tail : tail + 2 * half])
    inner(
        whole, hidden, both[:, :half], both[:, half:], times(cotangent, held[:, tail + 2 * half :])
    )

    pair = jnp.concatenate([grads_ref[:, whole:hidden], grads_ref[:, hidden + whole :]], axis=1)
    for start in range(0, held.shape[0], WIDE):
        rows = slice(start, start + WIDE)
        term_ref[:, rows] = (
            times_transposed(grads_ref[:, :whole], held[rows, :whole])
            + times_transposed(grads_ref[:, hidden : hidden + whole], held[rows, whole : 2 * whole])
            + times_transposed(pair, held[rows, tail : tail + 2 * half])
        ).astype(low_type)
        mlp_ref[:, rows] = (
            times_transposed(activation_ref[:, :whole], held[rows, 2 * whole : tail])
            + times_transposed(activation_ref[:, whole:], held[rows, tail + 2 * half :])
        ).astype(low_type)


def block_of(shape, *place):
    return pl.BlockSpec(shape, lambda i: place)


smem = pl.BlockSpec(memory_space=pltpu.SMEM)
anywhere = pl.BlockSpec(memory_space=pl.ANY)


def call(kernel, name, operands, results, shared, steps=1, scratch=(), flops=0, extra_bytes=0):
    arrays = [array for array, _ in operands]
    specs = [spec for _, spec in operands]
    aliases = {}
    for index, kept in shared.items():
        if kept is not None:
            aliases[len(arrays)] = index
            arrays.append(kept)
            specs.append(anywhere)
    return pl.pallas_call(
        kernel,
        grid=(steps,),
        in_specs=specs,
        out_specs=[spec for _, _, spec in results],
        out_shape=[jax.ShapeDtypeStruct(shape, dtype) for shape, dtype, _ in results],
        input_output_aliases=aliases,
        scratch_shapes=list(scratch),
        compiler_params=pltpu.CompilerParams(
            dimension_semantics=("arbitrary",), vmem_limit_bytes=56 * MEGA
        ),
        cost_estimate=pl.CostEstimate(
            flops=flops, bytes_accessed=8 * MEGA + extra_bytes, transcendentals=0
        ),
        name=name,
    )(*arrays)


class Layer:
    def __init__(self, tokens, cotangent, head_width, hidden):
        self.tokens, self.cotangent = tokens, cotangent
        self.total_rows, self.width = tokens.shape
        self.rows = self.total_rows // CHUNKS
        self.head_width, self.hidden = head_width, hidden
        self.place = lax.axis_index("mp").astype(jnp.int32).reshape(1)
        self.whole = block_of((self.rows, self.width), 0, 0)
        self.gain_row = block_of((1, self.width), 0, 0)

    def chunk(self, c, columns=None):
        return block_of((self.rows, columns or self.width), c, 0)

    def qkv_operands(self, c, qkv, halo, query_ids, key_ids):
        rows, head_width = self.rows, self.head_width
        own = [(qkv, block_of((rows, head_width), c, k)) for k in range(3)]
        if c == 0:
            before = [(halo, block_of((WINDOW, head_width), 0, k)) for k in range(2)]
        else:
            last = c * rows // WINDOW - 1
            before = [(qkv, block_of((WINDOW, head_width), last, k + 1)) for k in range(2)]
        parts = rows // QUERY_ROWS
        ids = [
            (query_ids, block_of((rows, 1), c, 0)),
            (key_ids, block_of((parts, 1, QUERY_ROWS + WINDOW), c, 0, 0)),
        ]
        return own + before + ids

    def attend(self, c, qkv_operands, attn_weight, attended):
        return call(
            attend_kernel,
            "attend",
            qkv_operands + [(attn_weight, block_of((self.width, self.head_width), 0, 3))],
            [
                ((self.total_rows, self.head_width), low_type, self.chunk(c, self.head_width)),
                ((self.rows, self.width), low_type, self.whole),
            ],
            {0: attended},
            flops=4 * self.rows * self.width * self.head_width,
        )

    def feed_forward(self, c, line, gain, weight, shared):
        rows, width, hidden = self.rows, self.width, self.hidden
        return call(
            mlp_kernel,
            "feed_forward",
            [
                (self.place, smem),
                (self.tokens, self.chunk(c)),
                (line[0], self.whole),
                (line[1], self.whole),
                (self.cotangent, self.chunk(c)),
                (gain, self.gain_row),
                (weight, anywhere),
            ],
            [
                ((rows, width), low_type, self.whole),
                ((self.total_rows, width), low_type, self.chunk(c)),
                ((self.total_rows, hidden), low_type, self.chunk(c, hidden)),
                ((self.total_rows, 2 * hidden), low_type, self.chunk(c, 2 * hidden)),
                ((rows, width), low_type, self.whole),
                ((rows, width), low_type, self.whole),
            ],
            {index + 1: kept for index, kept in enumerate(shared)},
            scratch=[
                pltpu.VMEM((width, 3 * hidden), low_type),
                pltpu.SemaphoreType.DMA((len(mlp_pieces(hidden)[1]),)),
            ],
            flops=12 * rows * width * hidden,
            extra_bytes=6 * width * hidden,
        )

    def attend_back(self, c, attn_sum, line, gain, qkv_operands, attn_weight, low_all):
        rows, width, head_width = self.rows, self.width, self.head_width
        return call(
            attend_back_kernel,
            "attend_back",
            [
                (self.place, smem),
                (self.tokens, self.chunk(c)),
                (attn_sum, self.whole),
                (line[0], self.whole),
                (line[1], self.whole),
                (self.cotangent, self.chunk(c)),
                (gain, self.gain_row),
            ]
            + qkv_operands
            + [(attn_weight, block_of((width, head_width), 0, 3))],
            [
                ((rows, width), jnp.float32, self.whole),
                ((self.total_rows, width), low_type, self.chunk(c)),
                ((1, width), jnp.float32, self.gain_row),
                ((rows, head_width), low_type, block_of((rows, head_width), 0, 0)),
                ((rows, 2 * head_width), jnp.float32, block_of((rows, 2 * head_width), 0, 0)),
                ((WINDOW, 2 * head_width), jnp.float32, block_of((WINDOW, 2 * head_width), 0, 0)),
            ],
            {1: low_all},
            scratch=[pltpu.VMEM((rows + WINDOW, 2 * head_width), jnp.float32)],
            flops=6 * rows * width * head_width,
        )

    def attn_term(self, c, query_grad, own, after, attn_weight, factor, grads_all):
        rows, width, head_width = self.rows, self.width, self.head_width
        part = width // CHUNKS
        return call(
            attn_term_kernel,
            "attn_term",
            [
                (query_grad, block_of((rows, head_width), 0, 0)),
                (own, block_of((rows, 2 * head_width), 0, 0)),
                (after, block_of((WINDOW, 2 * head_width), 0, 0)),
                (attn_weight, pl.BlockSpec((part, 3 * head_width), lambda i: (i, 0))),
                (self.tokens, pl.BlockSpec((rows, part), lambda i: (c, i))),
                (factor, block_of((rows, 1), c, 0)),
            ],
            [
                ((self.total_rows, 3 * head_width), low_type, self.chunk(c, 3 * head_width)),
                ((rows, width), low_type, pl.BlockSpec((rows, part), lambda i: (0, i))),
                ((1, width), jnp.float32, pl.BlockSpec((1, part), lambda i: (0, i))),
            ],
            {0: grads_all},
            steps=width // part,
            flops=6 * rows * width * head_width,
        )

    def tokens_back(self, c, middle_grad, line, factor, gain, tokens_grad):
        return call(
            tokens_back_kernel,
            "tokens_back",
            [
                (self.place, smem),
                (middle_grad, self.whole),
                (line[0], self.whole),
                (line[1], self.whole),
                (self.tokens, self.chunk(c)),
                (factor, block_of((self.rows, 1), c, 0)),
                (gain, self.gain_row),
            ],
            [((self.total_rows, self.width), jnp.float32, self.chunk(c))],
            {0: tokens_grad},
        )[0]

    def output(self, c, attn_sum, line, out):
        return call(
            output_kernel,
            "output",
            [
                (self.place, smem),
                (self.tokens, self.chunk(c)),
                (attn_sum, self.whole),
                (line[0], self.whole),
                (line[1], self.whole),
            ],
            [((self.total_rows, self.width), low_type, self.chunk(c))],
            {0: out},
        )[0]


def from_behind(block, axis, distance):
    devices = range(lax.axis_size(axis))
    route = [(i - distance, i) for i in devices if i - distance in devices]
    return lax.ppermute(block, axis, route)


def hold(values):
    return lax.optimization_barrier(values)


def add_low(left, right):
    return (left.astype(jnp.float32) + right.astype(jnp.float32)).astype(low_type)


class LineSums:
    def __init__(self, axis):
        self.axis = axis
        self.first = self.second = self.third = None

    def step(self, part, values):
        first, second, third = self.first, self.second, self.third
        own = None if first is None else first[0]
        half = None if second is None else second[0]
        part, own, half, values = hold((part, own, half, values))
        new_half = new_total = sent = across = outward = None
        if part is not None:
            sent = lax.ppermute(part, self.axis, [(0, 1), (3, 2)])
        if own is not None:
            new_half = add_low(own, first[1])
            across = lax.ppermute(new_half, self.axis, [(1, 2), (2, 1)])
        if half is not None:
            new_total = add_low(half, second[1])
            outward = lax.ppermute(new_total, self.axis, [(1, 0), (2, 3)])
        new_half, new_total, done, values = hold((new_half, new_total, third, values))
        self.first = None if part is None else (part, sent)
        self.second = None if new_half is None else (new_half, across)
        self.third = None if new_total is None else (new_total, outward)
        return done, values


def small_sum_scatter(value, axis):
    size = lax.axis_size(axis)
    place = lax.axis_index(axis)
    bit = size // 2
    while bit >= 1:
        half = value.shape[1] // 2
        low, high = value[:, :half], value[:, half:]
        upper = (place & bit) != 0
        keep = jnp.where(upper, high, low)
        give = jnp.where(upper, low, high)
        value = keep + lax.ppermute(give, axis, [(i, i ^ bit) for i in range(size)])
        bit //= 2
    return value


def small_sum(value, axis):
    size = lax.axis_size(axis)
    bit = 1
    while bit < size:
        value = value + lax.ppermute(value, axis, [(i, i ^ bit) for i in range(size)])
        bit *= 2
    return value


def scattered(value):
    return lax.psum_scatter(value, "seq", scatter_dimension=0, tiled=True)


def body(
    tokens,
    group_ids,
    gain_attn,
    w_query,
    w_key,
    w_value,
    w_out,
    gain_mlp,
    w_gate,
    w_up,
    w_down,
    cotangent,
):
    head_width = w_query.shape[1]
    hidden = w_gate.shape[1]
    layer = Layer(tokens, cotangent, head_width, hidden)
    line = LineSums("mp")
    total_rows = tokens.shape[0]

    attn_shard = jnp.concatenate([w_query, w_key, w_value, w_out.T], axis=1)
    attn_weight = lax.all_gather(attn_shard, "seq", axis=0, tiled=True)
    mlp_shard = mlp_layout(w_gate, w_up, w_down.T)
    mlp_shard, attn_weight = hold((mlp_shard, attn_weight))
    mlp_weight = lax.all_gather(mlp_shard, "seq", axis=0, tiled=True)
    gains = lax.all_gather(jnp.stack([gain_attn, gain_mlp]), "seq", axis=1, tiled=True)
    gain_one = gains[:1].astype(jnp.float32)
    gain_two = gains[1:].astype(jnp.float32)

    ids_halo = from_behind(group_ids[-WINDOW:] + 1, "seq", 1) - 1
    ids_ext = jnp.concatenate([ids_halo, group_ids], axis=0)
    query_ids = group_ids[:, None]
    key_ids = jnp.stack(
        [
            ids_ext[None, start : start + QUERY_ROWS + WINDOW]
            for start in range(0, total_rows, QUERY_ROWS)
        ]
    )
    inputs = tokens.astype(jnp.float32)
    factor_one = row_scale(inputs)
    normed_attn = (inputs * factor_one * gain_one).astype(low_type)
    qkv = times(normed_attn, attn_weight[:, : 3 * head_width]).astype(low_type)
    halo = from_behind(qkv[-WINDOW:, head_width:], "seq", 1)

    def pieces_of(c, qkv):
        return layer.qkv_operands(c, qkv, halo, query_ids, key_ids)

    attended, term = layer.attend(0, pieces_of(0, qkv), attn_weight, None)
    for c in range(1, CHUNKS):
        done, (attended, qkv) = line.step(term, (attended, qkv))
        attended, term = layer.attend(c, pieces_of(c, qkv), attn_weight, attended)
    done, (attended, qkv) = line.step(term, (attended, qkv))

    attn_sums, mlp_terms = [], []
    shared = (None, None, None)
    for c in range(CHUNKS):
        attn_sum, normed_mlp, activations, mlp_grads, term, mlp_term = layer.feed_forward(
            c, done, gain_two, mlp_weight, shared
        )
        attn_sums.append(attn_sum)
        mlp_terms.append(mlp_term)
        done, shared = line.step(term, (normed_mlp, activations, mlp_grads))
    normed_mlp, activations, mlp_grads = shared

    low_all = grads_all = tokens_grad = out = None
    middle_grads, gain_one_parts, gain_two_parts = [], [], []
    tokens_lines, out_lines = {}, {}

    def back(c, done, low_all):
        return layer.attend_back(
            c, attn_sums[c], done, gain_two, pieces_of(c, qkv), attn_weight, low_all
        )

    def term_of(c, query_grad, own, after, grads_all):
        return layer.attn_term(c, query_grad, own, after, attn_weight, factor_one, grads_all)

    middle_grad, low_all, part, query_grad, own, before = back(0, done, None)
    middle_grads.append(middle_grad)
    gain_two_parts.append(part)
    behind = from_behind(before.astype(low_type), "seq", -1)
    down_grad = inner_rows(cotangent, activations).astype(low_type)
    done, (low_all, query_grad, own, down_grad, mlp_grads) = line.step(
        mlp_terms[0], (low_all, query_grad, own, down_grad, mlp_grads)
    )
    down_share = scattered(down_grad)
    for c in range(1, CHUNKS):
        middle_grad, low_all, part, next_query_grad, next_own, before = back(c, done, low_all)
        middle_grads.append(middle_grad)
        gain_two_parts.append(part)
        grads_all, term, part = term_of(c - 1, query_grad, own, before, grads_all)
        gain_one_parts.append(part)
        query_grad, own = next_query_grad, next_own
        values = (low_all, query_grad, own, grads_all, mlp_grads)
        if c == 1:
            done, values = line.step(term, values)
            low_all, query_grad, own, grads_all, mlp_grads = values
        elif c == 2:
            gate_up_grad = inner_rows(normed_mlp, mlp_grads).astype(low_type)
            done, (values, gate_up_grad) = line.step(term, (values, gate_up_grad))
            low_all, query_grad, own, grads_all, mlp_grads = values
            gate_up_share = scattered(gate_up_grad)
        else:
            out_lines[0], values = line.step(term, values)
            low_all, query_grad, own, grads_all, mlp_grads = values
    grads_all, term, part = term_of(3, query_grad, own, behind.astype(jnp.float32), grads_all)
    gain_one_parts.append(part)
    qkv_grad = inner_rows(normed_attn, grads_all).astype(low_type)
    out_grad = inner_rows(low_all, attended).astype(low_type)
    attn_grad = jnp.concatenate([qkv_grad, out_grad], axis=1)
    gain_parts = jnp.concatenate([sum(gain_one_parts), sum(gain_two_parts)], axis=0)
    tokens_lines[0], (attn_grad, gain_parts) = line.step(term, (attn_grad, gain_parts))
    attn_share = scattered(attn_grad)
    gain_share = small_sum_scatter(gain_parts, "seq")
    gain_attn_share = small_sum(gain_share[:1], "mp")[0]
    out = layer.output(0, attn_sums[0], out_lines[0], None)
    for c in range(CHUNKS):
        tokens_grad = layer.tokens_back(
            c, middle_grads[c], tokens_lines[c], factor_one, gain_one, tokens_grad
        )
        if c + 1 < CHUNKS:
            tokens_lines[c + 1], (tokens_grad, out) = line.step(mlp_terms[c + 1], (tokens_grad, out))
    down_out = down_share.astype(jnp.float32).T
    out_lines[1], (tokens_grad, out, down_out) = line.step(None, (tokens_grad, out, down_out))
    out = layer.output(1, attn_sums[1], out_lines[1], out)
    gate_out = gate_up_share[:, :hidden].astype(jnp.float32)
    up_out = gate_up_share[:, hidden:].astype(jnp.float32)
    out_lines[2], (out, gate_out, up_out) = line.step(None, (out, gate_out, up_out))
    out = layer.output(2, attn_sums[2], out_lines[2], out)
    out_lines[3], out = line.step(None, out)
    out = layer.output(3, attn_sums[3], out_lines[3], out)
    attn_share = attn_share.astype(jnp.float32)
    return (
        out,
        tokens_grad,
        gain_attn_share,
        attn_share[:, :head_width],
        attn_share[:, head_width : 2 * head_width],
        attn_share[:, 2 * head_width : 3 * head_width],
        attn_share[:, 3 * head_width :].T,
        gain_share[1],
        gate_out,
        up_out,
        down_out,
    )


def solution(mesh):
    placed = (
        P("seq", None),
        P("seq"),
        P("seq"),
        P("seq", "mp"),
        P("seq", "mp"),
        P("seq", "mp"),
        P("mp", "seq"),
        P("seq"),
        P("seq", "mp"),
        P("seq", "mp"),
        P("mp", "seq"),
        P("seq", None),
    )
    return jax.shard_map(
        body,
        mesh=mesh,
        in_specs=placed,
        out_specs=(
            P("seq", None),
            P("seq", None),
            P("seq"),
            P("seq", "mp"),
            P("seq", "mp"),
            P("seq", "mp"),
            P("mp", "seq"),
            P("seq"),
            P("seq", "mp"),
            P("seq", "mp"),
            P("mp", "seq"),
        ),
        check_vma=False,
    )
```

```python
import functools

import jax
import jax.numpy as jnp
from jax import lax
from jax.experimental import pallas as pl
from jax.experimental.pallas import tpu as pltpu
from jax.sharding import PartitionSpec as P

HEAD_DIM = 128
WINDOW = 64
CHUNKS = 4
QUERY_ROWS = 128
WIDE = 256

epsilon = 1e-05
masked_score = -1e30
score_scale = HEAD_DIM ** (-0.5)
MEGA = 1024 * 1024
low_type = jnp.bfloat16


def times(left, right):
    return jnp.dot(left, right, preferred_element_type=jnp.float32)


def times_transposed(left, right):
    return lax.dot_general(
        left, right, (((1,), (1,)), ((), ())), preferred_element_type=jnp.float32
    )


def inner_rows(left, right):
    return lax.dot_general(
        left, right, (((0,), (0,)), ((), ())), preferred_element_type=jnp.float32
    )


def row_scale(value_in):
    return lax.rsqrt(jnp.mean(value_in * value_in, axis=-1, keepdims=True) + epsilon)


def norm_backward(grad_normed, normed_unit, row_factor, gain_full):
    scaled_grad = grad_normed * gain_full
    return row_factor * (
        scaled_grad - normed_unit * jnp.mean(scaled_grad * normed_unit, axis=-1, keepdims=True)
    )


def line_result(place_ref, total_ref, outward_ref):
    place = place_ref[0]
    in_middle = (place == 1) | (place == 2)
    return jnp.where(in_middle, total_ref[...], outward_ref[...])


def allowed_pairs(query_ids, key_ids):
    shape = (query_ids.shape[0], key_ids.shape[1])
    query_pos = lax.broadcasted_iota(jnp.int32, shape, 0)
    key_pos = lax.broadcasted_iota(jnp.int32, shape, 1)
    inside = (key_pos >= query_pos) & (key_pos <= query_pos + WINDOW)
    return inside & (query_ids == key_ids) & (query_ids >= 0)


def probabilities(query, key, allowed, valid):
    scores = jnp.where(allowed, times_transposed(query, key) * score_scale, masked_score)
    top_score = jnp.max(scores, axis=-1, keepdims=True)
    weights = jnp.where(allowed, jnp.exp(scores - top_score), 0.0)
    totals = jnp.where(valid, jnp.sum(weights, axis=-1, keepdims=True), 1.0)
    return weights / totals


def keys_of(step, first_refs, before_refs, refs, columns):
    out = []
    for first_ref, before_ref, ref in zip(first_refs, before_refs, refs):
        before = before_ref[:, columns]
        if first_ref is not None:
            before = jnp.where(step == 0, first_ref[:, columns], before)
        out.append(jnp.concatenate([before, ref[:, columns]], axis=0))
    return out


def split_refs(first, refs):
    q_ref, k_ref, v_ref, k_before, v_before = refs[:5]
    firsts = refs[5:7] if first else (None, None)
    refs = refs[7 if first else 5 :]
    return (q_ref, (k_ref, v_ref), (k_before, v_before), firsts), refs[:2], refs[2:]


def attend_kernel(first, *refs):
    (q_ref, own, before, firsts), (query_ids_ref, key_ids_ref), rest = split_refs(first, refs)
    out_weight_ref = rest[0]
    attended_ref, term_ref = rest[-2:]
    step = pl.program_id(0)
    query_ids = query_ids_ref[...]
    allowed = allowed_pairs(query_ids, key_ids_ref[0])
    valid = query_ids >= 0
    for head in range(q_ref.shape[1] // HEAD_DIM):
        columns = slice(head * HEAD_DIM, (head + 1) * HEAD_DIM)
        key, value = keys_of(step, firsts, before, own, columns)
        probs = probabilities(q_ref[:, columns], key, allowed, valid)
        attended_ref[:, columns] = times(probs.astype(low_type), value).astype(low_type)
    term_ref[...] = times_transposed(attended_ref[...], out_weight_ref[...]).astype(low_type)


def attend_back_kernel(
    first, place_ref, tokens_ref, attn_sum_ref, total_ref, outward_ref, cotangent_ref, gain_ref, *refs
):
    (q_ref, own, before, firsts), (query_ids_ref, key_ids_ref), rest = split_refs(first, refs)
    out_weight_ref = rest[0]
    low_ref, gain_part_ref, query_grad_ref, own_ref, before_ref, spread = rest[-6:]
    step = pl.program_id(0)
    rows, width = q_ref.shape
    middle = tokens_ref[...].astype(jnp.float32) + attn_sum_ref[...].astype(jnp.float32)
    factor = row_scale(middle)
    unit = middle * factor
    grad_sum = line_result(place_ref, total_ref, outward_ref).astype(jnp.float32)
    gain_part = jnp.sum(grad_sum * unit, axis=0, keepdims=True)
    middle_grad = cotangent_ref[...].astype(jnp.float32) + norm_backward(
        grad_sum, unit, factor, gain_ref[...]
    )
    low_ref[...] = middle_grad.astype(low_type)
    attended_grad = times(low_ref[...], out_weight_ref[...]).astype(low_type)

    @pl.when(step == 0)
    def _():
        gain_part_ref[...] = gain_part
        spread[...] = jnp.zeros_like(spread)

    @pl.when(step > 0)
    def _():
        gain_part_ref[...] += gain_part

    query_ids = query_ids_ref[...]
    allowed = allowed_pairs(query_ids, key_ids_ref[0])
    valid = query_ids >= 0
    span = pl.ds(pl.multiple_of(step * rows, rows), rows + WINDOW)
    for head in range(width // HEAD_DIM):
        columns = slice(head * HEAD_DIM, (head + 1) * HEAD_DIM)
        value_columns = slice(width + head * HEAD_DIM, width + (head + 1) * HEAD_DIM)
        query = q_ref[:, columns]
        key, value = keys_of(step, firsts, before, own, columns)
        out_grad = attended_grad[:, columns]
        probs = probabilities(query, key, allowed, valid)
        prob_grad = times_transposed(out_grad, value)
        centre = jnp.sum(prob_grad * probs, axis=-1, keepdims=True)
        score_grad = (probs * (prob_grad - centre)).astype(low_type)
        query_grad_ref[:, columns] = (times(score_grad, key) * score_scale).astype(low_type)
        spread[span, columns] += inner_rows(score_grad, query) * score_scale
        spread[span, value_columns] += inner_rows(probs.astype(low_type), out_grad)

    @pl.when(step == pl.num_programs(0) - 1)
    def _():
        own_ref[...] = spread[WINDOW:, :]
        before_ref[...] = spread[:WINDOW, :]


def attn_term_kernel(query_grad_ref, own_ref, after_ref, weight_ref, *rest):
    grads_ref, term_ref = rest[-2:]
    rows, width = query_grad_ref.shape

    @pl.when(pl.program_id(0) == 0)
    def _():
        kept = rows - WINDOW
        grads_ref[:, :width] = query_grad_ref[...]
        grads_ref[:kept, width:] = own_ref[:kept, :].astype(low_type)
        grads_ref[kept:, width:] = (own_ref[kept:, :] + after_ref[...]).astype(low_type)

    term_ref[...] = times_transposed(grads_ref[...], weight_ref[...]).astype(low_type)


def attn_weight_grads_kernel(normed_ref, low_ref, grads_ref, attended_ref, result_ref):
    step = pl.program_id(0)

    @pl.when(step < 3)
    def _():
        result_ref[...] = inner_rows(normed_ref[...], grads_ref[...]).astype(low_type)

    @pl.when(step == 3)
    def _():
        result_ref[...] = inner_rows(low_ref[...], attended_ref[...]).astype(low_type)


def tokens_back_kernel(
    place_ref, middle_grad_ref, total_ref, outward_ref, tokens_ref, factor_ref, gain_ref, *rest
):
    tokens_grad_ref, gain_part_ref = rest[-2:]
    factor = factor_ref[...]
    unit = tokens_ref[...].astype(jnp.float32) * factor
    grad_sum = line_result(place_ref, total_ref, outward_ref).astype(jnp.float32)
    tokens_grad_ref[...] = middle_grad_ref[...].astype(jnp.float32) + norm_backward(
        grad_sum, unit, factor, gain_ref[...]
    )
    gain_part = jnp.sum(grad_sum * unit, axis=0, keepdims=True)

    @pl.when(pl.program_id(0) == 0)
    def _():
        gain_part_ref[...] = gain_part

    @pl.when(pl.program_id(0) > 0)
    def _():
        gain_part_ref[...] += gain_part


def output_kernel(place_ref, tokens_ref, attn_sum_ref, total_ref, outward_ref, *rest):
    middle = tokens_ref[...].astype(jnp.float32) + attn_sum_ref[...].astype(jnp.float32)
    mlp_sum = line_result(place_ref, total_ref, outward_ref).astype(jnp.float32)
    rest[-1][...] = (middle + mlp_sum).astype(low_type)


def mlp_pieces(hidden):
    whole = hidden // WIDE * WIDE
    pieces = []
    for start in range(0, whole, WIDE):
        for k in range(3):
            pieces.append(slice(k * whole + start, k * whole + start + WIDE))
    pieces.append(slice(3 * whole, 3 * hidden))
    return whole, pieces


def mlp_layout(gate, up, down):
    whole = gate.shape[1] // WIDE * WIDE
    return jnp.concatenate(
        [m[:, :whole] for m in (gate, up, down)] + [m[:, whole:] for m in (gate, up, down)], axis=1
    )


def mlp_kernel(
    first_row, place_ref, tokens_ref, total_ref, outward_ref, cotangent_ref, gain_ref, weight_ref, *rest
):
    leaving = rest[-13:-9]
    term_ref, mlp_ref, attn_sum_ref, normed_ref, activation_ref, grads_ref, held, arrived, left = rest[-9:]
    hidden = activation_ref.shape[1]
    whole, pieces = mlp_pieces(hidden)
    half = hidden - whole
    tail = 3 * whole
    copies = [
        pltpu.make_async_copy(weight_ref.at[:, piece], held.at[:, piece], arrived.at[i])
        for i, piece in enumerate(pieces)
    ]
    for copy in copies:
        copy.start()

    attn_sum = line_result(place_ref, total_ref, outward_ref)
    attn_sum_ref[...] = attn_sum
    middle = tokens_ref[...].astype(jnp.float32) + attn_sum.astype(jnp.float32)
    normed_ref[...] = (middle * row_scale(middle) * gain_ref[...]).astype(low_type)
    normed = normed_ref[...]
    cotangent = cotangent_ref[...]

    def inner(start, stop, gate, up, act_grad):
        sigmoid_gate = jax.nn.sigmoid(gate)
        silu_gate = gate * sigmoid_gate
        activation_ref[:, start:stop] = (silu_gate * up).astype(low_type)
        grads_ref[:, start:stop] = (
            act_grad * up * (sigmoid_gate + silu_gate * (1.0 - sigmoid_gate))
        ).astype(low_type)
        grads_ref[:, hidden + start : hidden + stop] = (act_grad * silu_gate).astype(low_type)

    for j in range(whole // WIDE):
        for copy in copies[3 * j : 3 * j + 3]:
            copy.wait()
        gate, up, down = (held[:, piece] for piece in pieces[3 * j : 3 * j + 3])
        inner(
            j * WIDE, (j + 1) * WIDE, times(normed, gate), times(normed, up), times(cotangent, down)
        )
    copies[-1].wait()
    both = times(normed, held[:, tail : tail + 2 * half])
    inner(
        whole, hidden, both[:, :half], both[:, half:], times(cotangent, held[:, tail + 2 * half :])
    )

    out_copies = []
    for i, (source, target) in enumerate(
        zip((attn_sum_ref, normed_ref, activation_ref, grads_ref), leaving)
    ):
        rows = slice(0, None) if i == 0 else pl.ds(first_row, source.shape[0])
        out_copies.append(pltpu.make_async_copy(source, target.at[rows], left.at[i]))
        out_copies[-1].start()

    pair = jnp.concatenate([grads_ref[:, whole:hidden], grads_ref[:, hidden + whole :]], axis=1)
    for start in range(0, held.shape[0], WIDE):
        rows = slice(start, start + WIDE)
        term_ref[:, rows] = (
            times_transposed(grads_ref[:, :whole], held[rows, :whole])
            + times_transposed(grads_ref[:, hidden : hidden + whole], held[rows, whole : 2 * whole])
            + times_transposed(pair, held[rows, tail : tail + 2 * half])
        ).astype(low_type)
        mlp_ref[:, rows] = (
            times_transposed(activation_ref[:, :whole], held[rows, 2 * whole : tail])
            + times_transposed(activation_ref[:, whole:], held[rows, tail + 2 * half :])
        ).astype(low_type)
    for copy in out_copies:
        copy.wait()


def block_of(shape, *place):
    return pl.BlockSpec(shape, lambda i: place)


smem = pl.BlockSpec(memory_space=pltpu.SMEM)
anywhere = pl.BlockSpec(memory_space=pl.ANY)


def call(kernel, name, operands, results, shared, steps=1, scratch=(), flops=0, extra_bytes=0):
    arrays = [array for array, _ in operands]
    specs = [spec for _, spec in operands]
    aliases = {}
    for index, kept in shared.items():
        if kept is not None:
            aliases[len(arrays)] = index
            arrays.append(kept)
            specs.append(anywhere)
    return pl.pallas_call(
        kernel,
        grid=(steps,),
        in_specs=specs,
        out_specs=[spec for _, _, spec in results],
        out_shape=[jax.ShapeDtypeStruct(shape, dtype) for shape, dtype, _ in results],
        input_output_aliases=aliases,
        scratch_shapes=list(scratch),
        compiler_params=pltpu.CompilerParams(
            dimension_semantics=("arbitrary",), vmem_limit_bytes=56 * MEGA
        ),
        cost_estimate=pl.CostEstimate(
            flops=flops, bytes_accessed=8 * MEGA + extra_bytes, transcendentals=0
        ),
        name=name,
    )(*arrays)


class Layer:
    def __init__(self, tokens, cotangent, head_width, hidden):
        self.tokens, self.cotangent = tokens, cotangent
        self.total_rows, self.width = tokens.shape
        self.rows = self.total_rows // CHUNKS
        self.head_width, self.hidden = head_width, hidden
        self.place = lax.axis_index("mp").astype(jnp.int32).reshape(1)
        self.whole = block_of((self.rows, self.width), 0, 0)
        self.gain_row = block_of((1, self.width), 0, 0)

    def chunk(self, c, columns=None):
        return block_of((self.rows, columns or self.width), c, 0)

    def qkv_operands(self, c, halves, halo, query_ids, key_ids):
        head_width = self.head_width
        half_rows = halves[0].shape[0]
        half, first_row = divmod(c * self.rows, half_rows)
        first_part, first_window = first_row // QUERY_ROWS, first_row // WINDOW
        stride = QUERY_ROWS // WINDOW

        def part(k):
            return pl.BlockSpec((QUERY_ROWS, head_width), lambda i: (first_part + i, k))

        def before(k):
            return pl.BlockSpec(
                (WINDOW, head_width),
                lambda i: (jnp.maximum(first_window + stride * i - 1, 0), k),
            )

        source = halves[half]
        operands = [(source, part(k)) for k in range(3)]
        operands += [(source, before(k)) for k in (1, 2)]
        if c == 0:
            operands += [(halo, block_of((WINDOW, head_width), 0, k)) for k in range(2)]
        elif first_row == 0:
            last = half_rows // WINDOW - 1
            operands += [
                (halves[half - 1], block_of((WINDOW, head_width), last, k)) for k in (1, 2)
            ]
        parts = self.rows // QUERY_ROWS
        ids = [
            (query_ids, pl.BlockSpec((QUERY_ROWS, 1), lambda i: (c * parts + i, 0))),
            (
                key_ids,
                pl.BlockSpec((1, 1, QUERY_ROWS + WINDOW), lambda i: (c * parts + i, 0, 0)),
            ),
        ]
        return first_row == 0, operands + ids

    def part(self, c, columns):
        parts = self.rows // QUERY_ROWS
        return pl.BlockSpec((QUERY_ROWS, columns), lambda i: (c * parts + i, 0))

    def attend(self, c, first_and_qkv, attn_weight, attended):
        first, qkv_operands = first_and_qkv
        return call(
            functools.partial(attend_kernel, first),
            "attend",
            qkv_operands + [(attn_weight, block_of((self.width, self.head_width), 0, 3))],
            [
                ((self.total_rows, self.head_width), low_type, self.part(c, self.head_width)),
                ((self.rows, self.width), low_type, self.part(0, self.width)),
            ],
            {0: attended},
            steps=self.rows // QUERY_ROWS,
            flops=4 * self.rows * self.width * self.head_width,
        )

    def feed_forward(self, c, line, gain, weight, shared):
        rows, width, hidden = self.rows, self.width, self.hidden
        return call(
            functools.partial(mlp_kernel, c * rows),
            "feed_forward",
            [
                (self.place, smem),
                (self.tokens, self.chunk(c)),
                (line[0], self.whole),
                (line[1], self.whole),
                (self.cotangent, self.chunk(c)),
                (gain, self.gain_row),
                (weight, anywhere),
            ],
            [
                ((rows, width), low_type, anywhere),
                ((self.total_rows, width), low_type, anywhere),
                ((self.total_rows, hidden), low_type, anywhere),
                ((self.total_rows, 2 * hidden), low_type, anywhere),
                ((rows, width), low_type, self.whole),
                ((rows, width), low_type, self.whole),
            ],
            {index + 1: kept for index, kept in enumerate(shared)},
            scratch=[
                pltpu.VMEM((rows, width), low_type),
                pltpu.VMEM((rows, width), low_type),
                pltpu.VMEM((rows, hidden), low_type),
                pltpu.VMEM((rows, 2 * hidden), low_type),
                pltpu.VMEM((width, 3 * hidden), low_type),
                pltpu.SemaphoreType.DMA((len(mlp_pieces(hidden)[1]),)),
                pltpu.SemaphoreType.DMA((4,)),
            ],
            flops=12 * rows * width * hidden,
            extra_bytes=6 * width * hidden,
        )

    def attend_back(self, c, attn_sum, line, gain, first_and_qkv, attn_weight, low_all):
        first, qkv_operands = first_and_qkv
        rows, width, head_width = self.rows, self.width, self.head_width
        own, alone = self.part(c, width), self.part(0, width)
        return call(
            functools.partial(attend_back_kernel, first),
            "attend_back",
            [
                (self.place, smem),
                (self.tokens, own),
                (attn_sum, alone),
                (line[0], alone),
                (line[1], alone),
                (self.cotangent, own),
                (gain, self.gain_row),
            ]
            + qkv_operands
            + [(attn_weight, block_of((width, head_width), 0, 3))],
            [
                ((self.total_rows, width), low_type, own),
                ((1, width), jnp.float32, self.gain_row),
                ((rows, head_width), low_type, self.part(0, head_width)),
                ((rows, 2 * head_width), jnp.float32, block_of((rows, 2 * head_width), 0, 0)),
                ((WINDOW, 2 * head_width), jnp.float32, block_of((WINDOW, 2 * head_width), 0, 0)),
            ],
            {0: low_all},
            steps=rows // QUERY_ROWS,
            scratch=[pltpu.VMEM((rows + WINDOW, 2 * head_width), jnp.float32)],
            flops=6 * rows * width * head_width,
        )

    def attn_term(self, c, query_grad, own, after, attn_weight, grads_all):
        rows, width, head_width = self.rows, self.width, self.head_width
        part = width // CHUNKS
        return call(
            attn_term_kernel,
            "attn_term",
            [
                (query_grad, block_of((rows, head_width), 0, 0)),
                (own, block_of((rows, 2 * head_width), 0, 0)),
                (after, block_of((WINDOW, 2 * head_width), 0, 0)),
                (attn_weight, pl.BlockSpec((part, 3 * head_width), lambda i: (i, 0))),
            ],
            [
                ((self.total_rows, 3 * head_width), low_type, self.chunk(c, 3 * head_width)),
                ((rows, width), low_type, pl.BlockSpec((rows, part), lambda i: (0, i))),
            ],
            {0: grads_all},
            steps=width // part,
            flops=6 * rows * width * head_width,
        )

    def attn_weight_grads(self, normed_attn, grads_all, low_all, attended):
        rows, width, head_width = self.total_rows, self.width, self.head_width
        return call(
            attn_weight_grads_kernel,
            "attn_weight_grads",
            [
                (normed_attn, block_of((rows, width), 0, 0)),
                (low_all, block_of((rows, width), 0, 0)),
                (grads_all, pl.BlockSpec((rows, head_width), lambda i: (0, jnp.minimum(i, 2)))),
                (attended, block_of((rows, head_width), 0, 0)),
            ],
            [((width, 4 * head_width), low_type, pl.BlockSpec((width, head_width), lambda i: (0, i)))],
            {},
            steps=4,
            flops=8 * rows * width * head_width,
        )[0]

    def tokens_back(self, c, middle_grad, line, factor, gain, tokens_grad):
        return call(
            tokens_back_kernel,
            "tokens_back",
            [
                (self.place, smem),
                (middle_grad, self.part(c, self.width)),
                (line[0], self.part(0, self.width)),
                (line[1], self.part(0, self.width)),
                (self.tokens, self.part(c, self.width)),
                (factor, self.part(c, 1)),
                (gain, self.gain_row),
            ],
            [
                ((self.total_rows, self.width), jnp.float32, self.part(c, self.width)),
                ((1, self.width), jnp.float32, self.gain_row),
            ],
            {0: tokens_grad},
            steps=self.rows // QUERY_ROWS,
        )

    def output(self, c, attn_sum, line, out):
        return call(
            output_kernel,
            "output",
            [
                (self.place, smem),
                (self.tokens, self.part(c, self.width)),
                (attn_sum, self.part(0, self.width)),
                (line[0], self.part(0, self.width)),
                (line[1], self.part(0, self.width)),
            ],
            [((self.total_rows, self.width), low_type, self.part(c, self.width))],
            {0: out},
            steps=self.rows // QUERY_ROWS,
        )[0]


def from_behind(block, axis, distance):
    devices = range(lax.axis_size(axis))
    route = [(i - distance, i) for i in devices if i - distance in devices]
    return lax.ppermute(block, axis, route)


def hold(values):
    return lax.optimization_barrier(values)


def add_low(left, right):
    return (left.astype(jnp.float32) + right.astype(jnp.float32)).astype(low_type)


class LineSums:
    def __init__(self, axis):
        self.axis = axis
        self.first = self.second = self.third = None
        self.results = {}

    def step(self, name, part, values, early=False):
        first, second, third = self.first, self.second, self.third
        own = None if first is None else first[1]
        half = None if second is None else second[1]
        part, own, half, values = hold((part, own, half, values))
        self.first = self.second = self.third = None
        new_half = new_total = done = None
        if early and part is not None:
            self.first = (name, part, lax.ppermute(part, self.axis, [(0, 1), (3, 2)]))
        if own is not None:
            new_half = add_low(own, first[2])
            across = lax.ppermute(new_half, self.axis, [(1, 2), (2, 1)])
        if half is not None:
            new_total = add_low(half, second[2])
            outward = lax.ppermute(new_total, self.axis, [(1, 0), (2, 3)])
        if third is not None:
            done = third[1:]
        new_half, new_total, done, part, values = hold((new_half, new_total, done, part, values))
        if not early and part is not None:
            self.first = (name, part, lax.ppermute(part, self.axis, [(0, 1), (3, 2)]))
        if own is not None:
            self.second = (first[0], new_half, across)
        if half is not None:
            self.third = (second[0], new_total, outward)
        if third is not None:
            self.results[third[0]] = done
        return values


def small_sum_scatter(value, axis):
    size = lax.axis_size(axis)
    place = lax.axis_index(axis)
    bit = size // 2
    while bit >= 1:
        half = value.shape[1] // 2
        low, high = value[:, :half], value[:, half:]
        upper = (place & bit) != 0
        keep = jnp.where(upper, high, low)
        give = jnp.where(upper, low, high)
        value = keep + lax.ppermute(give, axis, [(i, i ^ bit) for i in range(size)])
        bit //= 2
    return value


def scattered(value):
    return lax.psum_scatter(value, "seq", scatter_dimension=0, tiled=True)


def body(
    tokens,
    group_ids,
    gain_attn,
    w_query,
    w_key,
    w_value,
    w_out,
    gain_mlp,
    w_gate,
    w_up,
    w_down,
    cotangent,
):
    head_width = w_query.shape[1]
    hidden = w_gate.shape[1]
    layer = Layer(tokens, cotangent, head_width, hidden)
    line = LineSums("mp")
    results = line.results
    total_rows = tokens.shape[0]

    attn_shard = jnp.concatenate([w_query, w_key, w_value, w_out.T], axis=1)
    attn_weight = lax.all_gather(attn_shard, "seq", axis=0, tiled=True)
    gains = lax.all_gather(jnp.stack([gain_attn, gain_mlp]), "seq", axis=1, tiled=True)
    gain_one = gains[:1].astype(jnp.float32)
    gain_two = gains[1:].astype(jnp.float32)
    ids_halo = from_behind(group_ids[-WINDOW:] + 1, "seq", 1) - 1
    ids_ext = jnp.concatenate([ids_halo, group_ids], axis=0)
    query_ids = group_ids[:, None]
    key_ids = jnp.stack(
        [
            ids_ext[None, start : start + QUERY_ROWS + WINDOW]
            for start in range(0, total_rows, QUERY_ROWS)
        ]
    )
    inputs = tokens.astype(jnp.float32)
    factor_one = row_scale(inputs)
    normed_attn = (inputs * factor_one * gain_one).astype(low_type)
    mlp_shard = mlp_layout(w_gate, w_up, w_down.T)
    mlp_shard, normed_attn, factor_one, query_ids, key_ids, gain_two, attn_weight = hold(
        (mlp_shard, normed_attn, factor_one, query_ids, key_ids, gain_two, attn_weight)
    )
    mlp_weight = lax.all_gather(mlp_shard, "seq", axis=0, tiled=True)

    half_rows = total_rows // 2
    qkv_weight = attn_weight[:, : 3 * head_width]
    halves = [times(normed_attn[:half_rows], qkv_weight).astype(low_type)]
    order = [1, 2, 3, 0]

    def pieces_of(c):
        return layer.qkv_operands(c, halves, halo, query_ids, key_ids)

    halo = None
    attended, term = layer.attend(order[0], pieces_of(order[0]), attn_weight, None)
    attended, later_rows, halves[0] = line.step(
        ("attn", order[0]), term, (attended, normed_attn[half_rows:], halves[0])
    )
    halves.append(times(later_rows, qkv_weight).astype(low_type))
    halo = from_behind(halves[1][-WINDOW:, head_width:], "seq", 1)
    for c in order[1:]:
        attended, term = layer.attend(c, pieces_of(c), attn_weight, attended)
        values = line.step(("attn", c), term, (attended, halves[0], halves[1], halo))
        attended, halves[0], halves[1], halo = values

    attn_sums, mlp_terms = {}, {}
    shared = (None, None, None)
    for c in order:
        attn_sums[c], *shared, term, mlp_terms[c] = layer.feed_forward(
            c, results["attn", c], gain_two, mlp_weight, shared
        )
        shared = line.step(("mlp", c), term, tuple(shared))
    normed_mlp, activations, mlp_grads = shared

    low_all = grads_all = tokens_grad = out = None
    query_grads, owns, befores = {}, {}, {}
    gain_one_parts, gain_two_parts = [], []

    def back(c):
        nonlocal low_all
        low_all, part, query_grads[c], owns[c], befores[c] = layer.attend_back(
            c, attn_sums[c], results["mlp", c], gain_two, pieces_of(c), attn_weight, low_all
        )
        gain_two_parts.append(part)

    def term_of(c, after):
        nonlocal grads_all
        grads_all, term = layer.attn_term(
            c, query_grads[c], owns[c], after, attn_weight, grads_all
        )
        return term

    def out_step(c, values, early=False):
        return line.step(("out", c), mlp_terms[c], values, early)

    gate_up_grad = inner_rows(normed_mlp, mlp_grads).astype(low_type)
    gate_up_grad, activations = out_step(order[0], (gate_up_grad, activations))
    gate_up_share = scattered(gate_up_grad)
    back(order[0])
    down_grad = inner_rows(cotangent, activations).astype(low_type)
    low_all, down_grad = out_step(order[1], (low_all, down_grad))
    down_share = scattered(down_grad)
    back(order[1])
    term = term_of(order[0], befores[order[1]])
    low_all, grads_all = line.step(("attn_back", order[0]), term, (low_all, grads_all))
    back(order[2])
    term = term_of(order[1], befores[order[2]])
    low_all, grads_all = line.step(("attn_back", order[1]), term, (low_all, grads_all))
    back(order[3])
    behind = from_behind(befores[0].astype(low_type), "seq", -1)
    term = term_of(0, befores[1])
    low_all, grads_all, behind = line.step(("attn_back", 0), term, (low_all, grads_all, behind))
    term = term_of(3, behind.astype(jnp.float32))
    attn_grad = layer.attn_weight_grads(normed_attn, grads_all, low_all, attended)
    attn_grad = line.step(("attn_back", 3), term, attn_grad)
    attn_share = scattered(attn_grad)

    def finish_tokens(c):
        nonlocal tokens_grad
        tokens_grad, part = layer.tokens_back(
            c, low_all, results["attn_back", c], factor_one, gain_one, tokens_grad
        )
        gain_one_parts.append(part)

    def finish_out(c):
        nonlocal out
        out = layer.output(c, attn_sums[c], results["out", c], out)

    finish_tokens(1)
    tokens_grad, gain_two_parts = out_step(order[2], (tokens_grad, gain_two_parts), True)
    finish_out(order[0])
    finish_tokens(2)
    tokens_grad, out = out_step(order[3], (tokens_grad, out), True)
    finish_tokens(0)
    finish_out(order[1])
    tokens_grad, out = line.step(None, None, (tokens_grad, out))
    finish_tokens(3)
    gain_parts = jnp.concatenate([sum(gain_one_parts), sum(gain_two_parts)], axis=0)
    gate_out = gate_up_share[:, :hidden].astype(jnp.float32)
    up_out = gate_up_share[:, hidden:].astype(jnp.float32)
    values = line.step(None, None, (tokens_grad, out, gain_parts, gate_out, up_out))
    tokens_grad, out, gain_parts, gate_out, up_out = values
    gain_share = small_sum_scatter(gain_parts, "seq")
    finish_out(order[2])
    down_out = down_share.astype(jnp.float32).T
    out, gain_share, down_out = line.step(None, None, (out, gain_share, down_out))
    finish_out(order[3])
    attn_out = attn_share.astype(jnp.float32)
    attn_outs = [attn_out[:, k * head_width : (k + 1) * head_width] for k in range(4)]
    attn_outs[3] = attn_outs[3].T
    return (
        out,
        tokens_grad,
        gain_share[0],
        attn_outs[0],
        attn_outs[1],
        attn_outs[2],
        attn_outs[3],
        gain_share[1],
        gate_out,
        up_out,
        down_out,
    )


def solution(mesh):
    placed = (
        P("seq", None),
        P("seq"),
        P("seq"),
        P("seq", "mp"),
        P("seq", "mp"),
        P("seq", "mp"),
        P("mp", "seq"),
        P("seq"),
        P("seq", "mp"),
        P("seq", "mp"),
        P("mp", "seq"),
        P("seq", None),
    )
    return jax.shard_map(
        body,
        mesh=mesh,
        in_specs=placed,
        out_specs=(
            P("seq", None),
            P("seq", None),
            P("seq"),
            P("seq", "mp"),
            P("seq", "mp"),
            P("seq", "mp"),
            P("mp", "seq"),
            P("seq"),
            P("seq", "mp"),
            P("seq", "mp"),
            P("mp", "seq"),
        ),
        check_vma=False,
    )
```

```python
import functools

import jax
import jax.numpy as jnp
from jax import lax
from jax.experimental import pallas as pl
from jax.experimental.pallas import tpu as pltpu
from jax.sharding import PartitionSpec as P

HEAD_DIM = 128
WINDOW = 64
CHUNKS = 4
QUERY_ROWS = 128
WIDE = 256

epsilon = 1e-05
masked_score = -1e30
score_scale = HEAD_DIM ** (-0.5)
MEGA = 1024 * 1024
low_type = jnp.bfloat16


def times(left, right):
    return jnp.dot(left, right, preferred_element_type=jnp.float32)


def times_transposed(left, right):
    return lax.dot_general(
        left, right, (((1,), (1,)), ((), ())), preferred_element_type=jnp.float32
    )


def inner_rows(left, right):
    return lax.dot_general(
        left, right, (((0,), (0,)), ((), ())), preferred_element_type=jnp.float32
    )


def row_scale(value_in):
    return lax.rsqrt(jnp.mean(value_in * value_in, axis=-1, keepdims=True) + epsilon)


def norm_backward(grad_normed, normed_unit, row_factor, gain_full):
    scaled_grad = grad_normed * gain_full
    return row_factor * (
        scaled_grad - normed_unit * jnp.mean(scaled_grad * normed_unit, axis=-1, keepdims=True)
    )


def line_result(place_ref, total_ref, outward_ref):
    place = place_ref[0]
    in_middle = (place == 1) | (place == 2)
    return jnp.where(in_middle, total_ref[...], outward_ref[...])


def allowed_pairs(query_ids, key_ids):
    shape = (query_ids.shape[0], key_ids.shape[1])
    query_pos = lax.broadcasted_iota(jnp.int32, shape, 0)
    key_pos = lax.broadcasted_iota(jnp.int32, shape, 1)
    inside = (key_pos >= query_pos) & (key_pos <= query_pos + WINDOW)
    return inside & (query_ids == key_ids) & (query_ids >= 0)


def probabilities(query, key, allowed, valid):
    scores = jnp.where(allowed, times_transposed(query, key) * score_scale, masked_score)
    top_score = jnp.max(scores, axis=-1, keepdims=True)
    weights = jnp.where(allowed, jnp.exp(scores - top_score), 0.0)
    totals = jnp.where(valid, jnp.sum(weights, axis=-1, keepdims=True), 1.0)
    return weights / totals


def keys_of(step, first_refs, before_refs, refs, columns):
    out = []
    for first_ref, before_ref, ref in zip(first_refs, before_refs, refs):
        before = before_ref[:, columns]
        if first_ref is not None:
            before = jnp.where(step == 0, first_ref[:, columns], before)
        out.append(jnp.concatenate([before, ref[:, columns]], axis=0))
    return out


def split_refs(first, refs):
    q_ref, k_ref, v_ref, k_before, v_before = refs[:5]
    firsts = refs[5:7] if first else (None, None)
    refs = refs[7 if first else 5 :]
    return (q_ref, (k_ref, v_ref), (k_before, v_before), firsts), refs[:2], refs[2:]


def attend_kernel(first, *refs):
    (q_ref, own, before, firsts), (query_ids_ref, key_ids_ref), rest = split_refs(first, refs)
    out_weight_ref = rest[0]
    attended_ref, term_ref = rest[-2:]
    step = pl.program_id(0)
    query_ids = query_ids_ref[...]
    allowed = allowed_pairs(query_ids, key_ids_ref[0])
    valid = query_ids >= 0
    for head in range(q_ref.shape[1] // HEAD_DIM):
        columns = slice(head * HEAD_DIM, (head + 1) * HEAD_DIM)
        key, value = keys_of(step, firsts, before, own, columns)
        probs = probabilities(q_ref[:, columns], key, allowed, valid)
        attended_ref[:, columns] = times(probs.astype(low_type), value).astype(low_type)
    term_ref[...] = times_transposed(attended_ref[...], out_weight_ref[...]).astype(low_type)


def attend_back_kernel(
    first, names, counts, place_ref, tokens_ref, attn_sum_ref, total_ref, outward_ref, cotangent_ref,
    gain_ref, *refs,
):
    (q_ref, own, before, firsts), (query_ids_ref, key_ids_ref), rest = split_refs(first, refs)
    out_weight_ref = rest[0]
    inputs = dict(zip(names[0], rest[1 : 1 + counts[0]]))
    outputs = dict(zip(names[1], rest[1 + counts[0] + counts[1] :]))
    scratch = rest[1 + counts[0] + counts[1] + len(names[1]) :]
    spread, query_grads = scratch[:2]
    step = pl.program_id(0)
    last = pl.num_programs(0) - 1
    rows, width = q_ref.shape
    if "weight" in inputs:
        held, arrived = scratch[2:]
        fetch = pltpu.make_async_copy(
            inputs["weight"].at[:, : held.shape[1]], held, arrived
        )

        @pl.when(step == 0)
        def _():
            fetch.start()

    middle = tokens_ref[...].astype(jnp.float32) + attn_sum_ref[...].astype(jnp.float32)
    factor = row_scale(middle)
    unit = middle * factor
    grad_sum = line_result(place_ref, total_ref, outward_ref).astype(jnp.float32)
    gain_part = jnp.sum(grad_sum * unit, axis=0, keepdims=True)
    middle_grad = cotangent_ref[...].astype(jnp.float32) + norm_backward(
        grad_sum, unit, factor, gain_ref[...]
    )
    low = middle_grad.astype(low_type)
    outputs["low"][...] = low
    attended_grad = times(low, out_weight_ref[...]).astype(low_type)

    @pl.when(step == 0)
    def _():
        outputs["gain_part"][...] = gain_part
        spread[...] = jnp.zeros_like(spread)

    @pl.when(step > 0)
    def _():
        outputs["gain_part"][...] += gain_part

    query_ids = query_ids_ref[...]
    allowed = allowed_pairs(query_ids, key_ids_ref[0])
    valid = query_ids >= 0
    part = pl.ds(pl.multiple_of(step * rows, rows), rows)
    span = pl.ds(pl.multiple_of(step * rows, rows), rows + WINDOW)
    for head in range(width // HEAD_DIM):
        columns = slice(head * HEAD_DIM, (head + 1) * HEAD_DIM)
        value_columns = slice(width + head * HEAD_DIM, width + (head + 1) * HEAD_DIM)
        query = q_ref[:, columns]
        key, value = keys_of(step, firsts, before, own, columns)
        out_grad = attended_grad[:, columns]
        probs = probabilities(query, key, allowed, valid)
        prob_grad = times_transposed(out_grad, value)
        centre = jnp.sum(prob_grad * probs, axis=-1, keepdims=True)
        score_grad = (probs * (prob_grad - centre)).astype(low_type)
        query_grads[part, columns] = (times(score_grad, key) * score_scale).astype(low_type)
        spread[span, columns] += inner_rows(score_grad, query) * score_scale
        spread[span, value_columns] += inner_rows(probs.astype(low_type), out_grad)

    @pl.when(step == last)
    def _():
        if "own" in outputs:
            outputs["query_grad"][...] = query_grads[...]
            outputs["own"][...] = spread[WINDOW:, :].astype(low_type)
        if "before" in outputs:
            outputs["before"][...] = spread[:WINDOW, :]
        if "weight" not in inputs:
            return
        grads_ref = outputs["grads"]
        kept = grads_ref.shape[0] - WINDOW
        if "own" in inputs:
            grads_ref[:, :width] = inputs["query_grad"][...]
            grads_ref[:kept, width:] = inputs["own"][:kept, :]
            tail, after = inputs["own"][kept:, :].astype(jnp.float32), spread[:WINDOW, :]
        else:
            grads_ref[:, :width] = query_grads[...]
            grads_ref[:kept, width:] = spread[WINDOW : WINDOW + kept, :].astype(low_type)
            tail, after = spread[WINDOW + kept :, :], inputs["after"][...]
        grads_ref[kept:, width:] = (tail + after).astype(low_type)
        fetch.wait()
        outputs["term"][...] = times_transposed(grads_ref[...], held[...]).astype(low_type)


def attn_term_kernel(query_grad_ref, own_ref, after_ref, weight_ref, *rest):
    grads_ref, term_ref = rest[-2:]
    rows, width = query_grad_ref.shape

    @pl.when(pl.program_id(0) == 0)
    def _():
        kept = rows - WINDOW
        grads_ref[:, :width] = query_grad_ref[...]
        grads_ref[:kept, width:] = own_ref[:kept, :]
        grads_ref[kept:, width:] = (
            own_ref[kept:, :].astype(jnp.float32) + after_ref[...]
        ).astype(low_type)

    term_ref[...] = times_transposed(grads_ref[...], weight_ref[...]).astype(low_type)


def attn_weight_grads_kernel(normed_ref, low_ref, grads_ref, attended_ref, result_ref):
    step = pl.program_id(0)

    @pl.when(step < 3)
    def _():
        result_ref[...] = inner_rows(normed_ref[...], grads_ref[...]).astype(low_type)

    @pl.when(step == 3)
    def _():
        result_ref[...] = inner_rows(low_ref[...], attended_ref[...]).astype(low_type)


def tokens_back_kernel(
    place_ref, middle_grad_ref, total_ref, outward_ref, tokens_ref, factor_ref, gain_ref, *rest
):
    tokens_grad_ref, gain_part_ref = rest[-2:]
    factor = factor_ref[...]
    unit = tokens_ref[...].astype(jnp.float32) * factor
    grad_sum = line_result(place_ref, total_ref, outward_ref).astype(jnp.float32)
    tokens_grad_ref[...] = middle_grad_ref[...].astype(jnp.float32) + norm_backward(
        grad_sum, unit, factor, gain_ref[...]
    )
    gain_part = jnp.sum(grad_sum * unit, axis=0, keepdims=True)

    @pl.when(pl.program_id(0) == 0)
    def _():
        gain_part_ref[...] = gain_part

    @pl.when(pl.program_id(0) > 0)
    def _():
        gain_part_ref[...] += gain_part


def output_kernel(place_ref, tokens_ref, attn_sum_ref, total_ref, outward_ref, *rest):
    middle = tokens_ref[...].astype(jnp.float32) + attn_sum_ref[...].astype(jnp.float32)
    mlp_sum = line_result(place_ref, total_ref, outward_ref).astype(jnp.float32)
    rest[-1][...] = (middle + mlp_sum).astype(low_type)


def mlp_pieces(hidden):
    whole = hidden // WIDE * WIDE
    pieces = []
    for start in range(0, whole, WIDE):
        for k in range(3):
            pieces.append(slice(k * whole + start, k * whole + start + WIDE))
    pieces.append(slice(3 * whole, 3 * hidden))
    return whole, pieces


def mlp_layout(gate, up, down):
    whole = gate.shape[1] // WIDE * WIDE
    return jnp.concatenate(
        [m[:, :whole] for m in (gate, up, down)] + [m[:, whole:] for m in (gate, up, down)], axis=1
    )


def mlp_kernel(
    first_row, place_ref, tokens_ref, total_ref, outward_ref, cotangent_ref, gain_ref, weight_ref, *rest
):
    leaving = rest[-13:-9]
    term_ref, mlp_ref, attn_sum_ref, normed_ref, activation_ref, grads_ref, held, arrived, left = rest[-9:]
    hidden = activation_ref.shape[1]
    whole, pieces = mlp_pieces(hidden)
    half = hidden - whole
    tail = 3 * whole
    copies = [
        pltpu.make_async_copy(weight_ref.at[:, piece], held.at[:, piece], arrived.at[i])
        for i, piece in enumerate(pieces)
    ]
    for copy in copies:
        copy.start()

    attn_sum = line_result(place_ref, total_ref, outward_ref)
    attn_sum_ref[...] = attn_sum
    middle = tokens_ref[...].astype(jnp.float32) + attn_sum.astype(jnp.float32)
    normed_ref[...] = (middle * row_scale(middle) * gain_ref[...]).astype(low_type)
    normed = normed_ref[...]
    cotangent = cotangent_ref[...]

    def inner(start, stop, gate, up, act_grad):
        sigmoid_gate = jax.nn.sigmoid(gate)
        silu_gate = gate * sigmoid_gate
        activation_ref[:, start:stop] = (silu_gate * up).astype(low_type)
        grads_ref[:, start:stop] = (
            act_grad * up * (sigmoid_gate + silu_gate * (1.0 - sigmoid_gate))
        ).astype(low_type)
        grads_ref[:, hidden + start : hidden + stop] = (act_grad * silu_gate).astype(low_type)

    for j in range(whole // WIDE):
        for copy in copies[3 * j : 3 * j + 3]:
            copy.wait()
        gate, up, down = (held[:, piece] for piece in pieces[3 * j : 3 * j + 3])
        inner(
            j * WIDE, (j + 1) * WIDE, times(normed, gate), times(normed, up), times(cotangent, down)
        )
    copies[-1].wait()
    both = times(normed, held[:, tail : tail + 2 * half])
    inner(
        whole, hidden, both[:, :half], both[:, half:], times(cotangent, held[:, tail + 2 * half :])
    )

    out_copies = []
    for i, (source, target) in enumerate(
        zip((attn_sum_ref, normed_ref, activation_ref, grads_ref), leaving)
    ):
        rows = slice(0, None) if i == 0 else pl.ds(first_row, source.shape[0])
        out_copies.append(pltpu.make_async_copy(source, target.at[rows], left.at[i]))
        out_copies[-1].start()

    pair = jnp.concatenate([grads_ref[:, whole:hidden], grads_ref[:, hidden + whole :]], axis=1)
    for start in range(0, held.shape[0], WIDE):
        rows = slice(start, start + WIDE)
        term_ref[:, rows] = (
            times_transposed(grads_ref[:, :whole], held[rows, :whole])
            + times_transposed(grads_ref[:, hidden : hidden + whole], held[rows, whole : 2 * whole])
            + times_transposed(pair, held[rows, tail : tail + 2 * half])
        ).astype(low_type)
        mlp_ref[:, rows] = (
            times_transposed(activation_ref[:, :whole], held[rows, 2 * whole : tail])
            + times_transposed(activation_ref[:, whole:], held[rows, tail + 2 * half :])
        ).astype(low_type)
    for copy in out_copies:
        copy.wait()


def block_of(shape, *place):
    return pl.BlockSpec(shape, lambda i: place)


smem = pl.BlockSpec(memory_space=pltpu.SMEM)
anywhere = pl.BlockSpec(memory_space=pl.ANY)


def call(kernel, name, operands, results, shared, steps=1, scratch=()):
    arrays = [array for array, _ in operands]
    specs = [spec for _, spec in operands]
    aliases = {}
    for index, kept in shared.items():
        if kept is not None:
            aliases[len(arrays)] = index
            arrays.append(kept)
            specs.append(anywhere)
    return pl.pallas_call(
        kernel,
        grid=(steps,),
        in_specs=specs,
        out_specs=[spec for _, _, spec in results],
        out_shape=[jax.ShapeDtypeStruct(shape, dtype) for shape, dtype, _ in results],
        input_output_aliases=aliases,
        scratch_shapes=list(scratch),
        compiler_params=pltpu.CompilerParams(
            dimension_semantics=("arbitrary",), vmem_limit_bytes=56 * MEGA
        ),
        cost_estimate=pl.CostEstimate(flops=1, bytes_accessed=1, transcendentals=0),
        name=name,
    )(*arrays)


class Layer:
    def __init__(self, tokens, cotangent, head_width, hidden):
        self.tokens, self.cotangent = tokens, cotangent
        self.total_rows, self.width = tokens.shape
        self.rows = self.total_rows // CHUNKS
        self.head_width, self.hidden = head_width, hidden
        self.place = lax.axis_index("mp").astype(jnp.int32).reshape(1)
        self.whole = block_of((self.rows, self.width), 0, 0)
        self.gain_row = block_of((1, self.width), 0, 0)

    def chunk(self, c, columns=None):
        return block_of((self.rows, columns or self.width), c, 0)

    def qkv_operands(self, c, halves, halo, query_ids, key_ids):
        head_width = self.head_width
        half_rows = halves[0].shape[0]
        half, first_row = divmod(c * self.rows, half_rows)
        first_part, first_window = first_row // QUERY_ROWS, first_row // WINDOW
        stride = QUERY_ROWS // WINDOW

        def part(k):
            return pl.BlockSpec((QUERY_ROWS, head_width), lambda i: (first_part + i, k))

        def before(k):
            return pl.BlockSpec(
                (WINDOW, head_width),
                lambda i: (jnp.maximum(first_window + stride * i - 1, 0), k),
            )

        source = halves[half]
        operands = [(source, part(k)) for k in range(3)]
        operands += [(source, before(k)) for k in (1, 2)]
        if c == 0:
            operands += [(halo, block_of((WINDOW, head_width), 0, k)) for k in range(2)]
        elif first_row == 0:
            last = half_rows // WINDOW - 1
            operands += [
                (halves[half - 1], block_of((WINDOW, head_width), last, k)) for k in (1, 2)
            ]
        parts = self.rows // QUERY_ROWS
        ids = [
            (query_ids, pl.BlockSpec((QUERY_ROWS, 1), lambda i: (c * parts + i, 0))),
            (
                key_ids,
                pl.BlockSpec((1, 1, QUERY_ROWS + WINDOW), lambda i: (c * parts + i, 0, 0)),
            ),
        ]
        return first_row == 0, operands + ids

    def part(self, c, columns):
        parts = self.rows // QUERY_ROWS
        return pl.BlockSpec((QUERY_ROWS, columns), lambda i: (c * parts + i, 0))

    def attend(self, c, first_and_qkv, attn_weight, attended):
        first, qkv_operands = first_and_qkv
        return call(
            functools.partial(attend_kernel, first),
            "attend",
            qkv_operands + [(attn_weight, block_of((self.width, self.head_width), 0, 3))],
            [
                ((self.total_rows, self.head_width), low_type, self.part(c, self.head_width)),
                ((self.rows, self.width), low_type, self.part(0, self.width)),
            ],
            {0: attended},
            steps=self.rows // QUERY_ROWS,
        )

    def feed_forward(self, c, line, gain, weight, shared):
        rows, width, hidden = self.rows, self.width, self.hidden
        return call(
            functools.partial(mlp_kernel, c * rows),
            "feed_forward",
            [
                (self.place, smem),
                (self.tokens, self.chunk(c)),
                (line[0], self.whole),
                (line[1], self.whole),
                (self.cotangent, self.chunk(c)),
                (gain, self.gain_row),
                (weight, anywhere),
            ],
            [
                ((rows, width), low_type, anywhere),
                ((self.total_rows, width), low_type, anywhere),
                ((self.total_rows, hidden), low_type, anywhere),
                ((self.total_rows, 2 * hidden), low_type, anywhere),
                ((rows, width), low_type, self.whole),
                ((rows, width), low_type, self.whole),
            ],
            {index + 1: kept for index, kept in enumerate(shared)},
            scratch=[
                pltpu.VMEM((rows, width), low_type),
                pltpu.VMEM((rows, width), low_type),
                pltpu.VMEM((rows, hidden), low_type),
                pltpu.VMEM((rows, 2 * hidden), low_type),
                pltpu.VMEM((width, 3 * hidden), low_type),
                pltpu.SemaphoreType.DMA((len(mlp_pieces(hidden)[1]),)),
                pltpu.SemaphoreType.DMA((4,)),
            ],
        )

    def attend_back(
        self, c, attn_sum, line, gain, first_and_qkv, attn_weight, low_all,
        keep=False, give_before=False, earlier=None, after=None, grads_all=None,
    ):
        first, qkv_operands = first_and_qkv
        rows, width, head_width = self.rows, self.width, self.head_width
        mine, alone = self.part(c, width), self.part(0, width)
        query_spec = block_of((rows, head_width), 0, 0)
        own_spec = block_of((rows, 2 * head_width), 0, 0)
        window_spec = block_of((WINDOW, 2 * head_width), 0, 0)
        more, results = {}, {
            "low": ((self.total_rows, width), low_type, mine),
            "gain_part": ((1, width), jnp.float32, self.gain_row),
        }
        shared = {0: low_all}
        scratch = [
            pltpu.VMEM((rows + WINDOW, 2 * head_width), jnp.float32),
            pltpu.VMEM((rows, head_width), low_type),
        ]
        if keep:
            results["query_grad"] = ((rows, head_width), low_type, query_spec)
            results["own"] = ((rows, 2 * head_width), low_type, own_spec)
        if give_before:
            results["before"] = ((WINDOW, 2 * head_width), jnp.float32, window_spec)
        term_chunk = None
        if earlier is not None:
            term_chunk = earlier[0]
            more["query_grad"], more["own"] = (earlier[1], query_spec), (earlier[2], own_spec)
        elif after is not None:
            term_chunk = c
            more["after"] = (after, window_spec)
        if term_chunk is not None:
            more["weight"] = (attn_weight, anywhere)
            shared[len(results)] = grads_all
            results["grads"] = (
                (self.total_rows, 3 * head_width),
                low_type,
                block_of((rows, 3 * head_width), term_chunk, 0),
            )
            results["term"] = ((rows, width), low_type, self.whole)
            scratch += [pltpu.VMEM((width, 3 * head_width), low_type), pltpu.SemaphoreType.DMA]
        kept = sum(array is not None for array in shared.values())
        outputs = call(
            functools.partial(
                attend_back_kernel, first, (tuple(more), tuple(results)), (len(more), kept)
            ),
            "attend_back",
            [
                (self.place, smem),
                (self.tokens, mine),
                (attn_sum, alone),
                (line[0], alone),
                (line[1], alone),
                (self.cotangent, mine),
                (gain, self.gain_row),
            ]
            + qkv_operands
            + [(attn_weight, block_of((width, head_width), 0, 3))]
            + list(more.values()),
            list(results.values()),
            shared,
            steps=rows // QUERY_ROWS,
            scratch=scratch,
        )
        return dict(zip(results, outputs))

    def attn_term(self, c, query_grad, own, after, attn_weight, grads_all):
        rows, width, head_width = self.rows, self.width, self.head_width
        part = width // CHUNKS
        return call(
            attn_term_kernel,
            "attn_term",
            [
                (query_grad, block_of((rows, head_width), 0, 0)),
                (own, block_of((rows, 2 * head_width), 0, 0)),
                (after, block_of((WINDOW, 2 * head_width), 0, 0)),
                (attn_weight, pl.BlockSpec((part, 3 * head_width), lambda i: (i, 0))),
            ],
            [
                ((self.total_rows, 3 * head_width), low_type, self.chunk(c, 3 * head_width)),
                ((rows, width), low_type, pl.BlockSpec((rows, part), lambda i: (0, i))),
            ],
            {0: grads_all},
            steps=width // part,
        )

    def attn_weight_grads(self, normed_attn, grads_all, low_all, attended):
        rows, width, head_width = self.total_rows, self.width, self.head_width
        return call(
            attn_weight_grads_kernel,
            "attn_weight_grads",
            [
                (normed_attn, block_of((rows, width), 0, 0)),
                (low_all, block_of((rows, width), 0, 0)),
                (grads_all, pl.BlockSpec((rows, head_width), lambda i: (0, jnp.minimum(i, 2)))),
                (attended, block_of((rows, head_width), 0, 0)),
            ],
            [((width, 4 * head_width), low_type, pl.BlockSpec((width, head_width), lambda i: (0, i)))],
            {},
            steps=4,
        )[0]

    def tokens_back(self, c, middle_grad, line, factor, gain, tokens_grad):
        return call(
            tokens_back_kernel,
            "tokens_back",
            [
                (self.place, smem),
                (middle_grad, self.part(c, self.width)),
                (line[0], self.part(0, self.width)),
                (line[1], self.part(0, self.width)),
                (self.tokens, self.part(c, self.width)),
                (factor, self.part(c, 1)),
                (gain, self.gain_row),
            ],
            [
                ((self.total_rows, self.width), jnp.float32, self.part(c, self.width)),
                ((1, self.width), jnp.float32, self.gain_row),
            ],
            {0: tokens_grad},
            steps=self.rows // QUERY_ROWS,
        )

    def output(self, c, attn_sum, line, out):
        return call(
            output_kernel,
            "output",
            [
                (self.place, smem),
                (self.tokens, self.part(c, self.width)),
                (attn_sum, self.part(0, self.width)),
                (line[0], self.part(0, self.width)),
                (line[1], self.part(0, self.width)),
            ],
            [((self.total_rows, self.width), low_type, self.part(c, self.width))],
            {0: out},
            steps=self.rows // QUERY_ROWS,
        )[0]


def from_behind(block, axis, distance):
    devices = range(lax.axis_size(axis))
    route = [(i - distance, i) for i in devices if i - distance in devices]
    return lax.ppermute(block, axis, route)


def hold(values):
    return lax.optimization_barrier(values)


def add_low(left, right):
    return (left.astype(jnp.float32) + right.astype(jnp.float32)).astype(low_type)


class LineSums:
    def __init__(self, axis):
        self.axis = axis
        self.first = self.second = self.third = None
        self.results = {}

    def step(self, name, part, values, early=False):
        first, second, third = self.first, self.second, self.third
        own = None if first is None else first[1]
        half = None if second is None else second[1]
        part, own, half, values = hold((part, own, half, values))
        self.first = self.second = self.third = None
        new_half = new_total = done = None

        def send_part():
            if part is not None:
                self.first = (name, part, lax.ppermute(part, self.axis, [(0, 1), (3, 2)]))

        if early:
            send_part()
        if own is not None:
            new_half = add_low(own, first[2])
            across = lax.ppermute(new_half, self.axis, [(1, 2), (2, 1)])
        if half is not None:
            new_total = add_low(half, second[2])
            outward = lax.ppermute(new_total, self.axis, [(1, 0), (2, 3)])
        if early:
            new_half, new_total, values = hold((new_half, new_total, values))
        else:
            new_half, new_total, part, values = hold((new_half, new_total, part, values))
            send_part()
        if third is not None:
            done, values = hold((third[1:], values))
        if own is not None:
            self.second = (first[0], new_half, across)
        if half is not None:
            self.third = (second[0], new_total, outward)
        if third is not None:
            self.results[third[0]] = done
        return values


def small_sum_scatter(value, axis):
    size = lax.axis_size(axis)
    place = lax.axis_index(axis)
    bit = size // 2
    while bit >= 1:
        half = value.shape[1] // 2
        low, high = value[:, :half], value[:, half:]
        upper = (place & bit) != 0
        keep = jnp.where(upper, high, low)
        give = jnp.where(upper, low, high)
        value = keep + lax.ppermute(give, axis, [(i, i ^ bit) for i in range(size)])
        bit //= 2
    return value


def scattered(value):
    return lax.psum_scatter(value, "seq", scatter_dimension=0, tiled=True)


def body(
    tokens,
    group_ids,
    gain_attn,
    w_query,
    w_key,
    w_value,
    w_out,
    gain_mlp,
    w_gate,
    w_up,
    w_down,
    cotangent,
):
    head_width = w_query.shape[1]
    hidden = w_gate.shape[1]
    layer = Layer(tokens, cotangent, head_width, hidden)
    line = LineSums("mp")
    results = line.results
    total_rows = tokens.shape[0]

    attn_shard = jnp.concatenate([w_query, w_key, w_value, w_out.T], axis=1)
    attn_weight = lax.all_gather(attn_shard, "seq", axis=0, tiled=True)
    gains = lax.all_gather(jnp.stack([gain_attn, gain_mlp]), "seq", axis=1, tiled=True)
    gain_one = gains[:1].astype(jnp.float32)
    gain_two = gains[1:].astype(jnp.float32)
    ids_halo = from_behind(group_ids[-WINDOW:] + 1, "seq", 1) - 1
    ids_ext = jnp.concatenate([ids_halo, group_ids], axis=0)
    query_ids = group_ids[:, None]
    key_ids = jnp.stack(
        [
            ids_ext[None, start : start + QUERY_ROWS + WINDOW]
            for start in range(0, total_rows, QUERY_ROWS)
        ]
    )
    inputs = tokens.astype(jnp.float32)
    factor_one = row_scale(inputs)
    normed_attn = (inputs * factor_one * gain_one).astype(low_type)
    mlp_shard = mlp_layout(w_gate, w_up, w_down.T)
    mlp_shard, normed_attn, factor_one, query_ids, key_ids, gain_two, attn_weight = hold(
        (mlp_shard, normed_attn, factor_one, query_ids, key_ids, gain_two, attn_weight)
    )
    mlp_weight = lax.all_gather(mlp_shard, "seq", axis=0, tiled=True)

    half_rows = total_rows // 2
    qkv_weight = attn_weight[:, : 3 * head_width]
    halves = [times(normed_attn[:half_rows], qkv_weight).astype(low_type)]
    order = [1, 2, 0, 3]

    def pieces_of(c):
        return layer.qkv_operands(c, halves, halo, query_ids, key_ids)

    halo = None
    attended, term = layer.attend(order[0], pieces_of(order[0]), attn_weight, None)
    attended, later_rows, halves[0] = line.step(
        ("attn", order[0]), term, (attended, normed_attn[half_rows:], halves[0]), True
    )
    halves.append(times(later_rows, qkv_weight).astype(low_type))
    halo = from_behind(halves[1][-WINDOW:, head_width:], "seq", 1)
    for c in order[1:]:
        attended, term = layer.attend(c, pieces_of(c), attn_weight, attended)
        values = line.step(("attn", c), term, (attended, halves[0], halves[1], halo), True)
        attended, halves[0], halves[1], halo = values

    attn_sums, mlp_terms = {}, {}
    shared = (None, None, None)
    for c in order:
        attn_sums[c], *shared, term, mlp_terms[c] = layer.feed_forward(
            c, results["attn", c], gain_two, mlp_weight, shared
        )
        shared = line.step(("mlp", c), term, tuple(shared), True)
    normed_mlp, activations, mlp_grads = shared

    tokens_grad = out = None
    gain_one_parts, gain_two_parts = [], []

    def back(c, low_all, **more):
        made = layer.attend_back(
            c, attn_sums[c], results["mlp", c], gain_two, pieces_of(c), attn_weight, low_all, **more
        )
        gain_two_parts.append(made["gain_part"])
        return made

    def out_step(c, values, early=True):
        return line.step(("out", c), mlp_terms[c], values, early)

    gate_up_grad = inner_rows(normed_mlp, mlp_grads).astype(low_type)
    gate_up_grad, activations = out_step(order[0], (gate_up_grad, activations))
    gate_up_share = scattered(gate_up_grad)
    down_grad = inner_rows(cotangent, activations).astype(low_type)
    results["mlp", 1], down_grad = hold((results["mlp", 1], down_grad))
    made = back(1, None, keep=True, give_before=True)
    made, down_grad = out_step(order[1], (made, down_grad))
    down_share = scattered(down_grad)
    after_none = made["before"]
    made = back(2, made["low"], keep=True, earlier=(1, made["query_grad"], made["own"]))
    made, after_none = line.step(("attn_back", 1), made["term"], (made, after_none), True)
    kept = made["query_grad"], made["own"]
    made = back(0, made["low"], give_before=True, after=after_none, grads_all=made["grads"])
    made, kept = line.step(("attn_back", 0), made["term"], (made, kept), True)
    behind = from_behind(made["before"].astype(low_type), "seq", -1)
    made = back(3, made["low"], keep=True, earlier=(2, *kept), grads_all=made["grads"])
    made, behind = line.step(("attn_back", 2), made["term"], (made, behind), True)
    grads_all, term = layer.attn_term(
        3, made["query_grad"], made["own"], behind.astype(jnp.float32), attn_weight, made["grads"]
    )
    low_all = made["low"]
    attn_grad = layer.attn_weight_grads(normed_attn, grads_all, low_all, attended)
    attn_grad = line.step(("attn_back", 3), term, attn_grad, True)
    attn_share = scattered(attn_grad)

    def finish_tokens(c):
        nonlocal tokens_grad
        tokens_grad, part = layer.tokens_back(
            c, low_all, results["attn_back", c], factor_one, gain_one, tokens_grad
        )
        gain_one_parts.append(part)

    def finish_out(c):
        nonlocal out
        out = layer.output(c, attn_sums[c], results["out", c], out)

    finish_tokens(1)
    tokens_grad, gain_two_parts = out_step(order[2], (tokens_grad, gain_two_parts), True)
    finish_out(order[0])
    finish_tokens(0)
    tokens_grad, out = out_step(order[3], (tokens_grad, out), True)
    finish_tokens(2)
    finish_out(order[1])
    tokens_grad, out = line.step(None, None, (tokens_grad, out))
    finish_tokens(3)
    gain_parts = jnp.concatenate([sum(gain_one_parts), sum(gain_two_parts)], axis=0)
    gate_out = gate_up_share[:, :hidden].astype(jnp.float32)
    up_out = gate_up_share[:, hidden:].astype(jnp.float32)
    values = line.step(None, None, (tokens_grad, out, gain_parts, gate_out, up_out))
    tokens_grad, out, gain_parts, gate_out, up_out = values
    finish_out(order[2])
    down_out = down_share.astype(jnp.float32).T
    out, down_out, gain_parts = line.step(None, None, (out, down_out, gain_parts))
    gain_share = small_sum_scatter(gain_parts, "seq")
    finish_out(order[3])
    attn_out = attn_share.astype(jnp.float32)
    attn_outs = [attn_out[:, k * head_width : (k + 1) * head_width] for k in range(4)]
    attn_outs[3] = attn_outs[3].T
    return (
        out,
        tokens_grad,
        gain_share[0],
        attn_outs[0],
        attn_outs[1],
        attn_outs[2],
        attn_outs[3],
        gain_share[1],
        gate_out,
        up_out,
        down_out,
    )


def solution(mesh):
    placed = (
        P("seq", None),
        P("seq"),
        P("seq"),
        P("seq", "mp"),
        P("seq", "mp"),
        P("seq", "mp"),
        P("mp", "seq"),
        P("seq"),
        P("seq", "mp"),
        P("seq", "mp"),
        P("mp", "seq"),
        P("seq", None),
    )
    return jax.shard_map(
        body,
        mesh=mesh,
        in_specs=placed,
        out_specs=(
            P("seq", None),
            P("seq", None),
            P("seq"),
            P("seq", "mp"),
            P("seq", "mp"),
            P("seq", "mp"),
            P("mp", "seq"),
            P("seq"),
            P("seq", "mp"),
            P("seq", "mp"),
            P("mp", "seq"),
        ),
        check_vma=False,
    )
```

```python
import functools

import jax
import jax.numpy as jnp
from jax import lax
from jax.experimental import pallas as pl
from jax.experimental.pallas import tpu as pltpu
from jax.sharding import PartitionSpec as P

HEAD_DIM = 128
WINDOW = 64
CHUNKS = 4
QUERY_ROWS = 128
WIDE = 256

epsilon = 1e-05
masked_score = -1e30
score_scale = HEAD_DIM ** (-0.5)
MEGA = 1024 * 1024
GRANTS = {'attend': 40, 'feed_forward': 40, 'attend_back': 56, 'attn_term': 40, 'attn_weight_grads': 40, 'tokens_back': 56, 'output': 56}
low_type = jnp.bfloat16


def times(left, right):
    return jnp.dot(left, right, preferred_element_type=jnp.float32)


def times_transposed(left, right):
    return lax.dot_general(
        left, right, (((1,), (1,)), ((), ())), preferred_element_type=jnp.float32
    )


def inner_rows(left, right):
    return lax.dot_general(
        left, right, (((0,), (0,)), ((), ())), preferred_element_type=jnp.float32
    )


def row_scale(value_in):
    return lax.rsqrt(jnp.mean(value_in * value_in, axis=-1, keepdims=True) + epsilon)


def norm_backward(grad_normed, normed_unit, row_factor, gain_full):
    scaled_grad = grad_normed * gain_full
    return row_factor * (
        scaled_grad - normed_unit * jnp.mean(scaled_grad * normed_unit, axis=-1, keepdims=True)
    )


def line_result(place_ref, total_ref, outward_ref):
    place = place_ref[0]
    in_middle = (place == 1) | (place == 2)
    return jnp.where(in_middle, total_ref[...], outward_ref[...])


def allowed_pairs(query_ids, key_ids):
    shape = (query_ids.shape[0], key_ids.shape[1])
    query_pos = lax.broadcasted_iota(jnp.int32, shape, 0)
    key_pos = lax.broadcasted_iota(jnp.int32, shape, 1)
    inside = (key_pos >= query_pos) & (key_pos <= query_pos + WINDOW)
    return inside & (query_ids == key_ids) & (query_ids >= 0)


def probabilities(query, key, allowed, valid):
    scores = jnp.where(allowed, times_transposed(query, key) * score_scale, masked_score)
    top_score = jnp.max(scores, axis=-1, keepdims=True)
    weights = jnp.where(allowed, jnp.exp(scores - top_score), 0.0)
    totals = jnp.where(valid, jnp.sum(weights, axis=-1, keepdims=True), 1.0)
    return weights / totals


def keys_of(step, first_refs, before_refs, refs, columns):
    out = []
    for first_ref, before_ref, ref in zip(first_refs, before_refs, refs):
        before = before_ref[:, columns]
        if first_ref is not None:
            before = jnp.where(step == 0, first_ref[:, columns], before)
        out.append(jnp.concatenate([before, ref[:, columns]], axis=0))
    return out


def split_refs(first, refs):
    q_ref, k_ref, v_ref, k_before, v_before = refs[:5]
    firsts = refs[5:7] if first else (None, None)
    refs = refs[7 if first else 5 :]
    return (q_ref, (k_ref, v_ref), (k_before, v_before), firsts), refs[:2], refs[2:]


def attend_kernel(first, *refs):
    (q_ref, own, before, firsts), (query_ids_ref, key_ids_ref), rest = split_refs(first, refs)
    out_weight_ref = rest[0]
    attended_ref, term_ref = rest[-2:]
    step = pl.program_id(0)
    query_ids = query_ids_ref[...]
    allowed = allowed_pairs(query_ids, key_ids_ref[0])
    valid = query_ids >= 0
    for head in range(q_ref.shape[1] // HEAD_DIM):
        columns = slice(head * HEAD_DIM, (head + 1) * HEAD_DIM)
        key, value = keys_of(step, firsts, before, own, columns)
        probs = probabilities(q_ref[:, columns], key, allowed, valid)
        attended_ref[:, columns] = times(probs.astype(low_type), value).astype(low_type)
    term_ref[...] = times_transposed(attended_ref[...], out_weight_ref[...]).astype(low_type)


def attend_back_kernel(
    first, names, counts, place_ref, tokens_ref, attn_sum_ref, total_ref, outward_ref, cotangent_ref,
    gain_ref, *refs,
):
    (q_ref, own, before, firsts), (query_ids_ref, key_ids_ref), rest = split_refs(first, refs)
    out_weight_ref = rest[0]
    inputs = dict(zip(names[0], rest[1 : 1 + counts[0]]))
    outputs = dict(zip(names[1], rest[1 + counts[0] + counts[1] :]))
    scratch = rest[1 + counts[0] + counts[1] + len(names[1]) :]
    spread, query_grads = scratch[:2]
    step = pl.program_id(0)
    last = pl.num_programs(0) - 1
    rows, width = q_ref.shape
    if "weight" in inputs:
        held, arrived = scratch[2:]
        fetch = pltpu.make_async_copy(
            inputs["weight"].at[:, : held.shape[1]], held, arrived
        )

        @pl.when(step == 0)
        def _():
            fetch.start()

    middle = tokens_ref[...].astype(jnp.float32) + attn_sum_ref[...].astype(jnp.float32)
    factor = row_scale(middle)
    unit = middle * factor
    grad_sum = line_result(place_ref, total_ref, outward_ref).astype(jnp.float32)
    gain_part = jnp.sum(grad_sum * unit, axis=0, keepdims=True)
    middle_grad = cotangent_ref[...].astype(jnp.float32) + norm_backward(
        grad_sum, unit, factor, gain_ref[...]
    )
    low = middle_grad.astype(low_type)
    outputs["low"][...] = low
    attended_grad = times(low, out_weight_ref[...]).astype(low_type)

    @pl.when(step == 0)
    def _():
        outputs["gain_part"][...] = gain_part
        spread[...] = jnp.zeros_like(spread)

    @pl.when(step > 0)
    def _():
        outputs["gain_part"][...] += gain_part

    query_ids = query_ids_ref[...]
    allowed = allowed_pairs(query_ids, key_ids_ref[0])
    valid = query_ids >= 0
    part = pl.ds(pl.multiple_of(step * rows, rows), rows)
    span = pl.ds(pl.multiple_of(step * rows, rows), rows + WINDOW)
    for head in range(width // HEAD_DIM):
        columns = slice(head * HEAD_DIM, (head + 1) * HEAD_DIM)
        value_columns = slice(width + head * HEAD_DIM, width + (head + 1) * HEAD_DIM)
        query = q_ref[:, columns]
        key, value = keys_of(step, firsts, before, own, columns)
        out_grad = attended_grad[:, columns]
        probs = probabilities(query, key, allowed, valid)
        prob_grad = times_transposed(out_grad, value)
        centre = jnp.sum(prob_grad * probs, axis=-1, keepdims=True)
        score_grad = (probs * (prob_grad - centre)).astype(low_type)
        query_grads[part, columns] = (times(score_grad, key) * score_scale).astype(low_type)
        spread[span, columns] += inner_rows(score_grad, query) * score_scale
        spread[span, value_columns] += inner_rows(probs.astype(low_type), out_grad)

    @pl.when(step == last)
    def _():
        if "own" in outputs:
            outputs["query_grad"][...] = query_grads[...]
            outputs["own"][...] = spread[WINDOW:, :].astype(low_type)
        if "before" in outputs:
            outputs["before"][...] = spread[:WINDOW, :]
        if "weight" not in inputs:
            return
        grads_ref = outputs["grads"]
        kept = grads_ref.shape[0] - WINDOW
        if "own" in inputs:
            grads_ref[:, :width] = inputs["query_grad"][...]
            grads_ref[:kept, width:] = inputs["own"][:kept, :]
            tail, after = inputs["own"][kept:, :].astype(jnp.float32), spread[:WINDOW, :]
        else:
            grads_ref[:, :width] = query_grads[...]
            grads_ref[:kept, width:] = spread[WINDOW : WINDOW + kept, :].astype(low_type)
            tail, after = spread[WINDOW + kept :, :], inputs["after"][...]
        grads_ref[kept:, width:] = (tail + after).astype(low_type)
        fetch.wait()
        outputs["term"][...] = times_transposed(grads_ref[...], held[...]).astype(low_type)


def attn_term_kernel(query_grad_ref, own_ref, after_ref, weight_ref, *rest):
    grads_ref, term_ref = rest[-2:]
    rows, width = query_grad_ref.shape

    @pl.when(pl.program_id(0) == 0)
    def _():
        kept = rows - WINDOW
        grads_ref[:, :width] = query_grad_ref[...]
        grads_ref[:kept, width:] = own_ref[:kept, :]
        grads_ref[kept:, width:] = (
            own_ref[kept:, :].astype(jnp.float32) + after_ref[...]
        ).astype(low_type)

    term_ref[...] = times_transposed(grads_ref[...], weight_ref[...]).astype(low_type)


def attn_weight_grads_kernel(normed_ref, low_ref, grads_ref, attended_ref, result_ref):
    step = pl.program_id(0)

    @pl.when(step < 3)
    def _():
        result_ref[...] = inner_rows(normed_ref[...], grads_ref[...]).astype(low_type)

    @pl.when(step == 3)
    def _():
        result_ref[...] = inner_rows(low_ref[...], attended_ref[...]).astype(low_type)


def tokens_back_kernel(
    place_ref, middle_grad_ref, total_ref, outward_ref, tokens_ref, factor_ref, gain_ref, *rest
):
    tokens_grad_ref, gain_part_ref = rest[-2:]
    factor = factor_ref[...]
    unit = tokens_ref[...].astype(jnp.float32) * factor
    grad_sum = line_result(place_ref, total_ref, outward_ref).astype(jnp.float32)
    tokens_grad_ref[...] = middle_grad_ref[...].astype(jnp.float32) + norm_backward(
        grad_sum, unit, factor, gain_ref[...]
    )
    gain_part = jnp.sum(grad_sum * unit, axis=0, keepdims=True)

    @pl.when(pl.program_id(0) == 0)
    def _():
        gain_part_ref[...] = gain_part

    @pl.when(pl.program_id(0) > 0)
    def _():
        gain_part_ref[...] += gain_part


def output_kernel(place_ref, tokens_ref, attn_sum_ref, total_ref, outward_ref, *rest):
    middle = tokens_ref[...].astype(jnp.float32) + attn_sum_ref[...].astype(jnp.float32)
    mlp_sum = line_result(place_ref, total_ref, outward_ref).astype(jnp.float32)
    rest[-1][...] = (middle + mlp_sum).astype(low_type)


def mlp_pieces(hidden):
    whole = hidden // WIDE * WIDE
    pieces = []
    for start in range(0, whole, WIDE):
        for k in range(3):
            pieces.append(slice(k * whole + start, k * whole + start + WIDE))
    pieces.append(slice(3 * whole, 3 * hidden))
    return whole, pieces


def mlp_layout(gate, up, down):
    whole = gate.shape[1] // WIDE * WIDE
    return jnp.concatenate(
        [m[:, :whole] for m in (gate, up, down)] + [m[:, whole:] for m in (gate, up, down)], axis=1
    )


def mlp_kernel(
    first_row, place_ref, tokens_ref, total_ref, outward_ref, cotangent_ref, gain_ref, weight_ref, *rest
):
    leaving = rest[-19:-13]
    (
        tokens, attn_sum, cotangent, normed_ref, activation_ref, grads_ref, term_ref, mlp_ref,
        term_part, mlp_part, held, arrived, left,
    ) = rest[-13:]
    rows, hidden = activation_ref.shape
    whole, pieces = mlp_pieces(hidden)
    half = hidden - whole
    tail = 3 * whole
    mine = pl.ds(first_row, rows)
    place = place_ref[0]
    in_middle = (place == 1) | (place == 2)

    fetch_tokens = pltpu.make_async_copy(tokens_ref.at[mine], tokens, arrived.at[0])
    fetch_total = pltpu.make_async_copy(total_ref, attn_sum, arrived.at[1])
    fetch_outward = pltpu.make_async_copy(outward_ref, attn_sum, arrived.at[1])
    fetch_cotangent = pltpu.make_async_copy(cotangent_ref.at[mine], cotangent, arrived.at[2])
    fetch_tokens.start()
    pl.when(in_middle)(fetch_total.start)
    pl.when(jnp.logical_not(in_middle))(fetch_outward.start)
    fetch_cotangent.start()
    copies = [
        pltpu.make_async_copy(weight_ref.at[:, piece], held.at[:, piece], arrived.at[3 + i])
        for i, piece in enumerate(pieces)
    ]
    for copy in copies:
        copy.start()
    sources = (attn_sum, normed_ref, activation_ref, grads_ref, term_ref, mlp_ref)
    out_copies = [
        pltpu.make_async_copy(
            source, target.at[mine] if i in (1, 2, 3) else target, left.at[i]
        )
        for i, (source, target) in enumerate(zip(sources, leaving))
    ]

    fetch_tokens.wait()
    fetch_total.wait()
    middle = tokens[...].astype(jnp.float32) + attn_sum[...].astype(jnp.float32)
    normed_ref[...] = (middle * row_scale(middle) * gain_ref[...]).astype(low_type)
    fetch_cotangent.wait()
    normed = normed_ref[...]
    cot = cotangent[...]

    def inner(start, stop, gate, up, act_grad):
        sigmoid_gate = jax.nn.sigmoid(gate)
        silu_gate = gate * sigmoid_gate
        activation_ref[:, start:stop] = (silu_gate * up).astype(low_type)
        grads_ref[:, start:stop] = (
            act_grad * up * (sigmoid_gate + silu_gate * (1.0 - sigmoid_gate))
        ).astype(low_type)
        grads_ref[:, hidden + start : hidden + stop] = (act_grad * silu_gate).astype(low_type)

    def whole_piece(j):
        for copy in copies[3 * j : 3 * j + 3]:
            copy.wait()
        gate, up, down = (held[:, piece] for piece in pieces[3 * j : 3 * j + 3])
        inner(j * WIDE, (j + 1) * WIDE, times(normed, gate), times(normed, up), times(cot, down))

    def back(rows, start, stop):
        term = times_transposed(grads_ref[:, start:stop], held[rows, start:stop])
        term += times_transposed(
            grads_ref[:, hidden + start : hidden + stop], held[rows, whole + start : whole + stop]
        )
        down = held[rows, 2 * whole + start : 2 * whole + stop]
        return term, times_transposed(activation_ref[:, start:stop], down)

    blocks = [slice(start, start + 2 * WIDE) for start in range(0, held.shape[0], 2 * WIDE)]
    early = whole // WIDE // 2 + 1
    for j in range(early):
        whole_piece(j)
    for rows in blocks:
        term_part[:, rows], mlp_part[:, rows] = back(rows, 0, early * WIDE)
    for j in range(early, whole // WIDE):
        whole_piece(j)
    copies[-1].wait()
    both = times(normed, held[:, tail : tail + 2 * half])
    inner(
        whole, hidden, both[:, :half], both[:, half:], times(cot, held[:, tail + 2 * half :])
    )
    for copy in out_copies[:4]:
        copy.start()

    pair = jnp.concatenate([grads_ref[:, whole:hidden], grads_ref[:, hidden + whole :]], axis=1)
    for rows in blocks:
        term, mlp = back(rows, early * WIDE, whole)
        term += times_transposed(pair, held[rows, tail : tail + 2 * half]) + term_part[:, rows]
        mlp += times_transposed(activation_ref[:, whole:], held[rows, tail + 2 * half :])
        term_ref[:, rows] = term.astype(low_type)
        mlp_ref[:, rows] = (mlp + mlp_part[:, rows]).astype(low_type)
    for copy in out_copies[4:]:
        copy.start()
    for copy in out_copies:
        copy.wait()


def block_of(shape, *place):
    return pl.BlockSpec(shape, lambda i: place)


smem = pl.BlockSpec(memory_space=pltpu.SMEM)
anywhere = pl.BlockSpec(memory_space=pl.ANY)


def call(kernel, name, operands, results, shared, steps=1, scratch=()):
    arrays = [array for array, _ in operands]
    specs = [spec for _, spec in operands]
    aliases = {}
    for index, kept in shared.items():
        if kept is not None:
            aliases[len(arrays)] = index
            arrays.append(kept)
            specs.append(anywhere)
    return pl.pallas_call(
        kernel,
        grid=(steps,),
        in_specs=specs,
        out_specs=[spec for _, _, spec in results],
        out_shape=[jax.ShapeDtypeStruct(shape, dtype) for shape, dtype, _ in results],
        input_output_aliases=aliases,
        scratch_shapes=list(scratch),
        compiler_params=pltpu.CompilerParams(
            dimension_semantics=("arbitrary",), vmem_limit_bytes=GRANTS[name] * MEGA
        ),
        cost_estimate=pl.CostEstimate(flops=1, bytes_accessed=1, transcendentals=0),
        name=name,
    )(*arrays)


class Layer:
    def __init__(self, tokens, cotangent, head_width, hidden):
        self.tokens, self.cotangent = tokens, cotangent
        self.total_rows, self.width = tokens.shape
        self.rows = self.total_rows // CHUNKS
        self.head_width, self.hidden = head_width, hidden
        self.place = lax.axis_index("mp").astype(jnp.int32).reshape(1)
        self.whole = block_of((self.rows, self.width), 0, 0)
        self.gain_row = block_of((1, self.width), 0, 0)

    def chunk(self, c, columns=None):
        return block_of((self.rows, columns or self.width), c, 0)

    def qkv_operands(self, c, halves, halo, query_ids, key_ids):
        head_width = self.head_width
        half_rows = halves[0].shape[0]
        half, first_row = divmod(c * self.rows, half_rows)
        first_part, first_window = first_row // QUERY_ROWS, first_row // WINDOW
        stride = QUERY_ROWS // WINDOW

        def part(k):
            return pl.BlockSpec((QUERY_ROWS, head_width), lambda i: (first_part + i, k))

        def before(k):
            return pl.BlockSpec(
                (WINDOW, head_width),
                lambda i: (jnp.maximum(first_window + stride * i - 1, 0), k),
            )

        source = halves[half]
        operands = [(source, part(k)) for k in range(3)]
        operands += [(source, before(k)) for k in (1, 2)]
        if c == 0:
            operands += [(halo, block_of((WINDOW, head_width), 0, k)) for k in range(2)]
        elif first_row == 0:
            last = half_rows // WINDOW - 1
            operands += [
                (halves[half - 1], block_of((WINDOW, head_width), last, k)) for k in (1, 2)
            ]
        parts = self.rows // QUERY_ROWS
        ids = [
            (query_ids, pl.BlockSpec((QUERY_ROWS, 1), lambda i: (c * parts + i, 0))),
            (
                key_ids,
                pl.BlockSpec((1, 1, QUERY_ROWS + WINDOW), lambda i: (c * parts + i, 0, 0)),
            ),
        ]
        return first_row == 0, operands + ids

    def part(self, c, columns):
        parts = self.rows // QUERY_ROWS
        return pl.BlockSpec((QUERY_ROWS, columns), lambda i: (c * parts + i, 0))

    def attend(self, c, first_and_qkv, attn_weight, attended):
        first, qkv_operands = first_and_qkv
        return call(
            functools.partial(attend_kernel, first),
            "attend",
            qkv_operands + [(attn_weight, block_of((self.width, self.head_width), 0, 3))],
            [
                ((self.total_rows, self.head_width), low_type, self.part(c, self.head_width)),
                ((self.rows, self.width), low_type, self.part(0, self.width)),
            ],
            {0: attended},
            steps=self.rows // QUERY_ROWS,
        )

    def feed_forward(self, c, line, gain, weight, shared):
        rows, width, hidden = self.rows, self.width, self.hidden
        block = pltpu.VMEM((rows, width), low_type)
        return call(
            functools.partial(mlp_kernel, c * rows),
            "feed_forward",
            [
                (self.place, smem),
                (self.tokens, anywhere),
                (line[0], anywhere),
                (line[1], anywhere),
                (self.cotangent, anywhere),
                (gain, self.gain_row),
                (weight, anywhere),
            ],
            [
                ((rows, width), low_type, anywhere),
                ((self.total_rows, width), low_type, anywhere),
                ((self.total_rows, hidden), low_type, anywhere),
                ((self.total_rows, 2 * hidden), low_type, anywhere),
                ((rows, width), low_type, anywhere),
                ((rows, width), low_type, anywhere),
            ],
            {index + 1: kept for index, kept in enumerate(shared)},
            scratch=[block, block, block, block]
            + [
                pltpu.VMEM((rows, hidden), low_type),
                pltpu.VMEM((rows, 2 * hidden), low_type),
                block,
                block,
                pltpu.VMEM((rows, width), jnp.float32),
                pltpu.VMEM((rows, width), jnp.float32),
                pltpu.VMEM((width, 3 * hidden), low_type),
                pltpu.SemaphoreType.DMA((3 + len(mlp_pieces(hidden)[1]),)),
                pltpu.SemaphoreType.DMA((6,)),
            ],
        )

    def attend_back(
        self, c, attn_sum, line, gain, first_and_qkv, attn_weight, low_all,
        keep=False, give_before=False, earlier=None, after=None, grads_all=None,
    ):
        first, qkv_operands = first_and_qkv
        rows, width, head_width = self.rows, self.width, self.head_width
        mine, alone = self.part(c, width), self.part(0, width)
        query_spec = block_of((rows, head_width), 0, 0)
        own_spec = block_of((rows, 2 * head_width), 0, 0)
        window_spec = block_of((WINDOW, 2 * head_width), 0, 0)
        more, results = {}, {
            "low": ((self.total_rows, width), low_type, mine),
            "gain_part": ((1, width), jnp.float32, self.gain_row),
        }
        shared = {0: low_all}
        scratch = [
            pltpu.VMEM((rows + WINDOW, 2 * head_width), jnp.float32),
            pltpu.VMEM((rows, head_width), low_type),
        ]
        if keep:
            results["query_grad"] = ((rows, head_width), low_type, query_spec)
            results["own"] = ((rows, 2 * head_width), low_type, own_spec)
        if give_before:
            results["before"] = ((WINDOW, 2 * head_width), jnp.float32, window_spec)
        term_chunk = None
        if earlier is not None:
            term_chunk = earlier[0]
            more["query_grad"], more["own"] = (earlier[1], query_spec), (earlier[2], own_spec)
        elif after is not None:
            term_chunk = c
            more["after"] = (after, window_spec)
        if term_chunk is not None:
            more["weight"] = (attn_weight, anywhere)
            shared[len(results)] = grads_all
            results["grads"] = (
                (self.total_rows, 3 * head_width),
                low_type,
                block_of((rows, 3 * head_width), term_chunk, 0),
            )
            results["term"] = ((rows, width), low_type, self.whole)
            scratch += [pltpu.VMEM((width, 3 * head_width), low_type), pltpu.SemaphoreType.DMA]
        kept = sum(array is not None for array in shared.values())
        outputs = call(
            functools.partial(
                attend_back_kernel, first, (tuple(more), tuple(results)), (len(more), kept)
            ),
            "attend_back",
            [
                (self.place, smem),
                (self.tokens, mine),
                (attn_sum, alone),
                (line[0], alone),
                (line[1], alone),
                (self.cotangent, mine),
                (gain, self.gain_row),
            ]
            + qkv_operands
            + [(attn_weight, block_of((width, head_width), 0, 3))]
            + list(more.values()),
            list(results.values()),
            shared,
            steps=rows // QUERY_ROWS,
            scratch=scratch,
        )
        return dict(zip(results, outputs))

    def attn_term(self, c, query_grad, own, after, attn_weight, grads_all):
        rows, width, head_width = self.rows, self.width, self.head_width
        part = width // CHUNKS
        return call(
            attn_term_kernel,
            "attn_term",
            [
                (query_grad, block_of((rows, head_width), 0, 0)),
                (own, block_of((rows, 2 * head_width), 0, 0)),
                (after, block_of((WINDOW, 2 * head_width), 0, 0)),
                (attn_weight, pl.BlockSpec((part, 3 * head_width), lambda i: (i, 0))),
            ],
            [
                ((self.total_rows, 3 * head_width), low_type, self.chunk(c, 3 * head_width)),
                ((rows, width), low_type, pl.BlockSpec((rows, part), lambda i: (0, i))),
            ],
            {0: grads_all},
            steps=width // part,
        )

    def attn_weight_grads(self, normed_attn, grads_all, low_all, attended):
        rows, width, head_width = self.total_rows, self.width, self.head_width
        return call(
            attn_weight_grads_kernel,
            "attn_weight_grads",
            [
                (normed_attn, block_of((rows, width), 0, 0)),
                (low_all, block_of((rows, width), 0, 0)),
                (grads_all, pl.BlockSpec((rows, head_width), lambda i: (0, jnp.minimum(i, 2)))),
                (attended, block_of((rows, head_width), 0, 0)),
            ],
            [((width, 4 * head_width), low_type, pl.BlockSpec((width, head_width), lambda i: (0, i)))],
            {},
            steps=4,
        )[0]

    def tokens_back(self, c, middle_grad, line, factor, gain, tokens_grad):
        return call(
            tokens_back_kernel,
            "tokens_back",
            [
                (self.place, smem),
                (middle_grad, self.part(c, self.width)),
                (line[0], self.part(0, self.width)),
                (line[1], self.part(0, self.width)),
                (self.tokens, self.part(c, self.width)),
                (factor, self.part(c, 1)),
                (gain, self.gain_row),
            ],
            [
                ((self.total_rows, self.width), jnp.float32, self.part(c, self.width)),
                ((1, self.width), jnp.float32, self.gain_row),
            ],
            {0: tokens_grad},
            steps=self.rows // QUERY_ROWS,
        )

    def output(self, c, attn_sum, line, out):
        return call(
            output_kernel,
            "output",
            [
                (self.place, smem),
                (self.tokens, self.part(c, self.width)),
                (attn_sum, self.part(0, self.width)),
                (line[0], self.part(0, self.width)),
                (line[1], self.part(0, self.width)),
            ],
            [((self.total_rows, self.width), low_type, self.part(c, self.width))],
            {0: out},
            steps=self.rows // QUERY_ROWS,
        )[0]


def from_behind(block, axis, distance):
    devices = range(lax.axis_size(axis))
    route = [(i - distance, i) for i in devices if i - distance in devices]
    return lax.ppermute(block, axis, route)


def hold(values):
    return lax.optimization_barrier(values)


def add_low(left, right):
    return (left.astype(jnp.float32) + right.astype(jnp.float32)).astype(low_type)


class LineSums:
    def __init__(self, axis):
        self.axis = axis
        self.first = self.second = self.third = None
        self.results = {}

    def step(self, name, part, values, early=False):
        first, second, third = self.first, self.second, self.third
        own = None if first is None else first[1]
        half = None if second is None else second[1]
        part, own, half, values = hold((part, own, half, values))
        self.first = self.second = self.third = None
        new_half = new_total = done = None

        def send_part():
            if part is not None:
                self.first = (name, part, lax.ppermute(part, self.axis, [(0, 1), (3, 2)]))

        if early:
            send_part()
        if own is not None:
            new_half = add_low(own, first[2])
            across = lax.ppermute(new_half, self.axis, [(1, 2), (2, 1)])
        if half is not None:
            new_total = add_low(half, second[2])
            outward = lax.ppermute(new_total, self.axis, [(1, 0), (2, 3)])
        if early:
            new_half, new_total, values = hold((new_half, new_total, values))
        else:
            new_half, new_total, part, values = hold((new_half, new_total, part, values))
            send_part()
        if third is not None:
            done, values = hold((third[1:], values))
        if own is not None:
            self.second = (first[0], new_half, across)
        if half is not None:
            self.third = (second[0], new_total, outward)
        if third is not None:
            self.results[third[0]] = done
        return values


def small_sum_scatter(value, axis):
    size = lax.axis_size(axis)
    place = lax.axis_index(axis)
    bit = size // 2
    while bit >= 1:
        half = value.shape[1] // 2
        low, high = value[:, :half], value[:, half:]
        upper = (place & bit) != 0
        keep = jnp.where(upper, high, low)
        give = jnp.where(upper, low, high)
        value = keep + lax.ppermute(give, axis, [(i, i ^ bit) for i in range(size)])
        bit //= 2
    return value


def scattered(value):
    return lax.psum_scatter(value, "seq", scatter_dimension=0, tiled=True)


def body(
    tokens,
    group_ids,
    gain_attn,
    w_query,
    w_key,
    w_value,
    w_out,
    gain_mlp,
    w_gate,
    w_up,
    w_down,
    cotangent,
):
    head_width = w_query.shape[1]
    hidden = w_gate.shape[1]
    layer = Layer(tokens, cotangent, head_width, hidden)
    line = LineSums("mp")
    results = line.results
    total_rows = tokens.shape[0]

    attn_shard = jnp.concatenate([w_query, w_key, w_value, w_out.T], axis=1)
    attn_weight = lax.all_gather(attn_shard, "seq", axis=0, tiled=True)
    gains = lax.all_gather(jnp.stack([gain_attn, gain_mlp]), "seq", axis=1, tiled=True)
    gain_one = gains[:1].astype(jnp.float32)
    gain_two = gains[1:].astype(jnp.float32)
    ids_halo = from_behind(group_ids[-WINDOW:] + 1, "seq", 1) - 1
    ids_ext = jnp.concatenate([ids_halo, group_ids], axis=0)
    query_ids = group_ids[:, None]
    key_ids = jnp.stack(
        [
            ids_ext[None, start : start + QUERY_ROWS + WINDOW]
            for start in range(0, total_rows, QUERY_ROWS)
        ]
    )
    inputs = tokens.astype(jnp.float32)
    factor_one = row_scale(inputs)
    normed_attn = (inputs * factor_one * gain_one).astype(low_type)
    mlp_shard = mlp_layout(w_gate, w_up, w_down.T)
    mlp_shard, normed_attn, factor_one, query_ids, key_ids, gain_two, attn_weight = hold(
        (mlp_shard, normed_attn, factor_one, query_ids, key_ids, gain_two, attn_weight)
    )
    mlp_weight = lax.all_gather(mlp_shard, "seq", axis=0, tiled=True)

    half_rows = total_rows // 2
    qkv_weight = attn_weight[:, : 3 * head_width]
    halves = [times(normed_attn[:half_rows], qkv_weight).astype(low_type)]
    order = [1, 2, 0, 3]

    def pieces_of(c):
        return layer.qkv_operands(c, halves, halo, query_ids, key_ids)

    halo = None
    attended, term = layer.attend(order[0], pieces_of(order[0]), attn_weight, None)
    attended, later_rows, halves[0] = line.step(
        ("attn", order[0]), term, (attended, normed_attn[half_rows:], halves[0]), True
    )
    halves.append(times(later_rows, qkv_weight).astype(low_type))
    halo = from_behind(halves[1][-WINDOW:, head_width:], "seq", 1)
    for c in order[1:]:
        attended, term = layer.attend(c, pieces_of(c), attn_weight, attended)
        values = line.step(("attn", c), term, (attended, halves[0], halves[1], halo), True)
        attended, halves[0], halves[1], halo = values

    attn_sums, mlp_terms = {}, {}
    shared = (None, None, None)
    for c in order:
        attn_sums[c], *shared, term, mlp_terms[c] = layer.feed_forward(
            c, results["attn", c], gain_two, mlp_weight, shared
        )
        shared = line.step(("mlp", c), term, tuple(shared), True)
    normed_mlp, activations, mlp_grads = shared

    tokens_grad = out = None
    gain_one_parts, gain_two_parts = [], []

    def back(c, low_all, **more):
        made = layer.attend_back(
            c, attn_sums[c], results["mlp", c], gain_two, pieces_of(c), attn_weight, low_all, **more
        )
        gain_two_parts.append(made["gain_part"])
        return made

    def out_step(c, values, early=True):
        return line.step(("out", c), mlp_terms[c], values, early)

    gate_up_grad = inner_rows(normed_mlp, mlp_grads).astype(low_type)
    gate_up_grad, activations = out_step(order[0], (gate_up_grad, activations))
    gate_up_share = scattered(gate_up_grad)
    down_grad = inner_rows(cotangent, activations).astype(low_type)
    results["mlp", 1], down_grad = hold((results["mlp", 1], down_grad))
    made = back(1, None, keep=True, give_before=True)
    made, down_grad = out_step(order[1], (made, down_grad))
    down_share = scattered(down_grad)
    after_none = made["before"]
    made = back(2, made["low"], keep=True, earlier=(1, made["query_grad"], made["own"]))
    made, after_none = line.step(("attn_back", 1), made["term"], (made, after_none), True)
    kept = made["query_grad"], made["own"]
    made = back(0, made["low"], give_before=True, after=after_none, grads_all=made["grads"])
    made, kept = line.step(("attn_back", 0), made["term"], (made, kept), True)
    behind = from_behind(made["before"].astype(low_type), "seq", -1)
    made = back(3, made["low"], keep=True, earlier=(2, *kept), grads_all=made["grads"])
    made, behind = line.step(("attn_back", 2), made["term"], (made, behind), True)
    grads_all, term = layer.attn_term(
        3, made["query_grad"], made["own"], behind.astype(jnp.float32), attn_weight, made["grads"]
    )
    low_all = made["low"]
    attn_grad = layer.attn_weight_grads(normed_attn, grads_all, low_all, attended)
    attn_grad = line.step(("attn_back", 3), term, attn_grad, True)
    attn_share = scattered(attn_grad)

    def finish_tokens(c):
        nonlocal tokens_grad
        tokens_grad, part = layer.tokens_back(
            c, low_all, results["attn_back", c], factor_one, gain_one, tokens_grad
        )
        gain_one_parts.append(part)

    def finish_out(c):
        nonlocal out
        out = layer.output(c, attn_sums[c], results["out", c], out)

    finish_tokens(1)
    tokens_grad, gain_two_parts = out_step(order[2], (tokens_grad, gain_two_parts), True)
    finish_out(order[0])
    finish_tokens(0)
    tokens_grad, out = out_step(order[3], (tokens_grad, out), True)
    finish_tokens(2)
    finish_out(order[1])
    tokens_grad, out = line.step(None, None, (tokens_grad, out))
    finish_tokens(3)
    gain_parts = jnp.concatenate([sum(gain_one_parts), sum(gain_two_parts)], axis=0)
    gate_out = gate_up_share[:, :hidden].astype(jnp.float32)
    up_out = gate_up_share[:, hidden:].astype(jnp.float32)
    values = line.step(None, None, (tokens_grad, out, gain_parts, gate_out, up_out))
    tokens_grad, out, gain_parts, gate_out, up_out = values
    finish_out(order[2])
    down_out = down_share.astype(jnp.float32).T
    attn_out = attn_share.astype(jnp.float32)
    attn_outs = [attn_out[:, k * head_width : (k + 1) * head_width] for k in range(4)]
    attn_outs[3] = attn_outs[3].T
    out, down_out, gain_parts, attn_outs = line.step(
        None, None, (out, down_out, gain_parts, attn_outs)
    )
    gain_share = small_sum_scatter(gain_parts, "seq")
    finish_out(order[3])
    return (
        out,
        tokens_grad,
        gain_share[0],
        attn_outs[0],
        attn_outs[1],
        attn_outs[2],
        attn_outs[3],
        gain_share[1],
        gate_out,
        up_out,
        down_out,
    )


def solution(mesh):
    placed = (
        P("seq", None),
        P("seq"),
        P("seq"),
        P("seq", "mp"),
        P("seq", "mp"),
        P("seq", "mp"),
        P("mp", "seq"),
        P("seq"),
        P("seq", "mp"),
        P("seq", "mp"),
        P("mp", "seq"),
        P("seq", None),
    )
    return jax.shard_map(
        body,
        mesh=mesh,
        in_specs=placed,
        out_specs=(
            P("seq", None),
            P("seq", None),
            P("seq"),
            P("seq", "mp"),
            P("seq", "mp"),
            P("seq", "mp"),
            P("mp", "seq"),
            P("seq"),
            P("seq", "mp"),
            P("seq", "mp"),
            P("mp", "seq"),
        ),
        check_vma=False,
    )
```

```python
import functools

import jax
import jax.numpy as jnp
from jax import lax
from jax.experimental import pallas as pl
from jax.experimental.pallas import tpu as pltpu
from jax.sharding import PartitionSpec as P

HEAD_DIM = 128
WINDOW = 64
CHUNKS = 4
QUERY_ROWS = 128
WIDE = 256

epsilon = 1e-05
masked_score = -1e30
score_scale = HEAD_DIM ** (-0.5)
MEGA = 1024 * 1024
GRANTS = {'middle_add': 8, 'attend': 40, 'feed_forward': 44, 'attend_back': 56, 'attn_term': 40, 'attn_weight_grads': 40, 'tokens_back': 56, 'output': 56}
low_type = jnp.bfloat16


def times(left, right):
    return jnp.dot(left, right, preferred_element_type=jnp.float32)


def times_transposed(left, right):
    return lax.dot_general(
        left, right, (((1,), (1,)), ((), ())), preferred_element_type=jnp.float32
    )


def inner_rows(left, right):
    return lax.dot_general(
        left, right, (((0,), (0,)), ((), ())), preferred_element_type=jnp.float32
    )


def row_scale(value_in):
    return lax.rsqrt(jnp.mean(value_in * value_in, axis=-1, keepdims=True) + epsilon)


def norm_backward(grad_normed, normed_unit, row_factor, gain_full):
    scaled_grad = grad_normed * gain_full
    return row_factor * (
        scaled_grad - normed_unit * jnp.mean(scaled_grad * normed_unit, axis=-1, keepdims=True)
    )


def line_result(place_ref, total_ref, outward_ref):
    place = place_ref[0]
    in_middle = (place == 1) | (place == 2)
    return jnp.where(in_middle, total_ref[...], outward_ref[...])


def allowed_pairs(query_ids, key_ids):
    shape = (query_ids.shape[0], key_ids.shape[1])
    query_pos = lax.broadcasted_iota(jnp.int32, shape, 0)
    key_pos = lax.broadcasted_iota(jnp.int32, shape, 1)
    inside = (key_pos >= query_pos) & (key_pos <= query_pos + WINDOW)
    return inside & (query_ids == key_ids) & (query_ids >= 0)


def probabilities(query, key, allowed, valid):
    scores = jnp.where(allowed, times_transposed(query, key) * score_scale, masked_score)
    top_score = jnp.max(scores, axis=-1, keepdims=True)
    weights = jnp.where(allowed, jnp.exp(scores - top_score), 0.0)
    totals = jnp.where(valid, jnp.sum(weights, axis=-1, keepdims=True), 1.0)
    return weights / totals


def keys_of(step, first_refs, before_refs, refs, columns):
    out = []
    for first_ref, before_ref, ref in zip(first_refs, before_refs, refs):
        before = before_ref[:, columns]
        if first_ref is not None:
            before = jnp.where(step == 0, first_ref[:, columns], before)
        out.append(jnp.concatenate([before, ref[:, columns]], axis=0))
    return out


def split_refs(first, refs):
    q_ref, k_ref, v_ref, k_before, v_before = refs[:5]
    firsts = refs[5:7] if first else (None, None)
    refs = refs[7 if first else 5 :]
    return (q_ref, (k_ref, v_ref), (k_before, v_before), firsts), refs[:2], refs[2:]


def attend_kernel(first, *refs):
    (q_ref, own, before, firsts), (query_ids_ref, key_ids_ref), rest = split_refs(first, refs)
    out_weight_ref = rest[0]
    attended_ref, term_ref = rest[-2:]
    step = pl.program_id(0)
    query_ids = query_ids_ref[...]
    allowed = allowed_pairs(query_ids, key_ids_ref[0])
    valid = query_ids >= 0
    for head in range(q_ref.shape[1] // HEAD_DIM):
        columns = slice(head * HEAD_DIM, (head + 1) * HEAD_DIM)
        key, value = keys_of(step, firsts, before, own, columns)
        probs = probabilities(q_ref[:, columns], key, allowed, valid)
        attended_ref[:, columns] = times(probs.astype(low_type), value).astype(low_type)
    term_ref[...] = times_transposed(attended_ref[...], out_weight_ref[...]).astype(low_type)


def attend_back_kernel(
    first, names, counts, place_ref, tokens_ref, attn_sum_ref, total_ref, outward_ref, cotangent_ref,
    gain_ref, *refs,
):
    (q_ref, own, before, firsts), (query_ids_ref, key_ids_ref), rest = split_refs(first, refs)
    out_weight_ref = rest[0]
    inputs = dict(zip(names[0], rest[1 : 1 + counts[0]]))
    outputs = dict(zip(names[1], rest[1 + counts[0] + counts[1] :]))
    scratch = rest[1 + counts[0] + counts[1] + len(names[1]) :]
    spread, query_grads = scratch[:2]
    step = pl.program_id(0)
    last = pl.num_programs(0) - 1
    rows, width = q_ref.shape
    if "weight" in inputs:
        held, arrived = scratch[2:]
        fetch = pltpu.make_async_copy(
            inputs["weight"].at[:, : held.shape[1]], held, arrived
        )

        @pl.when(step == 0)
        def _():
            fetch.start()

    middle = tokens_ref[...].astype(jnp.float32) + attn_sum_ref[...].astype(jnp.float32)
    factor = row_scale(middle)
    unit = middle * factor
    grad_sum = line_result(place_ref, total_ref, outward_ref).astype(jnp.float32)
    gain_part = jnp.sum(grad_sum * unit, axis=0, keepdims=True)
    middle_grad = cotangent_ref[...].astype(jnp.float32) + norm_backward(
        grad_sum, unit, factor, gain_ref[...]
    )
    low = middle_grad.astype(low_type)
    outputs["low"][...] = low
    attended_grad = times(low, out_weight_ref[...]).astype(low_type)

    @pl.when(step == 0)
    def _():
        outputs["gain_part"][...] = gain_part
        spread[...] = jnp.zeros_like(spread)

    @pl.when(step > 0)
    def _():
        outputs["gain_part"][...] += gain_part

    query_ids = query_ids_ref[...]
    allowed = allowed_pairs(query_ids, key_ids_ref[0])
    valid = query_ids >= 0
    part = pl.ds(pl.multiple_of(step * rows, rows), rows)
    span = pl.ds(pl.multiple_of(step * rows, rows), rows + WINDOW)
    for head in range(width // HEAD_DIM):
        columns = slice(head * HEAD_DIM, (head + 1) * HEAD_DIM)
        value_columns = slice(width + head * HEAD_DIM, width + (head + 1) * HEAD_DIM)
        query = q_ref[:, columns]
        key, value = keys_of(step, firsts, before, own, columns)
        out_grad = attended_grad[:, columns]
        probs = probabilities(query, key, allowed, valid)
        prob_grad = times_transposed(out_grad, value)
        centre = jnp.sum(prob_grad * probs, axis=-1, keepdims=True)
        score_grad = (probs * (prob_grad - centre)).astype(low_type)
        query_grads[part, columns] = (times(score_grad, key) * score_scale).astype(low_type)
        spread[span, columns] += inner_rows(score_grad, query) * score_scale
        spread[span, value_columns] += inner_rows(probs.astype(low_type), out_grad)

    @pl.when(step == last)
    def _():
        if "own" in outputs:
            outputs["query_grad"][...] = query_grads[...]
            outputs["own"][...] = spread[WINDOW:, :].astype(low_type)
        if "before" in outputs:
            outputs["before"][...] = spread[:WINDOW, :]
        if "weight" not in inputs:
            return
        grads_ref = outputs["grads"]
        kept = grads_ref.shape[0] - WINDOW
        if "own" in inputs:
            grads_ref[:, :width] = inputs["query_grad"][...]
            grads_ref[:kept, width:] = inputs["own"][:kept, :]
            tail, after = inputs["own"][kept:, :].astype(jnp.float32), spread[:WINDOW, :]
        else:
            grads_ref[:, :width] = query_grads[...]
            grads_ref[:kept, width:] = spread[WINDOW : WINDOW + kept, :].astype(low_type)
            tail, after = spread[WINDOW + kept :, :], inputs["after"][...]
        grads_ref[kept:, width:] = (tail + after).astype(low_type)
        fetch.wait()
        outputs["term"][...] = times_transposed(grads_ref[...], held[...]).astype(low_type)


def attn_term_kernel(query_grad_ref, own_ref, after_ref, weight_ref, *rest):
    grads_ref, term_ref = rest[-2:]
    rows, width = query_grad_ref.shape

    @pl.when(pl.program_id(0) == 0)
    def _():
        kept = rows - WINDOW
        grads_ref[:, :width] = query_grad_ref[...]
        grads_ref[:kept, width:] = own_ref[:kept, :]
        grads_ref[kept:, width:] = (
            own_ref[kept:, :].astype(jnp.float32) + after_ref[...]
        ).astype(low_type)

    term_ref[...] = times_transposed(grads_ref[...], weight_ref[...]).astype(low_type)


def attn_weight_grads_kernel(normed_ref, low_ref, grads_ref, attended_ref, result_ref):
    step = pl.program_id(0)

    @pl.when(step < 3)
    def _():
        result_ref[...] = inner_rows(normed_ref[...], grads_ref[...]).astype(low_type)

    @pl.when(step == 3)
    def _():
        result_ref[...] = inner_rows(low_ref[...], attended_ref[...]).astype(low_type)


def tokens_back_kernel(
    place_ref, middle_grad_ref, total_ref, outward_ref, tokens_ref, factor_ref, gain_ref, *rest
):
    tokens_grad_ref, gain_part_ref = rest[-2:]
    factor = factor_ref[...]
    unit = tokens_ref[...].astype(jnp.float32) * factor
    grad_sum = line_result(place_ref, total_ref, outward_ref).astype(jnp.float32)
    tokens_grad_ref[...] = middle_grad_ref[...].astype(jnp.float32) + norm_backward(
        grad_sum, unit, factor, gain_ref[...]
    )
    gain_part = jnp.sum(grad_sum * unit, axis=0, keepdims=True)

    @pl.when(pl.program_id(0) == 0)
    def _():
        gain_part_ref[...] = gain_part

    @pl.when(pl.program_id(0) > 0)
    def _():
        gain_part_ref[...] += gain_part


def output_kernel(place_ref, tokens_ref, attn_sum_ref, total_ref, outward_ref, *rest):
    middle = tokens_ref[...].astype(jnp.float32) + attn_sum_ref[...].astype(jnp.float32)
    mlp_sum = line_result(place_ref, total_ref, outward_ref).astype(jnp.float32)
    rest[-1][...] = (middle + mlp_sum).astype(low_type)


def mlp_pieces(hidden):
    whole = hidden // WIDE * WIDE
    pieces = []
    for start in range(0, whole, WIDE):
        for k in range(3):
            pieces.append(slice(k * whole + start, k * whole + start + WIDE))
    pieces.append(slice(3 * whole, 3 * hidden))
    return whole, pieces


def mlp_layout(gate, up, down):
    whole = gate.shape[1] // WIDE * WIDE
    return jnp.concatenate(
        [m[:, :whole] for m in (gate, up, down)] + [m[:, whole:] for m in (gate, up, down)], axis=1
    )


def mlp_kernel(
    first_row, place_ref, tokens_ref, total_ref, outward_ref, cotangent_ref, gain_ref, weight_ref, *rest
):
    leaving = rest[-19:-13]
    (
        tokens, attn_sum, cotangent, normed_ref, activation_ref, grads_ref, term_ref, mlp_ref,
        term_part, mlp_part, held, arrived, left,
    ) = rest[-13:]
    rows, hidden = activation_ref.shape
    whole, pieces = mlp_pieces(hidden)
    half = hidden - whole
    tail = 3 * whole
    mine = pl.ds(first_row, rows)
    place = place_ref[0]
    in_middle = (place == 1) | (place == 2)

    fetch_tokens = pltpu.make_async_copy(tokens_ref.at[mine], tokens, arrived.at[0])
    fetch_total = pltpu.make_async_copy(total_ref, attn_sum, arrived.at[1])
    fetch_outward = pltpu.make_async_copy(outward_ref, attn_sum, arrived.at[1])
    fetch_cotangent = pltpu.make_async_copy(cotangent_ref.at[mine], cotangent, arrived.at[2])
    fetch_tokens.start()
    pl.when(in_middle)(fetch_total.start)
    pl.when(jnp.logical_not(in_middle))(fetch_outward.start)
    fetch_cotangent.start()
    copies = [
        pltpu.make_async_copy(weight_ref.at[:, piece], held.at[:, piece], arrived.at[3 + i])
        for i, piece in enumerate(pieces)
    ]
    for copy in copies:
        copy.start()
    sources = (attn_sum, normed_ref, activation_ref, grads_ref, term_ref, mlp_ref)
    out_copies = [
        pltpu.make_async_copy(
            source, target.at[mine] if i in (1, 2, 3) else target, left.at[i]
        )
        for i, (source, target) in enumerate(zip(sources, leaving))
    ]

    fetch_tokens.wait()
    fetch_total.wait()
    middle = tokens[...].astype(jnp.float32) + attn_sum[...].astype(jnp.float32)
    normed_ref[...] = (middle * row_scale(middle) * gain_ref[...]).astype(low_type)
    fetch_cotangent.wait()
    normed = normed_ref[...]
    cot = cotangent[...]

    def inner(start, stop, gate, up, act_grad):
        sigmoid_gate = jax.nn.sigmoid(gate)
        silu_gate = gate * sigmoid_gate
        activation_ref[:, start:stop] = (silu_gate * up).astype(low_type)
        grads_ref[:, start:stop] = (
            act_grad * up * (sigmoid_gate + silu_gate * (1.0 - sigmoid_gate))
        ).astype(low_type)
        grads_ref[:, hidden + start : hidden + stop] = (act_grad * silu_gate).astype(low_type)

    def whole_piece(j):
        for copy in copies[3 * j : 3 * j + 3]:
            copy.wait()
        gate, up, down = (held[:, piece] for piece in pieces[3 * j : 3 * j + 3])
        inner(j * WIDE, (j + 1) * WIDE, times(normed, gate), times(normed, up), times(cot, down))

    def back(rows, start, stop):
        term = times_transposed(grads_ref[:, start:stop], held[rows, start:stop])
        term += times_transposed(
            grads_ref[:, hidden + start : hidden + stop], held[rows, whole + start : whole + stop]
        )
        down = held[rows, 2 * whole + start : 2 * whole + stop]
        return term, times_transposed(activation_ref[:, start:stop], down)

    blocks = [slice(start, start + 2 * WIDE) for start in range(0, held.shape[0], 2 * WIDE)]
    early = whole // WIDE // 2 + 1
    for j in range(early):
        whole_piece(j)
    for rows in blocks:
        term_part[:, rows], mlp_part[:, rows] = back(rows, 0, early * WIDE)
    for j in range(early, whole // WIDE):
        whole_piece(j)
    copies[-1].wait()
    both = times(normed, held[:, tail : tail + 2 * half])
    inner(
        whole, hidden, both[:, :half], both[:, half:], times(cot, held[:, tail + 2 * half :])
    )
    for copy in out_copies[:4]:
        copy.start()

    pair = jnp.concatenate([grads_ref[:, whole:hidden], grads_ref[:, hidden + whole :]], axis=1)
    for rows in blocks:
        term, mlp = back(rows, early * WIDE, whole)
        term += times_transposed(pair, held[rows, tail : tail + 2 * half]) + term_part[:, rows]
        mlp += times_transposed(activation_ref[:, whole:], held[rows, tail + 2 * half :])
        term_ref[:, rows] = term.astype(low_type)
        mlp_ref[:, rows] = (mlp + mlp_part[:, rows]).astype(low_type)
    for copy in out_copies[4:]:
        copy.start()
    for copy in out_copies:
        copy.wait()


def block_of(shape, *place):
    return pl.BlockSpec(shape, lambda i: place)


smem = pl.BlockSpec(memory_space=pltpu.SMEM)
anywhere = pl.BlockSpec(memory_space=pl.ANY)


def call(kernel, name, operands, results, shared, steps=1, scratch=()):
    arrays = [array for array, _ in operands]
    specs = [spec for _, spec in operands]
    aliases = {}
    for index, kept in shared.items():
        if kept is not None:
            aliases[len(arrays)] = index
            arrays.append(kept)
            specs.append(anywhere)
    return pl.pallas_call(
        kernel,
        grid=(steps,),
        in_specs=specs,
        out_specs=[spec for _, _, spec in results],
        out_shape=[jax.ShapeDtypeStruct(shape, dtype) for shape, dtype, _ in results],
        input_output_aliases=aliases,
        scratch_shapes=list(scratch),
        compiler_params=pltpu.CompilerParams(
            dimension_semantics=("arbitrary",), vmem_limit_bytes=GRANTS[name] * MEGA
        ),
        cost_estimate=pl.CostEstimate(flops=1, bytes_accessed=1, transcendentals=0),
        name=name,
    )(*arrays)


class Layer:
    def __init__(self, tokens, cotangent, head_width, hidden):
        self.tokens, self.cotangent = tokens, cotangent
        self.total_rows, self.width = tokens.shape
        self.rows = self.total_rows // CHUNKS
        self.head_width, self.hidden = head_width, hidden
        self.place = lax.axis_index("mp").astype(jnp.int32).reshape(1)
        self.whole = block_of((self.rows, self.width), 0, 0)
        self.gain_row = block_of((1, self.width), 0, 0)

    def chunk(self, c, columns=None):
        return block_of((self.rows, columns or self.width), c, 0)

    def qkv_operands(self, c, halves, halo, query_ids, key_ids):
        head_width = self.head_width
        half_rows = halves[0].shape[0]
        half, first_row = divmod(c * self.rows, half_rows)
        first_part, first_window = first_row // QUERY_ROWS, first_row // WINDOW
        stride = QUERY_ROWS // WINDOW

        def part(k):
            return pl.BlockSpec((QUERY_ROWS, head_width), lambda i: (first_part + i, k))

        def before(k):
            return pl.BlockSpec(
                (WINDOW, head_width),
                lambda i: (jnp.maximum(first_window + stride * i - 1, 0), k),
            )

        source = halves[half]
        operands = [(source, part(k)) for k in range(3)]
        operands += [(source, before(k)) for k in (1, 2)]
        if c == 0:
            operands += [(halo, block_of((WINDOW, head_width), 0, k)) for k in range(2)]
        elif first_row == 0:
            last = half_rows // WINDOW - 1
            operands += [
                (halves[half - 1], block_of((WINDOW, head_width), last, k)) for k in (1, 2)
            ]
        parts = self.rows // QUERY_ROWS
        ids = [
            (query_ids, pl.BlockSpec((QUERY_ROWS, 1), lambda i: (c * parts + i, 0))),
            (
                key_ids,
                pl.BlockSpec((1, 1, QUERY_ROWS + WINDOW), lambda i: (c * parts + i, 0, 0)),
            ),
        ]
        return first_row == 0, operands + ids

    def part(self, c, columns):
        parts = self.rows // QUERY_ROWS
        return pl.BlockSpec((QUERY_ROWS, columns), lambda i: (c * parts + i, 0))

    def attend(self, c, first_and_qkv, attn_weight, attended):
        first, qkv_operands = first_and_qkv
        return call(
            functools.partial(attend_kernel, first),
            "attend",
            qkv_operands + [(attn_weight, block_of((self.width, self.head_width), 0, 3))],
            [
                ((self.total_rows, self.head_width), low_type, self.part(c, self.head_width)),
                ((self.rows, self.width), low_type, self.part(0, self.width)),
            ],
            {0: attended},
            steps=self.rows // QUERY_ROWS,
        )

    def feed_forward(self, c, line, gain, weight, shared):
        rows, width, hidden = self.rows, self.width, self.hidden
        block = pltpu.VMEM((rows, width), low_type)
        return call(
            functools.partial(mlp_kernel, c * rows),
            "feed_forward",
            [
                (self.place, smem),
                (self.tokens, anywhere),
                (line[0], anywhere),
                (line[1], anywhere),
                (self.cotangent, anywhere),
                (gain, self.gain_row),
                (weight, anywhere),
            ],
            [
                ((rows, width), low_type, anywhere),
                ((self.total_rows, width), low_type, anywhere),
                ((self.total_rows, hidden), low_type, anywhere),
                ((self.total_rows, 2 * hidden), low_type, anywhere),
                ((rows, width), low_type, anywhere),
                ((rows, width), low_type, anywhere),
            ],
            {index + 1: kept for index, kept in enumerate(shared)},
            scratch=[block, block, block, block]
            + [
                pltpu.VMEM((rows, hidden), low_type),
                pltpu.VMEM((rows, 2 * hidden), low_type),
                block,
                block,
                pltpu.VMEM((rows, width), jnp.float32),
                pltpu.VMEM((rows, width), jnp.float32),
                pltpu.VMEM((width, 3 * hidden), low_type),
                pltpu.SemaphoreType.DMA((3 + len(mlp_pieces(hidden)[1]),)),
                pltpu.SemaphoreType.DMA((6,)),
            ],
        )

    def attend_back(
        self, c, attn_sum, line, gain, first_and_qkv, attn_weight, low_all,
        keep=False, give_before=False, earlier=None, after=None, grads_all=None,
    ):
        first, qkv_operands = first_and_qkv
        rows, width, head_width = self.rows, self.width, self.head_width
        mine, alone = self.part(c, width), self.part(0, width)
        query_spec = block_of((rows, head_width), 0, 0)
        own_spec = block_of((rows, 2 * head_width), 0, 0)
        window_spec = block_of((WINDOW, 2 * head_width), 0, 0)
        more, results = {}, {
            "low": ((self.total_rows, width), low_type, mine),
            "gain_part": ((1, width), jnp.float32, self.gain_row),
        }
        shared = {0: low_all}
        scratch = [
            pltpu.VMEM((rows + WINDOW, 2 * head_width), jnp.float32),
            pltpu.VMEM((rows, head_width), low_type),
        ]
        if keep:
            results["query_grad"] = ((rows, head_width), low_type, query_spec)
            results["own"] = ((rows, 2 * head_width), low_type, own_spec)
        if give_before:
            results["before"] = ((WINDOW, 2 * head_width), jnp.float32, window_spec)
        term_chunk = None
        if earlier is not None:
            term_chunk = earlier[0]
            more["query_grad"], more["own"] = (earlier[1], query_spec), (earlier[2], own_spec)
        elif after is not None:
            term_chunk = c
            more["after"] = (after, window_spec)
        if term_chunk is not None:
            more["weight"] = (attn_weight, anywhere)
            shared[len(results)] = grads_all
            results["grads"] = (
                (self.total_rows, 3 * head_width),
                low_type,
                block_of((rows, 3 * head_width), term_chunk, 0),
            )
            results["term"] = ((rows, width), low_type, self.whole)
            scratch += [pltpu.VMEM((width, 3 * head_width), low_type), pltpu.SemaphoreType.DMA]
        kept = sum(array is not None for array in shared.values())
        outputs = call(
            functools.partial(
                attend_back_kernel, first, (tuple(more), tuple(results)), (len(more), kept)
            ),
            "attend_back",
            [
                (self.place, smem),
                (self.tokens, mine),
                (attn_sum, alone),
                (line[0], alone),
                (line[1], alone),
                (self.cotangent, mine),
                (gain, self.gain_row),
            ]
            + qkv_operands
            + [(attn_weight, block_of((width, head_width), 0, 3))]
            + list(more.values()),
            list(results.values()),
            shared,
            steps=rows // QUERY_ROWS,
            scratch=scratch,
        )
        return dict(zip(results, outputs))

    def attn_term(self, c, query_grad, own, after, attn_weight, grads_all):
        rows, width, head_width = self.rows, self.width, self.head_width
        part = width // CHUNKS
        return call(
            attn_term_kernel,
            "attn_term",
            [
                (query_grad, block_of((rows, head_width), 0, 0)),
                (own, block_of((rows, 2 * head_width), 0, 0)),
                (after, block_of((WINDOW, 2 * head_width), 0, 0)),
                (attn_weight, pl.BlockSpec((part, 3 * head_width), lambda i: (i, 0))),
            ],
            [
                ((self.total_rows, 3 * head_width), low_type, self.chunk(c, 3 * head_width)),
                ((rows, width), low_type, pl.BlockSpec((rows, part), lambda i: (0, i))),
            ],
            {0: grads_all},
            steps=width // part,
        )

    def attn_weight_grads(self, normed_attn, grads_all, low_all, attended):
        rows, width, head_width = self.total_rows, self.width, self.head_width
        return call(
            attn_weight_grads_kernel,
            "attn_weight_grads",
            [
                (normed_attn, block_of((rows, width), 0, 0)),
                (low_all, block_of((rows, width), 0, 0)),
                (grads_all, pl.BlockSpec((rows, head_width), lambda i: (0, jnp.minimum(i, 2)))),
                (attended, block_of((rows, head_width), 0, 0)),
            ],
            [((width, 4 * head_width), low_type, pl.BlockSpec((width, head_width), lambda i: (0, i)))],
            {},
            steps=4,
        )[0]

    def tokens_back(self, c, middle_grad, line, factor, gain, tokens_grad):
        return call(
            tokens_back_kernel,
            "tokens_back",
            [
                (self.place, smem),
                (middle_grad, self.part(c, self.width)),
                (line[0], self.part(0, self.width)),
                (line[1], self.part(0, self.width)),
                (self.tokens, self.part(c, self.width)),
                (factor, self.part(c, 1)),
                (gain, self.gain_row),
            ],
            [
                ((self.total_rows, self.width), jnp.float32, self.part(c, self.width)),
                ((1, self.width), jnp.float32, self.gain_row),
            ],
            {0: tokens_grad},
            steps=self.rows // QUERY_ROWS,
        )

    def output(self, c, attn_sum, line, out):
        return call(
            output_kernel,
            "output",
            [
                (self.place, smem),
                (self.tokens, self.part(c, self.width)),
                (attn_sum, self.part(0, self.width)),
                (line[0], self.part(0, self.width)),
                (line[1], self.part(0, self.width)),
            ],
            [((self.total_rows, self.width), low_type, self.part(c, self.width))],
            {0: out},
            steps=self.rows // QUERY_ROWS,
        )[0]


def middle_add_kernel(place_ref, left_ref, right_ref, result_ref, left, right, arrived, left_sem):
    place = place_ref[0]

    @pl.when((place == 1) | (place == 2))
    def _():
        parts = [
            pl.ds(start, QUERY_ROWS // 2) for start in range(0, left.shape[0], QUERY_ROWS // 2)
        ]
        fetches = [
            (
                pltpu.make_async_copy(left_ref.at[rows], left.at[rows], arrived.at[2 * i]),
                pltpu.make_async_copy(right_ref.at[rows], right.at[rows], arrived.at[2 * i + 1]),
            )
            for i, rows in enumerate(parts)
        ]
        for one, other in fetches:
            one.start()
            other.start()
        gives = [
            pltpu.make_async_copy(left.at[rows], result_ref.at[rows], left_sem.at[i])
            for i, rows in enumerate(parts)
        ]
        for rows, (one, other), give in zip(parts, fetches, gives):
            one.wait()
            other.wait()
            left[rows, :] = (
                left[rows, :].astype(jnp.float32) + right[rows, :].astype(jnp.float32)
            ).astype(low_type)
            give.start()
        for give in gives:
            give.wait()


def middle_add(place, left, right):
    rows, width = left.shape
    parts = 2 * rows // QUERY_ROWS
    return call(
        middle_add_kernel,
        "middle_add",
        [(place, smem), (left, anywhere), (right, anywhere)],
        [((rows, width), low_type, anywhere)],
        {},
        scratch=[
            pltpu.VMEM((rows, width), low_type),
            pltpu.VMEM((rows, width), low_type),
            pltpu.SemaphoreType.DMA((2 * parts,)),
            pltpu.SemaphoreType.DMA((parts,)),
        ],
    )[0]


def from_behind(block, axis, distance):
    devices = range(lax.axis_size(axis))
    route = [(i - distance, i) for i in devices if i - distance in devices]
    return lax.ppermute(block, axis, route)


def hold(values):
    return lax.optimization_barrier(values)


def add_low(left, right):
    return (left.astype(jnp.float32) + right.astype(jnp.float32)).astype(low_type)


class LineSums:
    def __init__(self, axis):
        self.axis = axis
        self.place = lax.axis_index(axis).astype(jnp.int32).reshape(1)
        self.first = self.second = self.third = None
        self.results = {}

    def step(self, name, part, values, early=False):
        first, second, third = self.first, self.second, self.third
        own = None if first is None else first[1]
        half = None if second is None else second[1]
        part, own, half, values = hold((part, own, half, values))
        self.first = self.second = self.third = None
        new_half = new_total = done = None

        def send_part():
            if part is not None:
                self.first = (name, part, lax.ppermute(part, self.axis, [(0, 1), (3, 2)]))

        if early:
            send_part()
        if own is not None:
            new_half = middle_add(self.place, own, first[2])
            across = lax.ppermute(new_half, self.axis, [(1, 2), (2, 1)])
        if half is not None:
            new_total = middle_add(self.place, half, second[2])
            outward = lax.ppermute(new_total, self.axis, [(1, 0), (2, 3)])
        if early:
            new_half, new_total, values = hold((new_half, new_total, values))
        else:
            new_half, new_total, part, values = hold((new_half, new_total, part, values))
            send_part()
        if third is not None:
            done, values = hold((third[1:], values))
        if own is not None:
            self.second = (first[0], new_half, across)
        if half is not None:
            self.third = (second[0], new_total, outward)
        if third is not None:
            self.results[third[0]] = done
        return values


def small_sum_scatter(value, axis):
    size = lax.axis_size(axis)
    place = lax.axis_index(axis)
    bit = size // 2
    while bit >= 1:
        half = value.shape[1] // 2
        low, high = value[:, :half], value[:, half:]
        upper = (place & bit) != 0
        keep = jnp.where(upper, high, low)
        give = jnp.where(upper, low, high)
        value = keep + lax.ppermute(give, axis, [(i, i ^ bit) for i in range(size)])
        bit //= 2
    return value


def scattered(value):
    return lax.psum_scatter(value, "seq", scatter_dimension=0, tiled=True)


def body(
    tokens,
    group_ids,
    gain_attn,
    w_query,
    w_key,
    w_value,
    w_out,
    gain_mlp,
    w_gate,
    w_up,
    w_down,
    cotangent,
):
    head_width = w_query.shape[1]
    hidden = w_gate.shape[1]
    layer = Layer(tokens, cotangent, head_width, hidden)
    line = LineSums("mp")
    results = line.results
    total_rows = tokens.shape[0]

    attn_shard = jnp.concatenate([w_query, w_key, w_value, w_out.T], axis=1)
    attn_weight = lax.all_gather(attn_shard, "seq", axis=0, tiled=True)
    gains = lax.all_gather(jnp.stack([gain_attn, gain_mlp]), "seq", axis=1, tiled=True)
    gain_one = gains[:1].astype(jnp.float32)
    gain_two = gains[1:].astype(jnp.float32)
    ids_halo = from_behind(group_ids[-WINDOW:] + 1, "seq", 1) - 1
    ids_ext = jnp.concatenate([ids_halo, group_ids], axis=0)
    query_ids = group_ids[:, None]
    key_ids = jnp.stack(
        [
            ids_ext[None, start : start + QUERY_ROWS + WINDOW]
            for start in range(0, total_rows, QUERY_ROWS)
        ]
    )
    inputs = tokens.astype(jnp.float32)
    factor_one = row_scale(inputs)
    normed_attn = (inputs * factor_one * gain_one).astype(low_type)
    mlp_shard = mlp_layout(w_gate, w_up, w_down.T)
    mlp_shard, normed_attn, factor_one, query_ids, key_ids, gain_two, attn_weight = hold(
        (mlp_shard, normed_attn, factor_one, query_ids, key_ids, gain_two, attn_weight)
    )
    mlp_weight = lax.all_gather(mlp_shard, "seq", axis=0, tiled=True)

    half_rows = total_rows // 2
    qkv_weight = attn_weight[:, : 3 * head_width]
    halves = [times(normed_attn[:half_rows], qkv_weight).astype(low_type)]
    order = [1, 2, 0, 3]

    def pieces_of(c):
        return layer.qkv_operands(c, halves, halo, query_ids, key_ids)

    halo = None
    attended, term = layer.attend(order[0], pieces_of(order[0]), attn_weight, None)
    attended, later_rows, halves[0] = line.step(
        ("attn", order[0]), term, (attended, normed_attn[half_rows:], halves[0]), True
    )
    halves.append(times(later_rows, qkv_weight).astype(low_type))
    halo = from_behind(halves[1][-WINDOW:, head_width:], "seq", 1)
    for c in order[1:]:
        attended, term = layer.attend(c, pieces_of(c), attn_weight, attended)
        values = line.step(("attn", c), term, (attended, halves[0], halves[1], halo), True)
        attended, halves[0], halves[1], halo = values

    attn_sums, mlp_terms = {}, {}
    shared = (None, None, None)
    for c in order:
        attn_sums[c], *shared, term, mlp_terms[c] = layer.feed_forward(
            c, results["attn", c], gain_two, mlp_weight, shared
        )
        shared = line.step(("mlp", c), term, tuple(shared), True)
    normed_mlp, activations, mlp_grads = shared

    tokens_grad = out = None
    gain_one_parts, gain_two_parts = [], []

    def back(c, low_all, **more):
        made = layer.attend_back(
            c, attn_sums[c], results["mlp", c], gain_two, pieces_of(c), attn_weight, low_all, **more
        )
        gain_two_parts.append(made["gain_part"])
        return made

    def out_step(c, values, early=True):
        return line.step(("out", c), mlp_terms[c], values, early)

    gate_up_grad = inner_rows(normed_mlp, mlp_grads).astype(low_type)
    gate_up_grad, activations = out_step(order[0], (gate_up_grad, activations))
    gate_up_share = scattered(gate_up_grad)
    down_grad = inner_rows(cotangent, activations).astype(low_type)
    results["mlp", 1], down_grad = hold((results["mlp", 1], down_grad))
    made = back(1, None, keep=True, give_before=True)
    made, down_grad = out_step(order[1], (made, down_grad))
    down_share = scattered(down_grad)
    after_none = made["before"]
    made = back(2, made["low"], keep=True, earlier=(1, made["query_grad"], made["own"]))
    made, after_none = line.step(("attn_back", 1), made["term"], (made, after_none), True)
    kept = made["query_grad"], made["own"]
    made = back(0, made["low"], give_before=True, after=after_none, grads_all=made["grads"])
    made, kept = line.step(("attn_back", 0), made["term"], (made, kept), True)
    behind = from_behind(made["before"].astype(low_type), "seq", -1)
    made = back(3, made["low"], keep=True, earlier=(2, *kept), grads_all=made["grads"])
    made, behind = line.step(("attn_back", 2), made["term"], (made, behind), True)
    grads_all, term = layer.attn_term(
        3, made["query_grad"], made["own"], behind.astype(jnp.float32), attn_weight, made["grads"]
    )
    low_all = made["low"]
    attn_grad = layer.attn_weight_grads(normed_attn, grads_all, low_all, attended)
    attn_grad = line.step(("attn_back", 3), term, attn_grad, True)
    attn_share = scattered(attn_grad)

    def finish_tokens(c):
        nonlocal tokens_grad
        tokens_grad, part = layer.tokens_back(
            c, low_all, results["attn_back", c], factor_one, gain_one, tokens_grad
        )
        gain_one_parts.append(part)

    def finish_out(c):
        nonlocal out
        out = layer.output(c, attn_sums[c], results["out", c], out)

    finish_tokens(1)
    tokens_grad, gain_two_parts = out_step(order[2], (tokens_grad, gain_two_parts), True)
    finish_out(order[0])
    finish_tokens(0)
    tokens_grad, out = out_step(order[3], (tokens_grad, out), True)
    finish_tokens(2)
    finish_out(order[1])
    tokens_grad, out = line.step(None, None, (tokens_grad, out))
    finish_tokens(3)
    gain_parts = jnp.concatenate([sum(gain_one_parts), sum(gain_two_parts)], axis=0)
    gate_out = gate_up_share[:, :hidden].astype(jnp.float32)
    up_out = gate_up_share[:, hidden:].astype(jnp.float32)
    values = line.step(None, None, (tokens_grad, out, gain_parts, gate_out, up_out))
    tokens_grad, out, gain_parts, gate_out, up_out = values
    finish_out(order[2])
    down_out = down_share.astype(jnp.float32).T
    attn_out = attn_share.astype(jnp.float32)
    attn_outs = [attn_out[:, k * head_width : (k + 1) * head_width] for k in range(4)]
    attn_outs[3] = attn_outs[3].T
    out, down_out, gain_parts, attn_outs = line.step(
        None, None, (out, down_out, gain_parts, attn_outs)
    )
    gain_share = small_sum_scatter(gain_parts, "seq")
    finish_out(order[3])
    return (
        out,
        tokens_grad,
        gain_share[0],
        attn_outs[0],
        attn_outs[1],
        attn_outs[2],
        attn_outs[3],
        gain_share[1],
        gate_out,
        up_out,
        down_out,
    )


def solution(mesh):
    placed = (
        P("seq", None),
        P("seq"),
        P("seq"),
        P("seq", "mp"),
        P("seq", "mp"),
        P("seq", "mp"),
        P("mp", "seq"),
        P("seq"),
        P("seq", "mp"),
        P("seq", "mp"),
        P("mp", "seq"),
        P("seq", None),
    )
    return jax.shard_map(
        body,
        mesh=mesh,
        in_specs=placed,
        out_specs=(
            P("seq", None),
            P("seq", None),
            P("seq"),
            P("seq", "mp"),
            P("seq", "mp"),
            P("seq", "mp"),
            P("mp", "seq"),
            P("seq"),
            P("seq", "mp"),
            P("seq", "mp"),
            P("mp", "seq"),
        ),
        check_vma=False,
    )
```

```python
import functools

import jax
import jax.numpy as jnp
from jax import lax
from jax.experimental import pallas as pl
from jax.experimental.pallas import tpu as pltpu
from jax.sharding import PartitionSpec as P

HEAD_DIM = 128
WINDOW = 64
CHUNKS = 4
QUERY_ROWS = 128
WIDE = 256

epsilon = 1e-05
masked_score = -1e30
score_scale = HEAD_DIM ** (-0.5)
MEGA = 1024 * 1024
GRANTS = {'middle_add': 8, 'attend': 40, 'feed_forward': 44, 'attend_back': 56, 'attn_term': 40, 'attn_weight_grads': 40, 'tokens_back': 56, 'output': 56}
low_type = jnp.bfloat16


def times(left, right):
    return jnp.dot(left, right, preferred_element_type=jnp.float32)


def times_transposed(left, right):
    return lax.dot_general(
        left, right, (((1,), (1,)), ((), ())), preferred_element_type=jnp.float32
    )


def inner_rows(left, right):
    return lax.dot_general(
        left, right, (((0,), (0,)), ((), ())), preferred_element_type=jnp.float32
    )


def row_scale(value_in):
    return lax.rsqrt(jnp.mean(value_in * value_in, axis=-1, keepdims=True) + epsilon)


def norm_backward(grad_normed, normed_unit, row_factor, gain_full):
    scaled_grad = grad_normed * gain_full
    return row_factor * (
        scaled_grad - normed_unit * jnp.mean(scaled_grad * normed_unit, axis=-1, keepdims=True)
    )


def line_result(place_ref, total_ref, outward_ref):
    place = place_ref[0]
    in_middle = (place == 1) | (place == 2)
    return jnp.where(in_middle, total_ref[...], outward_ref[...])


def allowed_pairs(query_ids, key_ids):
    shape = (query_ids.shape[0], key_ids.shape[1])
    query_pos = lax.broadcasted_iota(jnp.int32, shape, 0)
    key_pos = lax.broadcasted_iota(jnp.int32, shape, 1)
    inside = (key_pos >= query_pos) & (key_pos <= query_pos + WINDOW)
    return inside & (query_ids == key_ids) & (query_ids >= 0)


def probabilities(query, key, allowed, valid):
    scores = jnp.where(allowed, times_transposed(query, key) * score_scale, masked_score)
    top_score = jnp.max(scores, axis=-1, keepdims=True)
    weights = jnp.where(allowed, jnp.exp(scores - top_score), 0.0)
    totals = jnp.where(valid, jnp.sum(weights, axis=-1, keepdims=True), 1.0)
    return weights / totals


def keys_of(step, first_refs, before_refs, refs, columns):
    out = []
    for first_ref, before_ref, ref in zip(first_refs, before_refs, refs):
        before = before_ref[:, columns]
        if first_ref is not None:
            before = jnp.where(step == 0, first_ref[:, columns], before)
        out.append(jnp.concatenate([before, ref[:, columns]], axis=0))
    return out


def split_refs(first, refs):
    q_ref, k_ref, v_ref, k_before, v_before = refs[:5]
    firsts = refs[5:7] if first else (None, None)
    refs = refs[7 if first else 5 :]
    return (q_ref, (k_ref, v_ref), (k_before, v_before), firsts), refs[:2], refs[2:]


def attend_kernel(first, *refs):
    (q_ref, own, before, firsts), (query_ids_ref, key_ids_ref), rest = split_refs(first, refs)
    out_weight_ref = rest[0]
    attended_ref, term_ref = rest[-2:]
    step = pl.program_id(0)
    query_ids = query_ids_ref[...]
    allowed = allowed_pairs(query_ids, key_ids_ref[0])
    valid = query_ids >= 0
    for head in range(q_ref.shape[1] // HEAD_DIM):
        columns = slice(head * HEAD_DIM, (head + 1) * HEAD_DIM)
        key, value = keys_of(step, firsts, before, own, columns)
        probs = probabilities(q_ref[:, columns], key, allowed, valid)
        attended_ref[:, columns] = times(probs.astype(low_type), value).astype(low_type)
    term_ref[...] = times_transposed(attended_ref[...], out_weight_ref[...]).astype(low_type)


def attend_back_kernel(
    first, names, counts, place_ref, tokens_ref, attn_sum_ref, total_ref, outward_ref, cotangent_ref,
    gain_ref, *refs,
):
    (q_ref, own, before, firsts), (query_ids_ref, key_ids_ref), rest = split_refs(first, refs)
    out_weight_ref = rest[0]
    inputs = dict(zip(names[0], rest[1 : 1 + counts[0]]))
    outputs = dict(zip(names[1], rest[1 + counts[0] + counts[1] :]))
    scratch = rest[1 + counts[0] + counts[1] + len(names[1]) :]
    spread, query_grads = scratch[:2]
    step = pl.program_id(0)
    last = pl.num_programs(0) - 1
    rows, width = q_ref.shape
    if "weight" in inputs:
        held, arrived = scratch[2:]
        fetch = pltpu.make_async_copy(
            inputs["weight"].at[:, : held.shape[1]], held, arrived
        )

        @pl.when(step == 0)
        def _():
            fetch.start()

    middle = tokens_ref[...].astype(jnp.float32) + attn_sum_ref[...].astype(jnp.float32)
    factor = row_scale(middle)
    unit = middle * factor
    grad_sum = line_result(place_ref, total_ref, outward_ref).astype(jnp.float32)
    gain_part = jnp.sum(grad_sum * unit, axis=0, keepdims=True)
    middle_grad = cotangent_ref[...].astype(jnp.float32) + norm_backward(
        grad_sum, unit, factor, gain_ref[...]
    )
    low = middle_grad.astype(low_type)
    outputs["low"][...] = low
    attended_grad = times(low, out_weight_ref[...]).astype(low_type)

    @pl.when(step == 0)
    def _():
        outputs["gain_part"][...] = gain_part
        spread[...] = jnp.zeros_like(spread)

    @pl.when(step > 0)
    def _():
        outputs["gain_part"][...] += gain_part

    query_ids = query_ids_ref[...]
    allowed = allowed_pairs(query_ids, key_ids_ref[0])
    valid = query_ids >= 0
    part = pl.ds(pl.multiple_of(step * rows, rows), rows)
    span = pl.ds(pl.multiple_of(step * rows, rows), rows + WINDOW)
    for head in range(width // HEAD_DIM):
        columns = slice(head * HEAD_DIM, (head + 1) * HEAD_DIM)
        value_columns = slice(width + head * HEAD_DIM, width + (head + 1) * HEAD_DIM)
        query = q_ref[:, columns]
        key, value = keys_of(step, firsts, before, own, columns)
        out_grad = attended_grad[:, columns]
        probs = probabilities(query, key, allowed, valid)
        prob_grad = times_transposed(out_grad, value)
        centre = jnp.sum(prob_grad * probs, axis=-1, keepdims=True)
        score_grad = (probs * (prob_grad - centre)).astype(low_type)
        query_grads[part, columns] = (times(score_grad, key) * score_scale).astype(low_type)
        spread[span, columns] += inner_rows(score_grad, query) * score_scale
        spread[span, value_columns] += inner_rows(probs.astype(low_type), out_grad)

    @pl.when(step == last)
    def _():
        if "own" in outputs:
            outputs["query_grad"][...] = query_grads[...]
            outputs["own"][...] = spread[WINDOW:, :].astype(low_type)
        if "before" in outputs:
            outputs["before"][...] = spread[:WINDOW, :]
        if "weight" not in inputs:
            return
        grads_ref = outputs["grads"]
        kept = grads_ref.shape[0] - WINDOW
        if "own" in inputs:
            grads_ref[:, :width] = inputs["query_grad"][...]
            grads_ref[:kept, width:] = inputs["own"][:kept, :]
            tail, after = inputs["own"][kept:, :].astype(jnp.float32), spread[:WINDOW, :]
        else:
            grads_ref[:, :width] = query_grads[...]
            grads_ref[:kept, width:] = spread[WINDOW : WINDOW + kept, :].astype(low_type)
            tail, after = spread[WINDOW + kept :, :], inputs["after"][...]
        grads_ref[kept:, width:] = (tail + after).astype(low_type)
        fetch.wait()
        outputs["term"][...] = times_transposed(grads_ref[...], held[...]).astype(low_type)


def attn_term_kernel(query_grad_ref, own_ref, after_ref, weight_ref, *rest):
    grads_ref, term_ref = rest[-2:]
    rows, width = query_grad_ref.shape

    @pl.when(pl.program_id(0) == 0)
    def _():
        kept = rows - WINDOW
        grads_ref[:, :width] = query_grad_ref[...]
        grads_ref[:kept, width:] = own_ref[:kept, :]
        grads_ref[kept:, width:] = (
            own_ref[kept:, :].astype(jnp.float32) + after_ref[...]
        ).astype(low_type)

    term_ref[...] = times_transposed(grads_ref[...], weight_ref[...]).astype(low_type)


def attn_weight_grads_kernel(normed_ref, low_ref, grads_ref, attended_ref, result_ref):
    step = pl.program_id(0)

    @pl.when(step < 3)
    def _():
        result_ref[...] = inner_rows(normed_ref[...], grads_ref[...]).astype(low_type)

    @pl.when(step == 3)
    def _():
        result_ref[...] = inner_rows(low_ref[...], attended_ref[...]).astype(low_type)


def tokens_back_kernel(
    place_ref, middle_grad_ref, total_ref, outward_ref, tokens_ref, factor_ref, gain_ref, *rest
):
    tokens_grad_ref, gain_part_ref = rest[-2:]
    factor = factor_ref[...]
    unit = tokens_ref[...].astype(jnp.float32) * factor
    grad_sum = line_result(place_ref, total_ref, outward_ref).astype(jnp.float32)
    tokens_grad_ref[...] = middle_grad_ref[...].astype(jnp.float32) + norm_backward(
        grad_sum, unit, factor, gain_ref[...]
    )
    gain_part = jnp.sum(grad_sum * unit, axis=0, keepdims=True)

    @pl.when(pl.program_id(0) == 0)
    def _():
        gain_part_ref[...] = gain_part

    @pl.when(pl.program_id(0) > 0)
    def _():
        gain_part_ref[...] += gain_part


def output_kernel(place_ref, tokens_ref, attn_sum_ref, total_ref, outward_ref, *rest):
    middle = tokens_ref[...].astype(jnp.float32) + attn_sum_ref[...].astype(jnp.float32)
    mlp_sum = line_result(place_ref, total_ref, outward_ref).astype(jnp.float32)
    rest[-1][...] = (middle + mlp_sum).astype(low_type)


def mlp_pieces(hidden):
    whole = hidden // WIDE * WIDE
    pieces = []
    for start in range(0, whole, WIDE):
        for k in range(3):
            pieces.append(slice(k * whole + start, k * whole + start + WIDE))
    pieces.append(slice(3 * whole, 3 * hidden))
    return whole, pieces


def mlp_layout(gate, up, down):
    whole = gate.shape[1] // WIDE * WIDE
    return jnp.concatenate(
        [m[:, :whole] for m in (gate, up, down)] + [m[:, whole:] for m in (gate, up, down)], axis=1
    )


def mlp_kernel(
    first_row, place_ref, tokens_ref, total_ref, outward_ref, cotangent_ref, gain_ref, weight_ref, *rest
):
    leaving = rest[-19:-13]
    (
        tokens, attn_sum, cotangent, normed_ref, activation_ref, grads_ref, term_ref, mlp_ref,
        term_part, mlp_part, held, arrived, left,
    ) = rest[-13:]
    rows, hidden = activation_ref.shape
    whole, pieces = mlp_pieces(hidden)
    half = hidden - whole
    tail = 3 * whole
    mine = pl.ds(first_row, rows)
    place = place_ref[0]
    in_middle = (place == 1) | (place == 2)

    fetch_tokens = pltpu.make_async_copy(tokens_ref.at[mine], tokens, arrived.at[0])
    fetch_total = pltpu.make_async_copy(total_ref, attn_sum, arrived.at[1])
    fetch_outward = pltpu.make_async_copy(outward_ref, attn_sum, arrived.at[1])
    fetch_cotangent = pltpu.make_async_copy(cotangent_ref.at[mine], cotangent, arrived.at[2])
    fetch_tokens.start()
    pl.when(in_middle)(fetch_total.start)
    pl.when(jnp.logical_not(in_middle))(fetch_outward.start)
    fetch_cotangent.start()
    copies = [
        pltpu.make_async_copy(weight_ref.at[:, piece], held.at[:, piece], arrived.at[3 + i])
        for i, piece in enumerate(pieces)
    ]
    for copy in copies:
        copy.start()
    sources = (attn_sum, normed_ref, activation_ref, grads_ref, term_ref, mlp_ref)
    out_copies = [
        pltpu.make_async_copy(
            source, target.at[mine] if i in (1, 2, 3) else target, left.at[i]
        )
        for i, (source, target) in enumerate(zip(sources, leaving))
    ]

    fetch_tokens.wait()
    fetch_total.wait()
    middle = tokens[...].astype(jnp.float32) + attn_sum[...].astype(jnp.float32)
    normed_ref[...] = (middle * row_scale(middle) * gain_ref[...]).astype(low_type)
    fetch_cotangent.wait()
    normed = normed_ref[...]
    cot = cotangent[...]

    def inner(start, stop, gate, up, act_grad):
        sigmoid_gate = jax.nn.sigmoid(gate)
        silu_gate = gate * sigmoid_gate
        activation_ref[:, start:stop] = (silu_gate * up).astype(low_type)
        grads_ref[:, start:stop] = (
            act_grad * up * (sigmoid_gate + silu_gate * (1.0 - sigmoid_gate))
        ).astype(low_type)
        grads_ref[:, hidden + start : hidden + stop] = (act_grad * silu_gate).astype(low_type)

    def whole_piece(j):
        for copy in copies[3 * j : 3 * j + 3]:
            copy.wait()
        gate, up, down = (held[:, piece] for piece in pieces[3 * j : 3 * j + 3])
        inner(j * WIDE, (j + 1) * WIDE, times(normed, gate), times(normed, up), times(cot, down))

    def back(rows, start, stop):
        term = times_transposed(grads_ref[:, start:stop], held[rows, start:stop])
        term += times_transposed(
            grads_ref[:, hidden + start : hidden + stop], held[rows, whole + start : whole + stop]
        )
        down = held[rows, 2 * whole + start : 2 * whole + stop]
        return term, times_transposed(activation_ref[:, start:stop], down)

    blocks = [slice(start, start + 2 * WIDE) for start in range(0, held.shape[0], 2 * WIDE)]
    early = whole // WIDE // 2 + 1
    for j in range(early):
        whole_piece(j)
    for rows in blocks:
        term_part[:, rows], mlp_part[:, rows] = back(rows, 0, early * WIDE)
    for j in range(early, whole // WIDE):
        whole_piece(j)
    copies[-1].wait()
    both = times(normed, held[:, tail : tail + 2 * half])
    inner(
        whole, hidden, both[:, :half], both[:, half:], times(cot, held[:, tail + 2 * half :])
    )
    for copy in out_copies[:4]:
        copy.start()

    pair = jnp.concatenate([grads_ref[:, whole:hidden], grads_ref[:, hidden + whole :]], axis=1)
    for rows in blocks:
        term, mlp = back(rows, early * WIDE, whole)
        term += times_transposed(pair, held[rows, tail : tail + 2 * half]) + term_part[:, rows]
        mlp += times_transposed(activation_ref[:, whole:], held[rows, tail + 2 * half :])
        term_ref[:, rows] = term.astype(low_type)
        mlp_ref[:, rows] = (mlp + mlp_part[:, rows]).astype(low_type)
    for copy in out_copies[4:]:
        copy.start()
    for copy in out_copies:
        copy.wait()


def block_of(shape, *place):
    return pl.BlockSpec(shape, lambda i: place)


smem = pl.BlockSpec(memory_space=pltpu.SMEM)
anywhere = pl.BlockSpec(memory_space=pl.ANY)


def call(kernel, name, operands, results, shared, steps=1, scratch=()):
    arrays = [array for array, _ in operands]
    specs = [spec for _, spec in operands]
    aliases = {}
    for index, kept in shared.items():
        if kept is not None:
            aliases[len(arrays)] = index
            arrays.append(kept)
            specs.append(anywhere)
    return pl.pallas_call(
        kernel,
        grid=(steps,),
        in_specs=specs,
        out_specs=[spec for _, _, spec in results],
        out_shape=[jax.ShapeDtypeStruct(shape, dtype) for shape, dtype, _ in results],
        input_output_aliases=aliases,
        scratch_shapes=list(scratch),
        compiler_params=pltpu.CompilerParams(
            dimension_semantics=("arbitrary",), vmem_limit_bytes=GRANTS[name] * MEGA
        ),
        cost_estimate=pl.CostEstimate(flops=1, bytes_accessed=1, transcendentals=0),
        name=name,
    )(*arrays)


class Layer:
    def __init__(self, tokens, cotangent, head_width, hidden):
        self.tokens, self.cotangent = tokens, cotangent
        self.total_rows, self.width = tokens.shape
        self.rows = self.total_rows // CHUNKS
        self.head_width, self.hidden = head_width, hidden
        self.place = lax.axis_index("mp").astype(jnp.int32).reshape(1)
        self.whole = block_of((self.rows, self.width), 0, 0)
        self.gain_row = block_of((1, self.width), 0, 0)

    def chunk(self, c, columns=None):
        return block_of((self.rows, columns or self.width), c, 0)

    def qkv_operands(self, c, halves, halo, query_ids, key_ids):
        head_width = self.head_width
        half_rows = halves[0].shape[0]
        half, first_row = divmod(c * self.rows, half_rows)
        first_part, first_window = first_row // QUERY_ROWS, first_row // WINDOW
        stride = QUERY_ROWS // WINDOW

        def part(k):
            return pl.BlockSpec((QUERY_ROWS, head_width), lambda i: (first_part + i, k))

        def before(k):
            return pl.BlockSpec(
                (WINDOW, head_width),
                lambda i: (jnp.maximum(first_window + stride * i - 1, 0), k),
            )

        source = halves[half]
        operands = [(source, part(k)) for k in range(3)]
        operands += [(source, before(k)) for k in (1, 2)]
        if c == 0:
            operands += [(halo, block_of((WINDOW, head_width), 0, k)) for k in range(2)]
        elif first_row == 0:
            last = half_rows // WINDOW - 1
            operands += [
                (halves[half - 1], block_of((WINDOW, head_width), last, k)) for k in (1, 2)
            ]
        parts = self.rows // QUERY_ROWS
        ids = [
            (query_ids, pl.BlockSpec((QUERY_ROWS, 1), lambda i: (c * parts + i, 0))),
            (
                key_ids,
                pl.BlockSpec((1, 1, QUERY_ROWS + WINDOW), lambda i: (c * parts + i, 0, 0)),
            ),
        ]
        return first_row == 0, operands + ids

    def part(self, c, columns):
        parts = self.rows // QUERY_ROWS
        return pl.BlockSpec((QUERY_ROWS, columns), lambda i: (c * parts + i, 0))

    def attend(self, c, first_and_qkv, attn_weight, attended):
        first, qkv_operands = first_and_qkv
        return call(
            functools.partial(attend_kernel, first),
            "attend",
            qkv_operands + [(attn_weight, block_of((self.width, self.head_width), 0, 3))],
            [
                ((self.total_rows, self.head_width), low_type, self.part(c, self.head_width)),
                ((self.rows, self.width), low_type, self.part(0, self.width)),
            ],
            {0: attended},
            steps=self.rows // QUERY_ROWS,
        )

    def feed_forward(self, c, line, gain, weight, shared):
        rows, width, hidden = self.rows, self.width, self.hidden
        block = pltpu.VMEM((rows, width), low_type)
        return call(
            functools.partial(mlp_kernel, c * rows),
            "feed_forward",
            [
                (self.place, smem),
                (self.tokens, anywhere),
                (line[0], anywhere),
                (line[1], anywhere),
                (self.cotangent, anywhere),
                (gain, self.gain_row),
                (weight, anywhere),
            ],
            [
                ((rows, width), low_type, anywhere),
                ((self.total_rows, width), low_type, anywhere),
                ((self.total_rows, hidden), low_type, anywhere),
                ((self.total_rows, 2 * hidden), low_type, anywhere),
                ((rows, width), low_type, anywhere),
                ((rows, width), low_type, anywhere),
            ],
            {index + 1: kept for index, kept in enumerate(shared)},
            scratch=[block, block, block, block]
            + [
                pltpu.VMEM((rows, hidden), low_type),
                pltpu.VMEM((rows, 2 * hidden), low_type),
                block,
                block,
                pltpu.VMEM((rows, width), jnp.float32),
                pltpu.VMEM((rows, width), jnp.float32),
                pltpu.VMEM((width, 3 * hidden), low_type),
                pltpu.SemaphoreType.DMA((3 + len(mlp_pieces(hidden)[1]),)),
                pltpu.SemaphoreType.DMA((6,)),
            ],
        )

    def attend_back(
        self, c, attn_sum, line, gain, first_and_qkv, attn_weight, low_all,
        keep=False, give_before=False, earlier=None, after=None, grads_all=None,
    ):
        first, qkv_operands = first_and_qkv
        rows, width, head_width = self.rows, self.width, self.head_width
        mine, alone = self.part(c, width), self.part(0, width)
        query_spec = block_of((rows, head_width), 0, 0)
        own_spec = block_of((rows, 2 * head_width), 0, 0)
        window_spec = block_of((WINDOW, 2 * head_width), 0, 0)
        more, results = {}, {
            "low": ((self.total_rows, width), low_type, mine),
            "gain_part": ((1, width), jnp.float32, self.gain_row),
        }
        shared = {0: low_all}
        scratch = [
            pltpu.VMEM((rows + WINDOW, 2 * head_width), jnp.float32),
            pltpu.VMEM((rows, head_width), low_type),
        ]
        if keep:
            results["query_grad"] = ((rows, head_width), low_type, query_spec)
            results["own"] = ((rows, 2 * head_width), low_type, own_spec)
        if give_before:
            results["before"] = ((WINDOW, 2 * head_width), jnp.float32, window_spec)
        term_chunk = None
        if earlier is not None:
            term_chunk = earlier[0]
            more["query_grad"], more["own"] = (earlier[1], query_spec), (earlier[2], own_spec)
        elif after is not None:
            term_chunk = c
            more["after"] = (after, window_spec)
        if term_chunk is not None:
            more["weight"] = (attn_weight, anywhere)
            shared[len(results)] = grads_all
            results["grads"] = (
                (self.total_rows, 3 * head_width),
                low_type,
                block_of((rows, 3 * head_width), term_chunk, 0),
            )
            results["term"] = ((rows, width), low_type, self.whole)
            scratch += [pltpu.VMEM((width, 3 * head_width), low_type), pltpu.SemaphoreType.DMA]
        kept = sum(array is not None for array in shared.values())
        outputs = call(
            functools.partial(
                attend_back_kernel, first, (tuple(more), tuple(results)), (len(more), kept)
            ),
            "attend_back",
            [
                (self.place, smem),
                (self.tokens, mine),
                (attn_sum, alone),
                (line[0], alone),
                (line[1], alone),
                (self.cotangent, mine),
                (gain, self.gain_row),
            ]
            + qkv_operands
            + [(attn_weight, block_of((width, head_width), 0, 3))]
            + list(more.values()),
            list(results.values()),
            shared,
            steps=rows // QUERY_ROWS,
            scratch=scratch,
        )
        return dict(zip(results, outputs))

    def attn_term(self, c, query_grad, own, after, attn_weight, grads_all):
        rows, width, head_width = self.rows, self.width, self.head_width
        part = width // CHUNKS
        return call(
            attn_term_kernel,
            "attn_term",
            [
                (query_grad, block_of((rows, head_width), 0, 0)),
                (own, block_of((rows, 2 * head_width), 0, 0)),
                (after, block_of((WINDOW, 2 * head_width), 0, 0)),
                (attn_weight, pl.BlockSpec((part, 3 * head_width), lambda i: (i, 0))),
            ],
            [
                ((self.total_rows, 3 * head_width), low_type, self.chunk(c, 3 * head_width)),
                ((rows, width), low_type, pl.BlockSpec((rows, part), lambda i: (0, i))),
            ],
            {0: grads_all},
            steps=width // part,
        )

    def attn_weight_grads(self, normed_attn, grads_all, low_all, attended):
        rows, width, head_width = self.total_rows, self.width, self.head_width
        return call(
            attn_weight_grads_kernel,
            "attn_weight_grads",
            [
                (normed_attn, block_of((rows, width), 0, 0)),
                (low_all, block_of((rows, width), 0, 0)),
                (grads_all, pl.BlockSpec((rows, head_width), lambda i: (0, jnp.minimum(i, 2)))),
                (attended, block_of((rows, head_width), 0, 0)),
            ],
            [((width, 4 * head_width), low_type, pl.BlockSpec((width, head_width), lambda i: (0, i)))],
            {},
            steps=4,
        )[0]

    def tokens_back(self, c, middle_grad, line, factor, gain, tokens_grad):
        return call(
            tokens_back_kernel,
            "tokens_back",
            [
                (self.place, smem),
                (middle_grad, self.part(c, self.width)),
                (line[0], self.part(0, self.width)),
                (line[1], self.part(0, self.width)),
                (self.tokens, self.part(c, self.width)),
                (factor, self.part(c, 1)),
                (gain, self.gain_row),
            ],
            [
                ((self.total_rows, self.width), jnp.float32, self.part(c, self.width)),
                ((1, self.width), jnp.float32, self.gain_row),
            ],
            {0: tokens_grad},
            steps=self.rows // QUERY_ROWS,
        )

    def output(self, c, attn_sum, line, out):
        return call(
            output_kernel,
            "output",
            [
                (self.place, smem),
                (self.tokens, self.part(c, self.width)),
                (attn_sum, self.part(0, self.width)),
                (line[0], self.part(0, self.width)),
                (line[1], self.part(0, self.width)),
            ],
            [((self.total_rows, self.width), low_type, self.part(c, self.width))],
            {0: out},
            steps=self.rows // QUERY_ROWS,
        )[0]


def middle_add_kernel(place_ref, left_ref, right_ref, result_ref, left, right, arrived, left_sem):
    place = place_ref[0]

    @pl.when((place == 1) | (place == 2))
    def _():
        parts = [
            pl.ds(start, QUERY_ROWS // 2) for start in range(0, left.shape[0], QUERY_ROWS // 2)
        ]
        fetches = [
            (
                pltpu.make_async_copy(left_ref.at[rows], left.at[rows], arrived.at[2 * i]),
                pltpu.make_async_copy(right_ref.at[rows], right.at[rows], arrived.at[2 * i + 1]),
            )
            for i, rows in enumerate(parts)
        ]
        for one, other in fetches:
            one.start()
            other.start()
        gives = [
            pltpu.make_async_copy(left.at[rows], result_ref.at[rows], left_sem.at[i])
            for i, rows in enumerate(parts)
        ]
        for rows, (one, other), give in zip(parts, fetches, gives):
            one.wait()
            other.wait()
            left[rows, :] = (
                left[rows, :].astype(jnp.float32) + right[rows, :].astype(jnp.float32)
            ).astype(low_type)
            give.start()
        for give in gives:
            give.wait()


def middle_add(place, left, right):
    rows, width = left.shape
    parts = 2 * rows // QUERY_ROWS
    return call(
        middle_add_kernel,
        "middle_add",
        [(place, smem), (left, anywhere), (right, anywhere)],
        [((rows, width), low_type, anywhere)],
        {},
        scratch=[
            pltpu.VMEM((rows, width), low_type),
            pltpu.VMEM((rows, width), low_type),
            pltpu.SemaphoreType.DMA((2 * parts,)),
            pltpu.SemaphoreType.DMA((parts,)),
        ],
    )[0]


def from_behind(block, axis, distance):
    devices = range(lax.axis_size(axis))
    route = [(i - distance, i) for i in devices if i - distance in devices]
    return lax.ppermute(block, axis, route)


def hold(values):
    return lax.optimization_barrier(values)


def add_low(left, right):
    return (left.astype(jnp.float32) + right.astype(jnp.float32)).astype(low_type)


class LineSums:
    def __init__(self, axis):
        self.axis = axis
        self.place = lax.axis_index(axis).astype(jnp.int32).reshape(1)
        self.first = self.second = self.third = None
        self.results = {}

    def step(self, name, part, values, early=False):
        first, second, third = self.first, self.second, self.third
        own = None if first is None else first[1]
        half = None if second is None else second[1]
        part, own, half, values = hold((part, own, half, values))
        self.first = self.second = self.third = None
        new_half = new_total = done = None

        def send_part():
            if part is not None:
                self.first = (name, part, lax.ppermute(part, self.axis, [(0, 1), (3, 2)]))

        if early:
            send_part()
        if own is not None:
            new_half = middle_add(self.place, own, first[2])
            across = lax.ppermute(new_half, self.axis, [(1, 2), (2, 1)])
        if half is not None:
            new_total = middle_add(self.place, half, second[2])
            outward = lax.ppermute(new_total, self.axis, [(1, 0), (2, 3)])
        if early:
            new_half, new_total, values = hold((new_half, new_total, values))
        else:
            new_half, new_total, part, values = hold((new_half, new_total, part, values))
            send_part()
        if third is not None:
            done, values = hold((third[1:], values))
        if own is not None:
            self.second = (first[0], new_half, across)
        if half is not None:
            self.third = (second[0], new_total, outward)
        if third is not None:
            self.results[third[0]] = done
        return values


def small_sum_scatter(value, axis):
    size = lax.axis_size(axis)
    place = lax.axis_index(axis)
    bit = size // 2
    while bit >= 1:
        half = value.shape[1] // 2
        low, high = value[:, :half], value[:, half:]
        upper = (place & bit) != 0
        keep = jnp.where(upper, high, low)
        give = jnp.where(upper, low, high)
        value = keep + lax.ppermute(give, axis, [(i, i ^ bit) for i in range(size)])
        bit //= 2
    return value


def scattered(value):
    return lax.psum_scatter(value, "seq", scatter_dimension=0, tiled=True)


def body(
    tokens,
    group_ids,
    gain_attn,
    w_query,
    w_key,
    w_value,
    w_out,
    gain_mlp,
    w_gate,
    w_up,
    w_down,
    cotangent,
):
    head_width = w_query.shape[1]
    hidden = w_gate.shape[1]
    layer = Layer(tokens, cotangent, head_width, hidden)
    line = LineSums("mp")
    results = line.results
    total_rows = tokens.shape[0]

    attn_shard = jnp.concatenate([w_query, w_key, w_value, w_out.T], axis=1)
    attn_weight = lax.all_gather(attn_shard, "seq", axis=0, tiled=True)
    gains = lax.all_gather(jnp.stack([gain_attn, gain_mlp]), "seq", axis=1, tiled=True)
    gain_one = gains[:1].astype(jnp.float32)
    gain_two = gains[1:].astype(jnp.float32)
    ids_halo = from_behind(group_ids[-WINDOW:] + 1, "seq", 1) - 1
    ids_ext = jnp.concatenate([ids_halo, group_ids], axis=0)
    query_ids = group_ids[:, None]
    key_ids = jnp.stack(
        [
            ids_ext[None, start : start + QUERY_ROWS + WINDOW]
            for start in range(0, total_rows, QUERY_ROWS)
        ]
    )
    inputs = tokens.astype(jnp.float32)
    factor_one = row_scale(inputs)
    normed_attn = (inputs * factor_one * gain_one).astype(low_type)
    mlp_shard = mlp_layout(w_gate, w_up, w_down.T)
    mlp_shard, normed_attn, factor_one, query_ids, key_ids, gain_two, attn_weight = hold(
        (mlp_shard, normed_attn, factor_one, query_ids, key_ids, gain_two, attn_weight)
    )
    mlp_weight = lax.all_gather(mlp_shard, "seq", axis=0, tiled=True)

    half_rows = total_rows // 2
    qkv_weight = attn_weight[:, : 3 * head_width]
    halves = [times(normed_attn[:half_rows], qkv_weight).astype(low_type)]
    order = [1, 2, 0, 3]

    def pieces_of(c):
        return layer.qkv_operands(c, halves, halo, query_ids, key_ids)

    halo = None
    attended, term = layer.attend(order[0], pieces_of(order[0]), attn_weight, None)
    attended, later_rows, halves[0] = line.step(
        ("attn", order[0]), term, (attended, normed_attn[half_rows:], halves[0]), True
    )
    halves.append(times(later_rows, qkv_weight).astype(low_type))
    halo = from_behind(halves[1][-WINDOW:, head_width:], "seq", 1)
    for c in order[1:]:
        attended, term = layer.attend(c, pieces_of(c), attn_weight, attended)
        values = line.step(("attn", c), term, (attended, halves[0], halves[1], halo), True)
        attended, halves[0], halves[1], halo = values

    attn_sums, mlp_terms = {}, {}
    shared = (None, None, None)
    for c in order:
        attn_sums[c], *shared, term, mlp_terms[c] = layer.feed_forward(
            c, results["attn", c], gain_two, mlp_weight, shared
        )
        shared = line.step(("mlp", c), term, tuple(shared), True)
    normed_mlp, activations, mlp_grads = shared

    tokens_grad = out = None
    gain_one_parts, gain_two_parts = [], []

    def back(c, low_all, **more):
        made = layer.attend_back(
            c, attn_sums[c], results["mlp", c], gain_two, pieces_of(c), attn_weight, low_all, **more
        )
        gain_two_parts.append(made["gain_part"])
        return made

    def out_step(c, values, early=True):
        return line.step(("out", c), mlp_terms[c], values, early)

    gate_up_grad = inner_rows(normed_mlp, mlp_grads).astype(low_type)
    gate_up_grad, activations = out_step(order[0], (gate_up_grad, activations))
    gate_up_share = scattered(gate_up_grad)
    down_grad = inner_rows(cotangent, activations).astype(low_type)
    results["mlp", 1], down_grad = hold((results["mlp", 1], down_grad))
    made = back(1, None, keep=True, give_before=True)
    made, down_grad = out_step(order[1], (made, down_grad))
    down_share = scattered(down_grad)
    after_none = made["before"]
    made = back(2, made["low"], keep=True, earlier=(1, made["query_grad"], made["own"]))
    made, after_none = line.step(("attn_back", 1), made["term"], (made, after_none), True)
    kept = made["query_grad"], made["own"]
    made = back(0, made["low"], give_before=True, after=after_none, grads_all=made["grads"])
    made, kept = line.step(("attn_back", 0), made["term"], (made, kept), True)
    behind = from_behind(made["before"].astype(low_type), "seq", -1)
    made = back(3, made["low"], keep=True, earlier=(2, *kept), grads_all=made["grads"])
    made, behind = line.step(("attn_back", 2), made["term"], (made, behind), True)
    grads_all, term = layer.attn_term(
        3, made["query_grad"], made["own"], behind.astype(jnp.float32), attn_weight, made["grads"]
    )
    low_all = made["low"]
    attn_grad = layer.attn_weight_grads(normed_attn, grads_all, low_all, attended)
    attn_grad = line.step(("attn_back", 3), term, attn_grad, True)
    attn_share = scattered(attn_grad)

    def finish_tokens(c):
        nonlocal tokens_grad
        tokens_grad, part = layer.tokens_back(
            c, low_all, results["attn_back", c], factor_one, gain_one, tokens_grad
        )
        gain_one_parts.append(part)

    def finish_out(c):
        nonlocal out
        out = layer.output(c, attn_sums[c], results["out", c], out)

    finish_tokens(1)
    tokens_grad, gain_two_parts = out_step(order[2], (tokens_grad, gain_two_parts), True)
    finish_out(order[0])
    finish_tokens(0)
    tokens_grad, out = out_step(order[3], (tokens_grad, out), True)
    finish_tokens(2)
    finish_out(order[1])
    tokens_grad, out = line.step(None, None, (tokens_grad, out))
    finish_tokens(3)
    gain_parts = jnp.concatenate([sum(gain_one_parts), sum(gain_two_parts)], axis=0)
    gate_out = gate_up_share[:, :hidden].astype(jnp.float32)
    up_out = gate_up_share[:, hidden:].astype(jnp.float32)
    values = line.step(None, None, (tokens_grad, out, gain_parts, gate_out, up_out))
    tokens_grad, out, gain_parts, gate_out, up_out = values
    finish_out(order[2])
    down_out = down_share.astype(jnp.float32).T
    attn_out = attn_share.astype(jnp.float32)
    attn_outs = [attn_out[:, k * head_width : (k + 1) * head_width] for k in range(4)]
    attn_outs[3] = attn_outs[3].T
    gain_share = small_sum_scatter(gain_parts, "seq")
    out, gain_share = line.step(None, None, (out, gain_share))
    finish_out(order[3])
    return (
        out,
        tokens_grad,
        gain_share[0],
        attn_outs[0],
        attn_outs[1],
        attn_outs[2],
        attn_outs[3],
        gain_share[1],
        gate_out,
        up_out,
        down_out,
    )


def solution(mesh):
    placed = (
        P("seq", None),
        P("seq"),
        P("seq"),
        P("seq", "mp"),
        P("seq", "mp"),
        P("seq", "mp"),
        P("mp", "seq"),
        P("seq"),
        P("seq", "mp"),
        P("seq", "mp"),
        P("mp", "seq"),
        P("seq", None),
    )
    return jax.shard_map(
        body,
        mesh=mesh,
        in_specs=placed,
        out_specs=(
            P("seq", None),
            P("seq", None),
            P("seq"),
            P("seq", "mp"),
            P("seq", "mp"),
            P("seq", "mp"),
            P("mp", "seq"),
            P("seq"),
            P("seq", "mp"),
            P("seq", "mp"),
            P("mp", "seq"),
        ),
        check_vma=False,
    )
```

```python
import functools

import jax
import jax.numpy as jnp
from jax import lax
from jax.experimental import pallas as pl
from jax.experimental.pallas import tpu as pltpu
from jax.sharding import PartitionSpec as P

HEAD_DIM = 128
WINDOW = 64
CHUNKS = 4
QUERY_ROWS = 128
WIDE = 256

epsilon = 1e-05
masked_score = -1e30
score_scale = HEAD_DIM ** (-0.5)
MEGA = 1024 * 1024
GRANTS = {'middle_add': 8, 'attend': 30, 'feed_forward': 44, 'attend_back': 56, 'attn_term': 40, 'attn_weight_grads': 40, 'tokens_back': 56, 'output': 56}
low_type = jnp.bfloat16


def times(left, right):
    return jnp.dot(left, right, preferred_element_type=jnp.float32)


def times_transposed(left, right):
    return lax.dot_general(
        left, right, (((1,), (1,)), ((), ())), preferred_element_type=jnp.float32
    )


def inner_rows(left, right):
    return lax.dot_general(
        left, right, (((0,), (0,)), ((), ())), preferred_element_type=jnp.float32
    )


def row_scale(value_in):
    return lax.rsqrt(jnp.mean(value_in * value_in, axis=-1, keepdims=True) + epsilon)


def norm_backward(grad_normed, normed_unit, row_factor, gain_full):
    scaled_grad = grad_normed * gain_full
    return row_factor * (
        scaled_grad - normed_unit * jnp.mean(scaled_grad * normed_unit, axis=-1, keepdims=True)
    )


def line_result(place_ref, total_ref, outward_ref):
    place = place_ref[0]
    in_middle = (place == 1) | (place == 2)
    return jnp.where(in_middle, total_ref[...], outward_ref[...])


def allowed_pairs(query_ids, key_ids):
    shape = (query_ids.shape[0], key_ids.shape[1])
    query_pos = lax.broadcasted_iota(jnp.int32, shape, 0)
    key_pos = lax.broadcasted_iota(jnp.int32, shape, 1)
    inside = (key_pos >= query_pos) & (key_pos <= query_pos + WINDOW)
    return inside & (query_ids == key_ids) & (query_ids >= 0)


def probabilities(query, key, allowed, valid):
    scores = jnp.where(allowed, times_transposed(query, key) * score_scale, masked_score)
    top_score = jnp.max(scores, axis=-1, keepdims=True)
    weights = jnp.where(allowed, jnp.exp(scores - top_score), 0.0)
    totals = jnp.where(valid, jnp.sum(weights, axis=-1, keepdims=True), 1.0)
    return weights / totals


def keys_of(step, first_refs, before_refs, refs, columns):
    out = []
    for first_ref, before_ref, ref in zip(first_refs, before_refs, refs):
        before = before_ref[:, columns]
        if first_ref is not None:
            before = jnp.where(step == 0, first_ref[:, columns], before)
        out.append(jnp.concatenate([before, ref[:, columns]], axis=0))
    return out


def split_refs(first, refs):
    q_ref, k_ref, v_ref, k_before, v_before = refs[:5]
    firsts = refs[5:7] if first else (None, None)
    refs = refs[7 if first else 5 :]
    return (q_ref, (k_ref, v_ref), (k_before, v_before), firsts), refs[:2], refs[2:]


def attend_kernel(first, *refs):
    (q_ref, own, before, firsts), (query_ids_ref, key_ids_ref), rest = split_refs(first, refs)
    out_weight_ref = rest[0]
    attended_ref, term_ref = rest[-2:]
    step = pl.program_id(0)
    query_ids = query_ids_ref[...]
    allowed = allowed_pairs(query_ids, key_ids_ref[0])
    valid = query_ids >= 0
    for head in range(q_ref.shape[1] // HEAD_DIM):
        columns = slice(head * HEAD_DIM, (head + 1) * HEAD_DIM)
        key, value = keys_of(step, firsts, before, own, columns)
        probs = probabilities(q_ref[:, columns], key, allowed, valid)
        attended_ref[:, columns] = times(probs.astype(low_type), value).astype(low_type)
    term_ref[...] = times_transposed(attended_ref[...], out_weight_ref[...]).astype(low_type)


def attend_back_kernel(
    first, names, counts, place_ref, tokens_ref, attn_sum_ref, total_ref, outward_ref, cotangent_ref,
    gain_ref, *refs,
):
    (q_ref, own, before, firsts), (query_ids_ref, key_ids_ref), rest = split_refs(first, refs)
    out_weight_ref = rest[0]
    inputs = dict(zip(names[0], rest[1 : 1 + counts[0]]))
    outputs = dict(zip(names[1], rest[1 + counts[0] + counts[1] :]))
    scratch = rest[1 + counts[0] + counts[1] + len(names[1]) :]
    spread, query_grads = scratch[:2]
    step = pl.program_id(0)
    last = pl.num_programs(0) - 1
    rows, width = q_ref.shape
    if "weight" in inputs:
        held, arrived = scratch[2:]
        fetch = pltpu.make_async_copy(
            inputs["weight"].at[:, : held.shape[1]], held, arrived
        )

        @pl.when(step == 0)
        def _():
            fetch.start()

    middle = tokens_ref[...].astype(jnp.float32) + attn_sum_ref[...].astype(jnp.float32)
    factor = row_scale(middle)
    unit = middle * factor
    grad_sum = line_result(place_ref, total_ref, outward_ref).astype(jnp.float32)
    gain_part = jnp.sum(grad_sum * unit, axis=0, keepdims=True)
    middle_grad = cotangent_ref[...].astype(jnp.float32) + norm_backward(
        grad_sum, unit, factor, gain_ref[...]
    )
    low = middle_grad.astype(low_type)
    outputs["low"][...] = low
    attended_grad = times(low, out_weight_ref[...]).astype(low_type)

    @pl.when(step == 0)
    def _():
        outputs["gain_part"][...] = gain_part
        spread[...] = jnp.zeros_like(spread)

    @pl.when(step > 0)
    def _():
        outputs["gain_part"][...] += gain_part

    query_ids = query_ids_ref[...]
    allowed = allowed_pairs(query_ids, key_ids_ref[0])
    valid = query_ids >= 0
    part = pl.ds(pl.multiple_of(step * rows, rows), rows)
    span = pl.ds(pl.multiple_of(step * rows, rows), rows + WINDOW)
    for head in range(width // HEAD_DIM):
        columns = slice(head * HEAD_DIM, (head + 1) * HEAD_DIM)
        value_columns = slice(width + head * HEAD_DIM, width + (head + 1) * HEAD_DIM)
        query = q_ref[:, columns]
        key, value = keys_of(step, firsts, before, own, columns)
        out_grad = attended_grad[:, columns]
        probs = probabilities(query, key, allowed, valid)
        prob_grad = times_transposed(out_grad, value)
        centre = jnp.sum(prob_grad * probs, axis=-1, keepdims=True)
        score_grad = (probs * (prob_grad - centre)).astype(low_type)
        query_grads[part, columns] = (times(score_grad, key) * score_scale).astype(low_type)
        spread[span, columns] += inner_rows(score_grad, query) * score_scale
        spread[span, value_columns] += inner_rows(probs.astype(low_type), out_grad)

    @pl.when(step == last)
    def _():
        if "own" in outputs:
            outputs["query_grad"][...] = query_grads[...]
            outputs["own"][...] = spread[WINDOW:, :].astype(low_type)
        if "before" in outputs:
            outputs["before"][...] = spread[:WINDOW, :]
        if "weight" not in inputs:
            return
        grads_ref = outputs["grads"]
        kept = grads_ref.shape[0] - WINDOW
        if "own" in inputs:
            grads_ref[:, :width] = inputs["query_grad"][...]
            grads_ref[:kept, width:] = inputs["own"][:kept, :]
            tail, after = inputs["own"][kept:, :].astype(jnp.float32), spread[:WINDOW, :]
        else:
            grads_ref[:, :width] = query_grads[...]
            grads_ref[:kept, width:] = spread[WINDOW : WINDOW + kept, :].astype(low_type)
            tail, after = spread[WINDOW + kept :, :], inputs["after"][...]
        grads_ref[kept:, width:] = (tail + after).astype(low_type)
        fetch.wait()
        outputs["term"][...] = times_transposed(grads_ref[...], held[...]).astype(low_type)


def attn_term_kernel(query_grad_ref, own_ref, after_ref, weight_ref, *rest):
    grads_ref, term_ref = rest[-2:]
    rows, width = query_grad_ref.shape

    @pl.when(pl.program_id(0) == 0)
    def _():
        kept = rows - WINDOW
        grads_ref[:, :width] = query_grad_ref[...]
        grads_ref[:kept, width:] = own_ref[:kept, :]
        grads_ref[kept:, width:] = (
            own_ref[kept:, :].astype(jnp.float32) + after_ref[...]
        ).astype(low_type)

    term_ref[...] = times_transposed(grads_ref[...], weight_ref[...]).astype(low_type)


def attn_weight_grads_kernel(normed_ref, low_ref, grads_ref, attended_ref, result_ref):
    step = pl.program_id(0)

    @pl.when(step < 3)
    def _():
        result_ref[...] = inner_rows(normed_ref[...], grads_ref[...]).astype(low_type)

    @pl.when(step == 3)
    def _():
        result_ref[...] = inner_rows(low_ref[...], attended_ref[...]).astype(low_type)


def tokens_back_kernel(
    place_ref, middle_grad_ref, total_ref, outward_ref, tokens_ref, factor_ref, gain_ref, *rest
):
    tokens_grad_ref, gain_part_ref = rest[-2:]
    factor = factor_ref[...]
    unit = tokens_ref[...].astype(jnp.float32) * factor
    grad_sum = line_result(place_ref, total_ref, outward_ref).astype(jnp.float32)
    tokens_grad_ref[...] = middle_grad_ref[...].astype(jnp.float32) + norm_backward(
        grad_sum, unit, factor, gain_ref[...]
    )
    gain_part = jnp.sum(grad_sum * unit, axis=0, keepdims=True)

    @pl.when(pl.program_id(0) == 0)
    def _():
        gain_part_ref[...] = gain_part

    @pl.when(pl.program_id(0) > 0)
    def _():
        gain_part_ref[...] += gain_part


def output_kernel(place_ref, tokens_ref, attn_sum_ref, total_ref, outward_ref, *rest):
    middle = tokens_ref[...].astype(jnp.float32) + attn_sum_ref[...].astype(jnp.float32)
    mlp_sum = line_result(place_ref, total_ref, outward_ref).astype(jnp.float32)
    rest[-1][...] = (middle + mlp_sum).astype(low_type)


def mlp_pieces(hidden):
    whole = hidden // WIDE * WIDE
    pieces = []
    for start in range(0, whole, WIDE):
        for k in range(3):
            pieces.append(slice(k * whole + start, k * whole + start + WIDE))
    pieces.append(slice(3 * whole, 3 * hidden))
    return whole, pieces


def mlp_layout(gate, up, down):
    whole = gate.shape[1] // WIDE * WIDE
    return jnp.concatenate(
        [m[:, :whole] for m in (gate, up, down)] + [m[:, whole:] for m in (gate, up, down)], axis=1
    )


def mlp_kernel(
    first_row, place_ref, tokens_ref, total_ref, outward_ref, cotangent_ref, gain_ref, weight_ref, *rest
):
    leaving = rest[-19:-13]
    (
        tokens, attn_sum, cotangent, normed_ref, activation_ref, grads_ref, term_ref, mlp_ref,
        term_part, mlp_part, held, arrived, left,
    ) = rest[-13:]
    rows, hidden = activation_ref.shape
    whole, pieces = mlp_pieces(hidden)
    half = hidden - whole
    tail = 3 * whole
    mine = pl.ds(first_row, rows)
    place = place_ref[0]
    in_middle = (place == 1) | (place == 2)

    fetch_tokens = pltpu.make_async_copy(tokens_ref.at[mine], tokens, arrived.at[0])
    fetch_total = pltpu.make_async_copy(total_ref, attn_sum, arrived.at[1])
    fetch_outward = pltpu.make_async_copy(outward_ref, attn_sum, arrived.at[1])
    fetch_cotangent = pltpu.make_async_copy(cotangent_ref.at[mine], cotangent, arrived.at[2])
    fetch_tokens.start()
    pl.when(in_middle)(fetch_total.start)
    pl.when(jnp.logical_not(in_middle))(fetch_outward.start)
    fetch_cotangent.start()
    copies = [
        pltpu.make_async_copy(weight_ref.at[:, piece], held.at[:, piece], arrived.at[3 + i])
        for i, piece in enumerate(pieces)
    ]
    for copy in copies:
        copy.start()
    sources = (attn_sum, normed_ref, activation_ref, grads_ref, term_ref, mlp_ref)
    out_copies = [
        pltpu.make_async_copy(
            source, target.at[mine] if i in (1, 2, 3) else target, left.at[i]
        )
        for i, (source, target) in enumerate(zip(sources, leaving))
    ]

    fetch_tokens.wait()
    fetch_total.wait()
    middle = tokens[...].astype(jnp.float32) + attn_sum[...].astype(jnp.float32)
    normed_ref[...] = (middle * row_scale(middle) * gain_ref[...]).astype(low_type)
    fetch_cotangent.wait()
    normed = normed_ref[...]
    cot = cotangent[...]

    def inner(start, stop, gate, up, act_grad):
        sigmoid_gate = jax.nn.sigmoid(gate)
        silu_gate = gate * sigmoid_gate
        activation_ref[:, start:stop] = (silu_gate * up).astype(low_type)
        grads_ref[:, start:stop] = (
            act_grad * up * (sigmoid_gate + silu_gate * (1.0 - sigmoid_gate))
        ).astype(low_type)
        grads_ref[:, hidden + start : hidden + stop] = (act_grad * silu_gate).astype(low_type)

    def whole_piece(j):
        for copy in copies[3 * j : 3 * j + 3]:
            copy.wait()
        gate, up, down = (held[:, piece] for piece in pieces[3 * j : 3 * j + 3])
        inner(j * WIDE, (j + 1) * WIDE, times(normed, gate), times(normed, up), times(cot, down))

    def back(rows, start, stop):
        term = times_transposed(grads_ref[:, start:stop], held[rows, start:stop])
        term += times_transposed(
            grads_ref[:, hidden + start : hidden + stop], held[rows, whole + start : whole + stop]
        )
        down = held[rows, 2 * whole + start : 2 * whole + stop]
        return term, times_transposed(activation_ref[:, start:stop], down)

    blocks = [slice(start, start + 2 * WIDE) for start in range(0, held.shape[0], 2 * WIDE)]
    early = whole // WIDE // 2 + 1
    for j in range(early):
        whole_piece(j)
    for rows in blocks:
        term_part[:, rows], mlp_part[:, rows] = back(rows, 0, early * WIDE)
    for j in range(early, whole // WIDE):
        whole_piece(j)
    copies[-1].wait()
    both = times(normed, held[:, tail : tail + 2 * half])
    inner(
        whole, hidden, both[:, :half], both[:, half:], times(cot, held[:, tail + 2 * half :])
    )
    for copy in out_copies[:4]:
        copy.start()

    pair = jnp.concatenate([grads_ref[:, whole:hidden], grads_ref[:, hidden + whole :]], axis=1)
    for rows in blocks:
        term, mlp = back(rows, early * WIDE, whole)
        term += times_transposed(pair, held[rows, tail : tail + 2 * half]) + term_part[:, rows]
        mlp += times_transposed(activation_ref[:, whole:], held[rows, tail + 2 * half :])
        term_ref[:, rows] = term.astype(low_type)
        mlp_ref[:, rows] = (mlp + mlp_part[:, rows]).astype(low_type)
    for copy in out_copies[4:]:
        copy.start()
    for copy in out_copies:
        copy.wait()


def block_of(shape, *place):
    return pl.BlockSpec(shape, lambda i: place)


smem = pl.BlockSpec(memory_space=pltpu.SMEM)
anywhere = pl.BlockSpec(memory_space=pl.ANY)


def call(kernel, name, operands, results, shared, steps=1, scratch=()):
    arrays = [array for array, _ in operands]
    specs = [spec for _, spec in operands]
    aliases = {}
    for index, kept in shared.items():
        if kept is not None:
            aliases[len(arrays)] = index
            arrays.append(kept)
            specs.append(anywhere)
    return pl.pallas_call(
        kernel,
        grid=(steps,),
        in_specs=specs,
        out_specs=[spec for _, _, spec in results],
        out_shape=[jax.ShapeDtypeStruct(shape, dtype) for shape, dtype, _ in results],
        input_output_aliases=aliases,
        scratch_shapes=list(scratch),
        compiler_params=pltpu.CompilerParams(
            dimension_semantics=("arbitrary",), vmem_limit_bytes=GRANTS[name] * MEGA
        ),
        cost_estimate=pl.CostEstimate(flops=1, bytes_accessed=1, transcendentals=0),
        name=name,
    )(*arrays)


class Layer:
    def __init__(self, tokens, cotangent, head_width, hidden):
        self.tokens, self.cotangent = tokens, cotangent
        self.total_rows, self.width = tokens.shape
        self.rows = self.total_rows // CHUNKS
        self.head_width, self.hidden = head_width, hidden
        self.place = lax.axis_index("mp").astype(jnp.int32).reshape(1)
        self.whole = block_of((self.rows, self.width), 0, 0)
        self.gain_row = block_of((1, self.width), 0, 0)

    def chunk(self, c, columns=None):
        return block_of((self.rows, columns or self.width), c, 0)

    def qkv_operands(self, c, halves, halo, query_ids, key_ids):
        head_width = self.head_width
        half_rows = halves[0].shape[0]
        half, first_row = divmod(c * self.rows, half_rows)
        first_part, first_window = first_row // QUERY_ROWS, first_row // WINDOW
        stride = QUERY_ROWS // WINDOW

        def part(k):
            return pl.BlockSpec((QUERY_ROWS, head_width), lambda i: (first_part + i, k))

        def before(k):
            return pl.BlockSpec(
                (WINDOW, head_width),
                lambda i: (jnp.maximum(first_window + stride * i - 1, 0), k),
            )

        source = halves[half]
        operands = [(source, part(k)) for k in range(3)]
        operands += [(source, before(k)) for k in (1, 2)]
        if c == 0:
            operands += [(halo, block_of((WINDOW, head_width), 0, k)) for k in range(2)]
        elif first_row == 0:
            last = half_rows // WINDOW - 1
            operands += [
                (halves[half - 1], block_of((WINDOW, head_width), last, k)) for k in (1, 2)
            ]
        parts = self.rows // QUERY_ROWS
        ids = [
            (query_ids, pl.BlockSpec((QUERY_ROWS, 1), lambda i: (c * parts + i, 0))),
            (
                key_ids,
                pl.BlockSpec((1, 1, QUERY_ROWS + WINDOW), lambda i: (c * parts + i, 0, 0)),
            ),
        ]
        return first_row == 0, operands + ids

    def part(self, c, columns):
        parts = self.rows // QUERY_ROWS
        return pl.BlockSpec((QUERY_ROWS, columns), lambda i: (c * parts + i, 0))

    def attend(self, c, first_and_qkv, attn_weight, attended):
        first, qkv_operands = first_and_qkv
        return call(
            functools.partial(attend_kernel, first),
            "attend",
            qkv_operands + [(attn_weight, block_of((self.width, self.head_width), 0, 3))],
            [
                ((self.total_rows, self.head_width), low_type, self.part(c, self.head_width)),
                ((self.rows, self.width), low_type, self.part(0, self.width)),
            ],
            {0: attended},
            steps=self.rows // QUERY_ROWS,
        )

    def feed_forward(self, c, line, gain, weight, shared):
        rows, width, hidden = self.rows, self.width, self.hidden
        block = pltpu.VMEM((rows, width), low_type)
        return call(
            functools.partial(mlp_kernel, c * rows),
            "feed_forward",
            [
                (self.place, smem),
                (self.tokens, anywhere),
                (line[0], anywhere),
                (line[1], anywhere),
                (self.cotangent, anywhere),
                (gain, self.gain_row),
                (weight, anywhere),
            ],
            [
                ((rows, width), low_type, anywhere),
                ((self.total_rows, width), low_type, anywhere),
                ((self.total_rows, hidden), low_type, anywhere),
                ((self.total_rows, 2 * hidden), low_type, anywhere),
                ((rows, width), low_type, anywhere),
                ((rows, width), low_type, anywhere),
            ],
            {index + 1: kept for index, kept in enumerate(shared)},
            scratch=[block, block, block, block]
            + [
                pltpu.VMEM((rows, hidden), low_type),
                pltpu.VMEM((rows, 2 * hidden), low_type),
                block,
                block,
                pltpu.VMEM((rows, width), jnp.float32),
                pltpu.VMEM((rows, width), jnp.float32),
                pltpu.VMEM((width, 3 * hidden), low_type),
                pltpu.SemaphoreType.DMA((3 + len(mlp_pieces(hidden)[1]),)),
                pltpu.SemaphoreType.DMA((6,)),
            ],
        )

    def attend_back(
        self, c, attn_sum, line, gain, first_and_qkv, attn_weight, low_all,
        keep=False, give_before=False, earlier=None, after=None, grads_all=None,
    ):
        first, qkv_operands = first_and_qkv
        rows, width, head_width = self.rows, self.width, self.head_width
        mine, alone = self.part(c, width), self.part(0, width)
        query_spec = block_of((rows, head_width), 0, 0)
        own_spec = block_of((rows, 2 * head_width), 0, 0)
        window_spec = block_of((WINDOW, 2 * head_width), 0, 0)
        more, results = {}, {
            "low": ((self.total_rows, width), low_type, mine),
            "gain_part": ((1, width), jnp.float32, self.gain_row),
        }
        shared = {0: low_all}
        scratch = [
            pltpu.VMEM((rows + WINDOW, 2 * head_width), jnp.float32),
            pltpu.VMEM((rows, head_width), low_type),
        ]
        if keep:
            results["query_grad"] = ((rows, head_width), low_type, query_spec)
            results["own"] = ((rows, 2 * head_width), low_type, own_spec)
        if give_before:
            results["before"] = ((WINDOW, 2 * head_width), jnp.float32, window_spec)
        term_chunk = None
        if earlier is not None:
            term_chunk = earlier[0]
            more["query_grad"], more["own"] = (earlier[1], query_spec), (earlier[2], own_spec)
        elif after is not None:
            term_chunk = c
            more["after"] = (after, window_spec)
        if term_chunk is not None:
            more["weight"] = (attn_weight, anywhere)
            shared[len(results)] = grads_all
            results["grads"] = (
                (self.total_rows, 3 * head_width),
                low_type,
                block_of((rows, 3 * head_width), term_chunk, 0),
            )
            results["term"] = ((rows, width), low_type, self.whole)
            scratch += [pltpu.VMEM((width, 3 * head_width), low_type), pltpu.SemaphoreType.DMA]
        kept = sum(array is not None for array in shared.values())
        outputs = call(
            functools.partial(
                attend_back_kernel, first, (tuple(more), tuple(results)), (len(more), kept)
            ),
            "attend_back",
            [
                (self.place, smem),
                (self.tokens, mine),
                (attn_sum, alone),
                (line[0], alone),
                (line[1], alone),
                (self.cotangent, mine),
                (gain, self.gain_row),
            ]
            + qkv_operands
            + [(attn_weight, block_of((width, head_width), 0, 3))]
            + list(more.values()),
            list(results.values()),
            shared,
            steps=rows // QUERY_ROWS,
            scratch=scratch,
        )
        return dict(zip(results, outputs))

    def attn_term(self, c, query_grad, own, after, attn_weight, grads_all):
        rows, width, head_width = self.rows, self.width, self.head_width
        part = width // CHUNKS
        return call(
            attn_term_kernel,
            "attn_term",
            [
                (query_grad, block_of((rows, head_width), 0, 0)),
                (own, block_of((rows, 2 * head_width), 0, 0)),
                (after, block_of((WINDOW, 2 * head_width), 0, 0)),
                (attn_weight, pl.BlockSpec((part, 3 * head_width), lambda i: (i, 0))),
            ],
            [
                ((self.total_rows, 3 * head_width), low_type, self.chunk(c, 3 * head_width)),
                ((rows, width), low_type, pl.BlockSpec((rows, part), lambda i: (0, i))),
            ],
            {0: grads_all},
            steps=width // part,
        )

    def attn_weight_grads(self, normed_attn, grads_all, low_all, attended):
        rows, width, head_width = self.total_rows, self.width, self.head_width
        return call(
            attn_weight_grads_kernel,
            "attn_weight_grads",
            [
                (normed_attn, block_of((rows, width), 0, 0)),
                (low_all, block_of((rows, width), 0, 0)),
                (grads_all, pl.BlockSpec((rows, head_width), lambda i: (0, jnp.minimum(i, 2)))),
                (attended, block_of((rows, head_width), 0, 0)),
            ],
            [((width, 4 * head_width), low_type, pl.BlockSpec((width, head_width), lambda i: (0, i)))],
            {},
            steps=4,
        )[0]

    def tokens_back(self, c, middle_grad, line, factor, gain, tokens_grad):
        return call(
            tokens_back_kernel,
            "tokens_back",
            [
                (self.place, smem),
                (middle_grad, self.part(c, self.width)),
                (line[0], self.part(0, self.width)),
                (line[1], self.part(0, self.width)),
                (self.tokens, self.part(c, self.width)),
                (factor, self.part(c, 1)),
                (gain, self.gain_row),
            ],
            [
                ((self.total_rows, self.width), jnp.float32, self.part(c, self.width)),
                ((1, self.width), jnp.float32, self.gain_row),
            ],
            {0: tokens_grad},
            steps=self.rows // QUERY_ROWS,
        )

    def output(self, c, attn_sum, line, out):
        return call(
            output_kernel,
            "output",
            [
                (self.place, smem),
                (self.tokens, self.part(c, self.width)),
                (attn_sum, self.part(0, self.width)),
                (line[0], self.part(0, self.width)),
                (line[1], self.part(0, self.width)),
            ],
            [((self.total_rows, self.width), low_type, self.part(c, self.width))],
            {0: out},
            steps=self.rows // QUERY_ROWS,
        )[0]


def middle_add_kernel(place_ref, left_ref, right_ref, result_ref, left, right, arrived, left_sem):
    place = place_ref[0]

    @pl.when((place == 1) | (place == 2))
    def _():
        parts = [
            pl.ds(start, QUERY_ROWS // 2) for start in range(0, left.shape[0], QUERY_ROWS // 2)
        ]
        fetches = [
            (
                pltpu.make_async_copy(left_ref.at[rows], left.at[rows], arrived.at[2 * i]),
                pltpu.make_async_copy(right_ref.at[rows], right.at[rows], arrived.at[2 * i + 1]),
            )
            for i, rows in enumerate(parts)
        ]
        for one, other in fetches:
            one.start()
            other.start()
        gives = [
            pltpu.make_async_copy(left.at[rows], result_ref.at[rows], left_sem.at[i])
            for i, rows in enumerate(parts)
        ]
        for rows, (one, other), give in zip(parts, fetches, gives):
            one.wait()
            other.wait()
            left[rows, :] = (
                left[rows, :].astype(jnp.float32) + right[rows, :].astype(jnp.float32)
            ).astype(low_type)
            give.start()
        for give in gives:
            give.wait()


def middle_add(place, left, right):
    rows, width = left.shape
    parts = 2 * rows // QUERY_ROWS
    return call(
        middle_add_kernel,
        "middle_add",
        [(place, smem), (left, anywhere), (right, anywhere)],
        [((rows, width), low_type, anywhere)],
        {},
        scratch=[
            pltpu.VMEM((rows, width), low_type),
            pltpu.VMEM((rows, width), low_type),
            pltpu.SemaphoreType.DMA((2 * parts,)),
            pltpu.SemaphoreType.DMA((parts,)),
        ],
    )[0]


def from_behind(block, axis, distance):
    devices = range(lax.axis_size(axis))
    route = [(i - distance, i) for i in devices if i - distance in devices]
    return lax.ppermute(block, axis, route)


def hold(values):
    return lax.optimization_barrier(values)


def add_low(left, right):
    return (left.astype(jnp.float32) + right.astype(jnp.float32)).astype(low_type)


class LineSums:
    def __init__(self, axis):
        self.axis = axis
        self.place = lax.axis_index(axis).astype(jnp.int32).reshape(1)
        self.first = self.second = self.third = None
        self.results = {}

    def step(self, name, part, values, early=False):
        first, second, third = self.first, self.second, self.third
        own = None if first is None else first[1]
        half = None if second is None else second[1]
        part, own, half, values = hold((part, own, half, values))
        self.first = self.second = self.third = None
        new_half = new_total = done = None

        def send_part():
            if part is not None:
                self.first = (name, part, lax.ppermute(part, self.axis, [(0, 1), (3, 2)]))

        if early:
            send_part()
        if own is not None:
            new_half = middle_add(self.place, own, first[2])
            across = lax.ppermute(new_half, self.axis, [(1, 2), (2, 1)])
        if half is not None:
            new_total = middle_add(self.place, half, second[2])
            outward = lax.ppermute(new_total, self.axis, [(1, 0), (2, 3)])
        if early:
            new_half, new_total, values = hold((new_half, new_total, values))
        else:
            new_half, new_total, part, values = hold((new_half, new_total, part, values))
            send_part()
        if third is not None:
            done, values = hold((third[1:], values))
        if own is not None:
            self.second = (first[0], new_half, across)
        if half is not None:
            self.third = (second[0], new_total, outward)
        if third is not None:
            self.results[third[0]] = done
        return values


def small_sum_scatter(value, axis):
    size = lax.axis_size(axis)
    place = lax.axis_index(axis)
    bit = size // 2
    while bit >= 1:
        half = value.shape[1] // 2
        low, high = value[:, :half], value[:, half:]
        upper = (place & bit) != 0
        keep = jnp.where(upper, high, low)
        give = jnp.where(upper, low, high)
        value = keep + lax.ppermute(give, axis, [(i, i ^ bit) for i in range(size)])
        bit //= 2
    return value


def scattered(value):
    return lax.psum_scatter(value, "seq", scatter_dimension=0, tiled=True)


def body(
    tokens,
    group_ids,
    gain_attn,
    w_query,
    w_key,
    w_value,
    w_out,
    gain_mlp,
    w_gate,
    w_up,
    w_down,
    cotangent,
):
    head_width = w_query.shape[1]
    hidden = w_gate.shape[1]
    layer = Layer(tokens, cotangent, head_width, hidden)
    line = LineSums("mp")
    results = line.results
    total_rows = tokens.shape[0]

    attn_shard = jnp.concatenate([w_query, w_key, w_value, w_out.T], axis=1)
    attn_weight = lax.all_gather(attn_shard, "seq", axis=0, tiled=True)
    gains = lax.all_gather(jnp.stack([gain_attn, gain_mlp]), "seq", axis=1, tiled=True)
    gain_one = gains[:1].astype(jnp.float32)
    gain_two = gains[1:].astype(jnp.float32)
    ids_halo = from_behind(group_ids[-WINDOW:] + 1, "seq", 1) - 1
    ids_ext = jnp.concatenate([ids_halo, group_ids], axis=0)
    query_ids = group_ids[:, None]
    key_ids = jnp.stack(
        [
            ids_ext[None, start : start + QUERY_ROWS + WINDOW]
            for start in range(0, total_rows, QUERY_ROWS)
        ]
    )
    inputs = tokens.astype(jnp.float32)
    factor_one = row_scale(inputs)
    normed_attn = (inputs * factor_one * gain_one).astype(low_type)
    mlp_shard = mlp_layout(w_gate, w_up, w_down.T)
    mlp_shard, normed_attn, factor_one, query_ids, key_ids, gain_two, attn_weight = hold(
        (mlp_shard, normed_attn, factor_one, query_ids, key_ids, gain_two, attn_weight)
    )
    mlp_weight = lax.all_gather(mlp_shard, "seq", axis=0, tiled=True)

    half_rows = total_rows // 2
    qkv_weight = attn_weight[:, : 3 * head_width]
    halves = [times(normed_attn[:half_rows], qkv_weight).astype(low_type)]
    order = [1, 2, 0, 3]

    def pieces_of(c):
        return layer.qkv_operands(c, halves, halo, query_ids, key_ids)

    halo = None
    attended, term = layer.attend(order[0], pieces_of(order[0]), attn_weight, None)
    attended, later_rows, halves[0] = line.step(
        ("attn", order[0]), term, (attended, normed_attn[half_rows:], halves[0]), True
    )
    halves.append(times(later_rows, qkv_weight).astype(low_type))
    halo = from_behind(halves[1][-WINDOW:, head_width:], "seq", 1)
    for c in order[1:]:
        attended, term = layer.attend(c, pieces_of(c), attn_weight, attended)
        values = line.step(("attn", c), term, (attended, halves[0], halves[1], halo), True)
        attended, halves[0], halves[1], halo = values

    attn_sums, mlp_terms = {}, {}
    shared = (None, None, None)
    for c in order:
        attn_sums[c], *shared, term, mlp_terms[c] = layer.feed_forward(
            c, results["attn", c], gain_two, mlp_weight, shared
        )
        shared = line.step(("mlp", c), term, tuple(shared), True)
    normed_mlp, activations, mlp_grads = shared

    tokens_grad = out = None
    gain_one_parts, gain_two_parts = [], []

    def back(c, low_all, **more):
        made = layer.attend_back(
            c, attn_sums[c], results["mlp", c], gain_two, pieces_of(c), attn_weight, low_all, **more
        )
        gain_two_parts.append(made["gain_part"])
        return made

    def out_step(c, values, early=True):
        return line.step(("out", c), mlp_terms[c], values, early)

    gate_up_grad = inner_rows(normed_mlp, mlp_grads).astype(low_type)
    gate_up_grad, activations = out_step(order[0], (gate_up_grad, activations))
    gate_up_share = scattered(gate_up_grad)
    down_grad = inner_rows(cotangent, activations).astype(low_type)
    results["mlp", 1], down_grad = hold((results["mlp", 1], down_grad))
    made = back(1, None, keep=True, give_before=True)
    made, down_grad = out_step(order[1], (made, down_grad))
    down_share = scattered(down_grad)
    after_none = made["before"]
    made = back(2, made["low"], keep=True, earlier=(1, made["query_grad"], made["own"]))
    made, after_none = line.step(("attn_back", 1), made["term"], (made, after_none), True)
    kept = made["query_grad"], made["own"]
    made = back(0, made["low"], give_before=True, after=after_none, grads_all=made["grads"])
    made, kept = line.step(("attn_back", 0), made["term"], (made, kept), True)
    behind = from_behind(made["before"].astype(low_type), "seq", -1)
    made = back(3, made["low"], keep=True, earlier=(2, *kept), grads_all=made["grads"])
    made, behind = line.step(("attn_back", 2), made["term"], (made, behind), True)
    grads_all, term = layer.attn_term(
        3, made["query_grad"], made["own"], behind.astype(jnp.float32), attn_weight, made["grads"]
    )
    low_all = made["low"]
    attn_grad = layer.attn_weight_grads(normed_attn, grads_all, low_all, attended)
    attn_grad = line.step(("attn_back", 3), term, attn_grad, True)
    attn_share = scattered(attn_grad)

    def finish_tokens(c):
        nonlocal tokens_grad
        tokens_grad, part = layer.tokens_back(
            c, low_all, results["attn_back", c], factor_one, gain_one, tokens_grad
        )
        gain_one_parts.append(part)

    def finish_out(c):
        nonlocal out
        out = layer.output(c, attn_sums[c], results["out", c], out)

    finish_tokens(1)
    tokens_grad, gain_two_parts = out_step(order[2], (tokens_grad, gain_two_parts), True)
    finish_out(order[0])
    finish_tokens(0)
    tokens_grad, out = out_step(order[3], (tokens_grad, out), True)
    finish_tokens(2)
    finish_out(order[1])
    tokens_grad, out = line.step(None, None, (tokens_grad, out))
    finish_tokens(3)
    gain_parts = jnp.concatenate([sum(gain_one_parts), sum(gain_two_parts)], axis=0)
    gate_out = gate_up_share[:, :hidden].astype(jnp.float32)
    up_out = gate_up_share[:, hidden:].astype(jnp.float32)
    values = line.step(None, None, (tokens_grad, out, gain_parts, gate_out, up_out))
    tokens_grad, out, gain_parts, gate_out, up_out = values
    finish_out(order[2])
    down_out = down_share.astype(jnp.float32).T
    attn_out = attn_share.astype(jnp.float32)
    attn_outs = [attn_out[:, k * head_width : (k + 1) * head_width] for k in range(4)]
    attn_outs[3] = attn_outs[3].T
    gain_share = small_sum_scatter(gain_parts, "seq")
    out, gain_share = line.step(None, None, (out, gain_share))
    finish_out(order[3])
    return (
        out,
        tokens_grad,
        gain_share[0],
        attn_outs[0],
        attn_outs[1],
        attn_outs[2],
        attn_outs[3],
        gain_share[1],
        gate_out,
        up_out,
        down_out,
    )


def solution(mesh):
    placed = (
        P("seq", None),
        P("seq"),
        P("seq"),
        P("seq", "mp"),
        P("seq", "mp"),
        P("seq", "mp"),
        P("mp", "seq"),
        P("seq"),
        P("seq", "mp"),
        P("seq", "mp"),
        P("mp", "seq"),
        P("seq", None),
    )
    return jax.shard_map(
        body,
        mesh=mesh,
        in_specs=placed,
        out_specs=(
            P("seq", None),
            P("seq", None),
            P("seq"),
            P("seq", "mp"),
            P("seq", "mp"),
            P("seq", "mp"),
            P("mp", "seq"),
            P("seq"),
            P("seq", "mp"),
            P("seq", "mp"),
            P("mp", "seq"),
        ),
        check_vma=False,
    )
```
